128 devices in a mesh: tm: 64 (over z, x, y), blk: 2 (over core).
Axes of the slice: x: 4, y: 4, z: 4, core: 2. Of those that a mesh axis runs over, the one named last changes fastest.
Arguments:
- diag_blocks: float32 [128, 1024, 1024], P('tm', None, 'blk'), may hold values from -24 to 60, as said below
- sub_blocks: float32 [128, 1024, 1024], P('tm', None, 'blk'), may hold values from -17 to 2
- arrow_blocks: float32 [128, 64, 1024], P('tm', None, 'blk'), may hold values from -1 to 1
- tip_block: float32 [64, 64], replicated, may hold values from -2 to 14, as said below
Outputs:
- pivot_diag: float32 [64, 1024, 1024], P('tm', None, 'blk')
- pivot_left: float32 [64, 1024, 1024], P('tm', None, 'blk')
- pivot_arrow: float32 [64, 64, 1024], P('tm', None, 'blk')
- tip_schur: float32 [64, 64], replicated
- log_det: float32 [], replicated
The draws below stay inside these ranges and needn't reach their ends.
Inputs may be any that keep to these rules, and one draw needn't show every extreme that they name: Every diag_blocks[s] is symmetric, and the slab part of Q (without the fixed-effect rows) is positive definite. tip_block is symmetric.
All inputs are finite; a program needn't handle non-finite values.
Results may differ from the reference program's by a relative error of at most 0.0003.
Values sent between devices are 32-bit elements; how exact they have to be, the bound alone decides.
A program may use at most 192 MiB of HBM per device.

```python
import math
import jax
import jax.numpy as jnp
import numpy as np
from jax import lax

MESH_NODES = 1024
FIXED_EFFECTS = 64
LOCAL_SLABS = 2
LEVELS = 1
TIME_SLABS = 128
N_TM = 64


PRECISE = lax.Precision.HIGHEST


DIAG_SHIFT = 0.05


def slab_couplings(initial_random_key, spread, gap_low, gap_high):
    node_count = MESH_NODES
    block_list = TIME_SLABS + 1
    gap_key = jax.random.fold_in(initial_random_key, 101)
    spike_random_key = jax.random.fold_in(initial_random_key, 102)
    depth_key = jax.random.fold_in(initial_random_key, 103)
    noise_key = jax.random.fold_in(initial_random_key, 104)
    gap_values = jnp.exp(jax.random.uniform(gap_key, (block_list, node_count), jnp.float32, math.log(gap_low), math.log(gap_high)))
    spike_slab_indices = jax.random.randint(spike_random_key, (3,), 1, block_list)
    is_spiking = jnp.any(jnp.arange(block_list)[:, None] == spike_slab_indices[None, :], axis=1)
    damping = jnp.where(is_spiking[:, None], jax.random.uniform(depth_key, (block_list, node_count), jnp.float32, 0.5, 0.8), 1.0)
    persist = (1.0 - gap_values) * damping
    noise_part = jax.random.uniform(noise_key, (block_list, node_count, node_count), jnp.float32, -1.0, 1.0) * (spread * math.sqrt(3.0 / node_count))
    identity = jnp.eye(node_count, dtype=jnp.float32)
    return noise_part - persist[:, :, None] * identity[None]


def shared_scales(initial_random_key, node_spread):
    ramp = jnp.arange(TIME_SLABS, dtype=jnp.float32) / max(TIME_SLABS - 1, 1)
    slab_scale = jnp.exp(1.4 * ramp)
    node_scale = jnp.exp(node_spread * jax.random.uniform(jax.random.fold_in(initial_random_key, 201), (MESH_NODES,), jnp.float32, -1.0, 1.0))
    return (slab_scale, node_scale)


def draw_diag_blocks(key, part):
    spread, gap_low, gap_high, node_spread = (1.8, 0.02, 0.4, 0.0)
    couplings = slab_couplings(key, spread, gap_low, gap_high)
    slab_scale, node_scale = shared_scales(key, node_spread)
    key = jax.random.fold_in(key, 1)
    later = couplings[1:]
    gram_part = jnp.einsum('sji,sjk->sik', later, later, precision=PRECISE)
    identity = jnp.eye(MESH_NODES, dtype=jnp.float32)
    block_list = (1.0 + DIAG_SHIFT) * identity[None] + gram_part
    pair_scale = node_scale[:, None] * node_scale[None, :]
    return block_list * slab_scale[:, None, None] * pair_scale[None]


def draw_sub_blocks(key, part):
    spread, gap_low, gap_high, node_spread = (1.8, 0.02, 0.4, 0.0)
    couplings = slab_couplings(key, spread, gap_low, gap_high)
    slab_scale, node_scale = shared_scales(key, node_spread)
    key = jax.random.fold_in(key, 2)
    earlier = jnp.concatenate([slab_scale[:1], slab_scale[:-1]])
    joint_scale = jnp.sqrt(slab_scale * earlier)
    pair_scale = node_scale[:, None] * node_scale[None, :]
    return couplings[:-1] * joint_scale[:, None, None] * pair_scale[None]


def draw_arrow_blocks(key, part):
    node_spread, common_weight = (0.0, 0.0)
    slab_scale, node_scale = shared_scales(key, node_spread)
    key = jax.random.fold_in(key, 3)
    own_part = jax.random.uniform(jax.random.fold_in(key, 1), (TIME_SLABS, FIXED_EFFECTS, MESH_NODES), jnp.float32, -1.0, 1.0)
    common_part = jax.random.uniform(jax.random.fold_in(key, 2), (1, FIXED_EFFECTS, MESH_NODES), jnp.float32, -1.0, 1.0)
    ramp = jnp.arange(TIME_SLABS, dtype=jnp.float32) / max(TIME_SLABS - 1, 1)
    rising = jnp.sqrt((1.0 + 2.0 * ramp) * slab_scale)
    mixed = own_part + common_weight * common_part
    return 0.017 * mixed * rising[:, None, None] * node_scale[None, None, :]


def draw_tip_block(key, part):
    key = jax.random.fold_in(key, 4)
    raw_part = jax.random.uniform(key, (FIXED_EFFECTS, FIXED_EFFECTS), jnp.float32, -1.0, 1.0)
    return 12.0 * jnp.eye(FIXED_EFFECTS, dtype=jnp.float32) + (raw_part + raw_part.T)


def setup_inputs(seed: int = 0) -> dict:
    key_list = jax.random.split(jax.random.key(seed), 5)
    diag_blocks = draw_diag_blocks(jax.random.fold_in(key_list[4], 71), 0)
    sub_blocks = draw_sub_blocks(jax.random.fold_in(key_list[4], 71), 0)
    arrow_blocks = draw_arrow_blocks(jax.random.fold_in(key_list[4], 71), 0)
    tip_block = draw_tip_block(jax.random.fold_in(key_list[4], 71), 0)
    return dict(diag_blocks=diag_blocks, sub_blocks=sub_blocks, arrow_blocks=arrow_blocks, tip_block=tip_block)


PRECISE = lax.Precision.HIGHEST

def gram_pair(former, latter):
    return jnp.matmul(former.T, latter, precision=PRECISE)

def blocked_cholesky(matrix):
    order = matrix.shape[0]
    block_rows = 512 if order % 512 == 0 else order
    if order <= block_rows:
        return jnp.linalg.cholesky(matrix)
    corner = jnp.linalg.cholesky(matrix[:block_rows, :block_rows])
    below = jax.scipy.linalg.solve_triangular(corner, matrix[block_rows:, :block_rows].T, lower=True).T
    remains = matrix[block_rows:, block_rows:] - jnp.matmul(below, below.T, precision=PRECISE)
    lower_rest = blocked_cholesky(remains)
    upper_rows = jnp.concatenate([corner, jnp.zeros((block_rows, order - block_rows), matrix.dtype)], axis=1)
    lower_rows = jnp.concatenate([below, lower_rest], axis=1)
    return jnp.concatenate([upper_rows, lower_rows], axis=0)

def eliminate(pivot_block, left_block, right_block, arrow_rows):
    factor_low = blocked_cholesky(pivot_block)
    node_count = pivot_block.shape[0]
    stacked = jnp.concatenate([left_block, right_block, arrow_rows.T], axis=1)
    solved = jax.scipy.linalg.solve_triangular(factor_low, stacked, lower=True)
    w_left = solved[:, :node_count]
    w_right = solved[:, node_count:2 * node_count]
    w_arrow = solved[:, 2 * node_count:]
    log_term = 2.0 * jnp.sum(jnp.log(jnp.diagonal(factor_low)))
    return (w_left, w_right, w_arrow, log_term)

def partition_sweep(operands):
    diag_part, sub_part, arrow_part, has_left = operands
    pivot_block = diag_part[0]
    left_block = sub_part[0] * has_left
    arrow_rows = arrow_part[0]
    lower_diag = jnp.zeros((MESH_NODES, MESH_NODES), jnp.float32)
    lower_arrow = jnp.zeros((FIXED_EFFECTS, MESH_NODES), jnp.float32)
    tip_terms = jnp.zeros((FIXED_EFFECTS, FIXED_EFFECTS), jnp.float32)
    log_total = jnp.zeros((), jnp.float32)
    for slab_index in range(LOCAL_SLABS - 1):
        w_left, w_right, w_arrow, log_term = eliminate(pivot_block, left_block, sub_part[slab_index + 1].T, arrow_rows)
        lower_diag = lower_diag + gram_pair(w_left, w_left)
        lower_arrow = lower_arrow + gram_pair(w_arrow, w_left)
        tip_terms = tip_terms + gram_pair(w_arrow, w_arrow)
        log_total = log_total + log_term
        pivot_block = diag_part[slab_index + 1] - gram_pair(w_right, w_right)
        left_block = -gram_pair(w_right, w_left)
        arrow_rows = arrow_part[slab_index + 1] - gram_pair(w_arrow, w_right)
    return (pivot_block, left_block, arrow_rows, lower_diag, lower_arrow, tip_terms, log_total)

def merge_one(operands):
    pivot_block, left_block, right_source, arrow_rows = operands
    w_left, w_right, w_arrow, log_term = eliminate(pivot_block, left_block, right_source.T, arrow_rows)
    return (gram_pair(w_left, w_left), gram_pair(w_arrow, w_left), gram_pair(w_right, w_right), -gram_pair(w_right, w_left), gram_pair(w_arrow, w_right), gram_pair(w_arrow, w_arrow), log_term)

def reference(diag_blocks, sub_blocks, arrow_blocks, tip_block):
    shaped = (N_TM, LOCAL_SLABS)
    has_left = (jnp.arange(N_TM) > 0).astype(jnp.float32)
    swept = lax.map(partition_sweep, (diag_blocks.reshape(shaped + (MESH_NODES, MESH_NODES)), sub_blocks.reshape(shaped + (MESH_NODES, MESH_NODES)), arrow_blocks.reshape(shaped + (FIXED_EFFECTS, MESH_NODES)), has_left))
    sep_diag, sep_left, sep_arrow, lower_diag, lower_arrow, tip_terms, log_terms = swept
    zero_block = jnp.zeros((1, MESH_NODES, MESH_NODES), jnp.float32)
    zero_rows = jnp.zeros((1, FIXED_EFFECTS, MESH_NODES), jnp.float32)
    sep_diag = sep_diag - jnp.concatenate([lower_diag[1:], zero_block], axis=0)
    sep_arrow = sep_arrow - jnp.concatenate([lower_arrow[1:], zero_rows], axis=0)
    tip_total = jnp.sum(tip_terms, axis=0)
    log_total = jnp.sum(log_terms)
    for level_index in range(LEVELS):
        stride = 2 ** level_index
        chosen = np.arange(stride - 1, N_TM, 2 * stride)
        beyond = chosen + stride
        outputs = lax.map(merge_one, (sep_diag[chosen], sep_left[chosen], sep_left[beyond], sep_arrow[chosen]))
        left_diag_upd, left_arrow_upd, right_diag_upd, fill_upd, right_arrow_upd, tip_upd, log_upd = outputs
        targets = chosen - stride
        valid = targets >= 0
        sep_diag = sep_diag.at[targets[valid]].add(-left_diag_upd[valid])
        sep_arrow = sep_arrow.at[targets[valid]].add(-left_arrow_upd[valid])
        sep_diag = sep_diag.at[beyond].add(-right_diag_upd)
        sep_left = sep_left.at[beyond].set(fill_upd)
        sep_arrow = sep_arrow.at[beyond].add(-right_arrow_upd)
        tip_total = tip_total + jnp.sum(tip_upd, axis=0)
        log_total = log_total + jnp.sum(log_upd)
    return (sep_diag, sep_left, sep_arrow, tip_block - tip_total, log_total)
```

```python
import functools

import jax
import jax.numpy as jnp
from jax import lax
from jax.experimental import pallas as pl
from jax.experimental.pallas import tpu as pltpu
from jax.sharding import PartitionSpec as P

F32 = jnp.float32
BF16 = jnp.bfloat16
TILE = 128


def row_of(value, index):
    return jnp.broadcast_to(value[index : index + 1, :], (8, value.shape[1]))


def column_of(value, index):
    return jnp.broadcast_to(value[:, index : index + 1], (8, TILE))


def split_three(value):
    high = value.astype(BF16).astype(F32)
    rest = value - high
    middle = rest.astype(BF16).astype(F32)
    return high, middle, rest - middle


def split_two(value):
    high = value.astype(BF16)
    return high, (value - high.astype(F32)).astype(BF16)


def left_pieces(value):
    high, low = split_two(value)
    return jnp.concatenate([high, low, high], axis=1)


def right_pieces(value):
    high, low = split_two(value)
    return jnp.concatenate([high, high, low], axis=0)


def outer_product(rows_a, rows_b):
    ah, am, al = split_three(rows_a)
    bh, bm, bl = split_three(rows_b)
    left = jnp.concatenate([ah, am, ah, am, al, ah], axis=0).astype(BF16)
    right = jnp.concatenate([bh, bh, bm, bm, bh, bl], axis=0).astype(BF16)
    return lax.dot_general(left, right, (((0,), (0,)), ((), ())), preferred_element_type=F32)


def sweep_tile(tile):
    lane = lax.broadcasted_iota(jnp.int32, (8, TILE), 1)
    sub = lax.broadcasted_iota(jnp.int32, (8, TILE), 0)
    pivots = jnp.ones((8, TILE), F32)
    count = TILE // 8
    rows = [tile[8 * i : 8 * i + 8, :] for i in range(count)]
    for i in range(count):
        source = rows[i]
        inside = (lane >= 8 * i) & (lane < 8 * i + 8)
        columns = [column_of(source, 8 * i + c) for c in range(8)]
        solved = jnp.where(lane == sub + 8 * i, -1.0, jnp.where(inside, 0.0, source))
        for c in range(8):
            pivot = row_of(columns[c], c)
            scale = 1.0 / pivot
            pivots = jnp.where(lane == 8 * i + c, pivot, pivots)
            pivot_row = row_of(solved, c) * scale
            solved = jnp.where(sub == c, pivot_row, solved - columns[c] * pivot_row)
            for d in range(c + 1, 8):
                entry = row_of(columns[d], c) * scale
                columns[d] = jnp.where(sub == c, entry, columns[d] - columns[c] * entry)
        update = outer_product(source, solved)
        for k in range(count):
            if k == i:
                continue
            kept = jnp.where(inside, 0.0, rows[k])
            if k == i + 1:
                for c in range(8):
                    kept = kept - column_of(rows[k], 8 * i + c) * row_of(solved, c)
                rows[k] = kept
            else:
                rows[k] = kept - update[8 * k : 8 * k + 8, :]
        rows[i] = solved
    return jnp.concatenate(rows, axis=0), pivots


def tile_span(index):
    return pl.ds(pl.multiple_of(index * TILE, TILE), TILE)


def inverse_kernel(order, source_ref, inverse_ref, log_ref, left_ref, right_ref):
    count = order // TILE

    def take(r, carry):
        inverse_ref[tile_span(r), :] = source_ref[tile_span(r), :]
        return carry

    lax.fori_loop(0, count, take, 0)

    def step(j, logs):
        here = tile_span(j)
        swept, pivots = sweep_tile(inverse_ref[here, here])
        rows = inverse_ref[here, :]
        lane = lax.broadcasted_iota(jnp.int32, (TILE, order), 1)
        inside = (lane >= j * TILE) & (lane < j * TILE + TILE)
        inverse_ref[here, here] = jnp.zeros((TILE, TILE), F32)
        for r in range(count):
            span = slice(r * TILE, (r + 1) * TILE)
            left_ref[span, :] = left_pieces(inverse_ref[span, here])
        solved = -jnp.dot(left_pieces(swept), right_pieces(rows), preferred_element_type=F32)
        solved = jnp.where(inside, jnp.concatenate([swept] * count, axis=1), solved)
        right_ref[...] = right_pieces(solved)
        inverse_ref[:, here] = jnp.zeros((order, TILE), F32)

        def update(r, carry):
            span = tile_span(r)
            inverse_ref[span, :] = inverse_ref[span, :] - jnp.dot(
                left_ref[span, :], right_ref[...], preferred_element_type=F32
            )
            return carry

        lax.fori_loop(0, count, update, 0)
        inverse_ref[here, :] = solved
        return logs + jnp.log(pivots)

    log_ref[...] = lax.fori_loop(0, count, step, jnp.zeros((8, TILE), F32))

    def negate(r, carry):
        inverse_ref[tile_span(r), :] = -inverse_ref[tile_span(r), :]
        return carry

    lax.fori_loop(0, count, negate, 0)


def inverse_and_log(matrix):
    order = matrix.shape[0]
    inverse, logs = pl.pallas_call(
        functools.partial(inverse_kernel, order),
        out_shape=[
            jax.ShapeDtypeStruct((order, order), F32),
            jax.ShapeDtypeStruct((8, TILE), F32),
        ],
        in_specs=[pl.BlockSpec(memory_space=pltpu.VMEM)],
        out_specs=[pl.BlockSpec(memory_space=pltpu.VMEM)] * 2,
        scratch_shapes=[pltpu.VMEM((order, 3 * TILE), BF16), pltpu.VMEM((3 * TILE, order), BF16)],
        compiler_params=pltpu.CompilerParams(vmem_limit_bytes=40 * 2**20),
        cost_estimate=pl.CostEstimate(
            flops=12 * order**3, bytes_accessed=8 * order**2, transcendentals=0
        ),
        name="spd_inverse",
    )(matrix)
    return inverse, jnp.sum(logs[0])


def times(left, right, left_dim=1, right_dim=0):
    return lax.dot_general(
        left, right, (((left_dim,), (right_dim,)), ((), ())), precision=lax.Precision.HIGH
    )


def both_cores(value, axis):
    return lax.all_gather(value, "blk", axis=axis, tiled=True)


def on_device(diag_blocks, sub_blocks, arrow_blocks, tip_block):
    partition = lax.axis_index("tm")
    parts = lax.axis_size("tm")
    even = partition % 2 == 0
    has_left = (partition > 0).astype(F32)
    half = diag_blocks.shape[2]
    start = lax.axis_index("blk") * half
    evens = range(0, parts, 2)

    pivot = both_cores(diag_blocks[0], 1)
    left_own = sub_blocks[0] * has_left
    left_full = both_cores(left_own, 1)
    right_rows = both_cores(sub_blocks[1], 1)
    arrow_full = both_cores(arrow_blocks[0], 1)
    inverse, log_first = inverse_and_log(pivot)
    x_left = times(inverse, left_own)
    x_right = times(inverse, lax.dynamic_slice_in_dim(right_rows, start, half, 0), 1, 1)
    lower = jnp.concatenate([times(left_full, x_left, 0, 0), times(arrow_full, x_left)], axis=0)
    upper = jnp.concatenate(
        [diag_blocks[1] - times(right_rows, x_right), arrow_blocks[1] - times(arrow_full, x_right)], axis=0
    )
    swap = [(p, p + 1) for p in evens] + [(p + 1, p) for p in evens]
    other = lax.ppermute(jnp.where(even, upper, lower), "tm", swap)
    separator = jnp.where(even, upper - other, other - lower)
    left_own = -times(right_rows, x_left)
    tip_first = times(times(arrow_full, inverse), arrow_full, 1, 1)
    down = [(p, p - 1) for p in evens if p > 0]
    lower_above = lax.ppermute(lower, "tm", down)
    left_pair = lax.ppermute(left_own, "tm", [(p, p + 1) for p in evens])
    left_full = both_cores(left_own, 1)

    node_count = diag_blocks.shape[1]
    separator_full = both_cores(separator, 1)
    arrow_full = separator_full[node_count:]
    inverse, log_second = inverse_and_log(separator_full[:node_count])
    x_left = times(inverse, jnp.where(even, left_own, left_pair))

    def keep_even(_):
        return jnp.concatenate([times(left_full, x_left, 0, 0), times(arrow_full, x_left)], axis=0), upper

    def keep_odd(_):
        x_right = times(inverse, lax.dynamic_slice_in_dim(left_full, start, half, 0), 1, 1)
        change = jnp.concatenate([times(left_full, x_right), times(arrow_full, x_right)], axis=0)
        return jnp.concatenate([-times(left_full, x_left), jnp.zeros_like(lower[node_count:])], axis=0), (
            upper - lower_above - change
        )

    product, kept = lax.cond(even, keep_even, keep_odd, 0)
    from_above = lax.ppermute(product, "tm", down)
    tip_second = times(times(arrow_full, inverse), arrow_full, 1, 1)
    result = jnp.where(even, separator, kept - from_above)
    left_result = jnp.where(even, left_own, product[:node_count])
    totals = lax.psum(
        (
            tip_first + jnp.where(even, tip_second, 0.0),
            log_first + jnp.where(even, log_second, 0.0),
        ),
        "tm",
    )
    return (
        result[:node_count][None],
        left_result[None],
        result[node_count:][None],
        tip_block - totals[0],
        totals[1],
    )


def solution(mesh):
    in_specs = (P("tm", None, "blk"), P("tm", None, "blk"), P("tm", None, "blk"), P())
    out_specs = (P("tm", None, "blk"), P("tm", None, "blk"), P("tm", None, "blk"), P(), P())
    return jax.shard_map(
        on_device, mesh=mesh, in_specs=in_specs, out_specs=out_specs, check_vma=False
    )
```

```python
import functools

import jax
import jax.numpy as jnp
from jax import lax
from jax.experimental import pallas as pl
from jax.experimental.pallas import tpu as pltpu
from jax.sharding import PartitionSpec as P

F32 = jnp.float32
BF16 = jnp.bfloat16
TILE = 128
BLOCK = 256
PACKED = 5
COPIES = 4


def row_of(value, index):
    return jnp.broadcast_to(value[index : index + 1, :], (8, value.shape[1]))


def column_of(value, index):
    return jnp.broadcast_to(value[:, index : index + 1], (8, TILE))


def split_three(value):
    high = value.astype(BF16).astype(F32)
    rest = value - high
    middle = rest.astype(BF16).astype(F32)
    return high, middle, rest - middle


def split_two(value):
    high = value.astype(BF16)
    return high, (value - high.astype(F32)).astype(BF16)


def left_pieces(value):
    high, low = split_two(value)
    return jnp.concatenate([high, low, high], axis=1)


def right_pieces(value):
    high, low = split_two(value)
    return jnp.concatenate([high, high, low], axis=0)


def outer_product(rows_a, rows_b):
    ah, am, al = split_three(rows_a)
    bh, bm, bl = split_three(rows_b)
    left = jnp.concatenate([ah, am, ah, am, al, ah], axis=0).astype(BF16)
    right = jnp.concatenate([bh, bh, bm, bm, bh, bl], axis=0).astype(BF16)
    return lax.dot_general(left, right, (((0,), (0,)), ((), ())), preferred_element_type=F32)


def sweep_tile(tile):
    lane = lax.broadcasted_iota(jnp.int32, (8, TILE), 1)
    sub = lax.broadcasted_iota(jnp.int32, (8, TILE), 0)
    pivots = jnp.ones((8, TILE), F32)
    count = TILE // 8
    rows = [tile[8 * i : 8 * i + 8, :] for i in range(count)]
    for i in range(count):
        source = rows[i]
        inside = (lane >= 8 * i) & (lane < 8 * i + 8)
        columns = [column_of(source, 8 * i + c) for c in range(8)]
        solved = jnp.where(lane == sub + 8 * i, -1.0, jnp.where(inside, 0.0, source))
        for c in range(8):
            pivot = row_of(columns[c], c)
            scale = 1.0 / pivot
            pivots = jnp.where(lane == 8 * i + c, pivot, pivots)
            pivot_row = row_of(solved, c) * scale
            solved = jnp.where(sub == c, pivot_row, solved - columns[c] * pivot_row)
            for d in range(c + 1, 8):
                entry = row_of(columns[d], c) * scale
                columns[d] = jnp.where(sub == c, entry, columns[d] - columns[c] * entry)
        update = outer_product(source, solved)
        for k in range(count):
            if k == i:
                continue
            kept = jnp.where(inside, 0.0, rows[k])
            if k == i + 1:
                for c in range(8):
                    kept = kept - column_of(rows[k], 8 * i + c) * row_of(solved, c)
                rows[k] = kept
            else:
                rows[k] = kept - update[8 * k : 8 * k + 8, :]
        rows[i] = solved
    return jnp.concatenate(rows, axis=0), pivots


def tile_span(index):
    return pl.ds(pl.multiple_of(index * TILE, TILE), TILE)


def eliminate_all(order, inverse_ref, log_ref, left_ref, right_ref):
    count = order // TILE

    def step(j, logs):
        here = tile_span(j)
        swept, pivots = sweep_tile(inverse_ref[here, here])
        rows = inverse_ref[here, :]
        lane = lax.broadcasted_iota(jnp.int32, (TILE, order), 1)
        inside = (lane >= j * TILE) & (lane < j * TILE + TILE)
        inverse_ref[here, here] = jnp.zeros((TILE, TILE), F32)
        for r in range(count):
            span = slice(r * TILE, (r + 1) * TILE)
            left_ref[span, :] = left_pieces(inverse_ref[span, here])
        solved = -jnp.dot(left_pieces(swept), right_pieces(rows), preferred_element_type=F32)
        solved = jnp.where(inside, jnp.concatenate([swept] * count, axis=1), solved)
        right_ref[...] = right_pieces(solved)
        inverse_ref[:, here] = jnp.zeros((order, TILE), F32)

        def update(r, carry):
            span = tile_span(r)
            inverse_ref[span, :] = inverse_ref[span, :] - jnp.dot(
                left_ref[span, :], right_ref[...], preferred_element_type=F32
            )
            return carry

        lax.fori_loop(0, count, update, 0)
        inverse_ref[here, :] = solved
        return logs + jnp.log(pivots)

    log_ref[...] = lax.fori_loop(0, count, step, jnp.zeros((8, TILE), F32))

    def negate(r, carry):
        inverse_ref[tile_span(r), :] = -inverse_ref[tile_span(r), :]
        return carry

    lax.fori_loop(0, count, negate, 0)


def inverse_kernel(source_ref, inverse_ref, log_ref, left_ref, right_ref):
    order = source_ref.shape[0]

    def take(r, carry):
        inverse_ref[tile_span(r), :] = source_ref[tile_span(r), :]
        return carry

    lax.fori_loop(0, order // TILE, take, 0)
    eliminate_all(order, inverse_ref, log_ref, left_ref, right_ref)


def packed_inverse_kernel(info_ref, both_ref, inverse_ref, log_ref, own_ref, left_ref, right_ref):
    order, half = own_ref.shape
    places = (((0, 0), (1, 0), (2, 0), (1, 1), (2, 1)), ((0, 3), (1, 3), (2, 3), (3, 3), (2, 2)))
    for source in range(2):
        for k, (row, column) in enumerate(places[source]):
            value = both_ref[source, k * BLOCK : (k + 1) * BLOCK, :]
            rows = slice(row * BLOCK, (row + 1) * BLOCK)
            columns = slice(column * BLOCK, (column + 1) * BLOCK)
            inverse_ref[rows, columns] = value
            if row != column:
                inverse_ref[columns, rows] = value.T
    own = pl.ds(pl.multiple_of(info_ref[0] * half, half), half)
    own_ref[...] = inverse_ref[:, own]
    eliminate_all(order, inverse_ref, log_ref, left_ref, right_ref)


def inverse_scratch(order):
    return [pltpu.VMEM((order, 3 * TILE), BF16), pltpu.VMEM((3 * TILE, order), BF16)]


def inverse_and_log(matrix):
    order = matrix.shape[0]
    return local_call(
        inverse_kernel, "first_inverse", 24 * order**3,
        out_shape=[shape_of(order, order), shape_of(8, TILE)],
        in_specs=vmem(1), out_specs=vmem(2), scratch_shapes=inverse_scratch(order),
    )(matrix)


def inverse_of_packed(info, both, order, half):
    return local_call(
        packed_inverse_kernel, "second_inverse", 24 * order**3,
        out_shape=[shape_of(order, order), shape_of(8, TILE), shape_of(order, half)],
        in_specs=[SMEM_SPEC, *vmem(1)], out_specs=vmem(3), scratch_shapes=inverse_scratch(order),
    )(info, both)


def times(left, right, left_dim=1, right_dim=0):
    dims = (((left_dim,), (right_dim,)), ((), ()))

    def dot(a, b):
        return lax.dot_general(a, b, dims, preferred_element_type=F32)

    return dot(left[0], right[0]) + (dot(left[0], right[1]) + dot(left[1], right[0]))


def split_rows(source, high_ref, low_ref):
    def part(r, carry):
        high, low = split_two(source[tile_span(r), :])
        high_ref[tile_span(r), :] = high
        low_ref[tile_span(r), :] = low
        return carry

    lax.fori_loop(0, high_ref.shape[0] // TILE, part, 0)


def block_span(index):
    return pl.ds(pl.multiple_of(index * BLOCK, BLOCK), BLOCK)


def packed_place(core, k):
    row = jnp.where(core == 0, jnp.where(k < 3, k, k - 2), jnp.where(k < 4, k, 2))
    column = jnp.where(core == 0, jnp.where(k < 3, 0, 1), jnp.where(k < 4, 1, 0))
    return row, column


def solve_into(inverse, right, out, right_dim):
    def part(r, carry):
        rows = block_span(r)
        value = times((inverse[0][rows, :], inverse[1][rows, :]), right, 1, right_dim)
        out[0][rows, :], out[1][rows, :] = split_two(value)
        return carry

    lax.fori_loop(0, inverse[0].shape[0] // BLOCK, part, 0)


def packed_gram(core, former, solved, left_dim, store):
    def part(k, carry):
        row, column = packed_place(core, k)
        if left_dim == 0:
            left = (former[0][:, block_span(row)], former[1][:, block_span(row)])
        else:
            left = (former[0][block_span(row), :], former[1][block_span(row), :])
        right = (solved[0][:, block_span(column)], solved[1][:, block_span(column)])
        store(k, row, column, times(left, right, left_dim, 0))
        return carry

    lax.fori_loop(0, PACKED, part, 0)


def arrow_pack(value):
    return jnp.concatenate([value[:, :BLOCK], value[:, BLOCK:]], axis=0)


def arrow_unpack(value):
    effects = value.shape[0] // 2
    return jnp.concatenate([value[:effects], value[effects:]], axis=1)


def first_products_kernel(
    info_ref, inverse_ref, sub_ref, arrow_ref, diag_ref, own_arrow_ref,
    swap_ref, lower_ref, upper_ref, xh_ref, xl_ref,
    vh, vl, bh, bl, sh, sl, yh, yl,
):
    core, even = info_ref[0], info_ref[1] == 1
    half = diag_ref.shape[2]
    own = pl.ds(pl.multiple_of(core * half, half), half)
    split_rows(inverse_ref, vh, vl)
    split_rows(sub_ref.at[0], bh, bl)
    split_rows(sub_ref.at[1], sh, sl)
    solve_into((vh, vl), (bh[:, own], bl[:, own]), (xh_ref, xl_ref), 0)
    solve_into((vh, vl), (sh[own, :], sl[own, :]), (yh, yl), 1)

    def store_lower(k, row, column, value):
        lower_ref[block_span(k), :] = value

    def store_upper(k, row, column, value):
        value = diag_ref[0, block_span(row), block_span(column)] - value
        upper_ref[block_span(k), :] = value
        swap_ref[block_span(k), :] = jnp.where(even, value, lower_ref[block_span(k), :])

    packed_gram(core, (bh, bl), (xh_ref, xl_ref), 0, store_lower)
    packed_gram(core, (sh, sl), (yh, yl), 1, store_upper)
    rows = split_two(arrow_ref[0])
    lower_arrow = arrow_pack(times(rows, (xh_ref[...], xl_ref[...])))
    upper_arrow = arrow_pack(own_arrow_ref[0] - times(rows, (yh[...], yl[...])))
    last = slice(PACKED * BLOCK, None)
    lower_ref[last, :] = lower_arrow
    upper_ref[last, :] = upper_arrow
    swap_ref[last, :] = jnp.where(even, upper_arrow, lower_arrow)


def arrow_form(rows, inverse_ref):
    pieces = split_two(rows)
    through = times(pieces, split_two(inverse_ref[...]))
    return times(split_two(through), pieces, 1, 1)


def first_fill_kernel(info_ref, inverse_ref, sub_ref, arrow_ref, xh_ref, xl_ref, left_ref, tip_ref, sh, sl):
    keep = info_ref[2] == 1
    split_rows(sub_ref.at[0], sh, sl)

    def part(r, carry):
        rows = block_span(r)
        value = -times((sh[rows, :], sl[rows, :]), (xh_ref[...], xl_ref[...]))
        left_ref[rows, :] = jnp.where(keep, value, 0.0)
        return carry

    lax.fori_loop(0, sh.shape[0] // BLOCK, part, 0)
    tip_ref[...] = arrow_form(arrow_ref[0], inverse_ref)


def separator_arrow(sep_ref):
    last = slice(PACKED * BLOCK, None)
    return jnp.concatenate([arrow_unpack(sep_ref[0, last, :]), arrow_unpack(sep_ref[1, last, :])], axis=1)


def second_products_kernel(
    info_ref, inverse_ref, left_ref, sep_ref, upper_ref, above_ref, out_ref, vh, vl, bh, bl, xh, xl
):
    core, even = info_ref[0], info_ref[1] == 1
    half = xh.shape[1]
    own = pl.ds(pl.multiple_of(core * half, half), half)
    split_rows(inverse_ref, vh, vl)
    split_rows(left_ref, bh, bl)
    rows = split_two(separator_arrow(sep_ref))
    last = slice(PACKED * BLOCK, None)

    @pl.when(even)
    def _():
        solve_into((vh, vl), (bh[:, own], bl[:, own]), (xh, xl), 0)

        def store(k, row, column, value):
            out_ref[block_span(k), :] = value

        packed_gram(core, (bh, bl), (xh, xl), 0, store)
        out_ref[last, :] = arrow_pack(times(rows, (xh[...], xl[...])))

    @pl.when(jnp.logical_not(even))
    def _():
        solve_into((vh, vl), (bh[own, :], bl[own, :]), (xh, xl), 1)

        def store(k, row, column, value):
            span = block_span(k)
            out_ref[span, :] = upper_ref[span, :] - above_ref[span, :] - value

        packed_gram(core, (bh, bl), (xh, xl), 1, store)
        change = arrow_pack(times(rows, (xh[...], xl[...])))
        out_ref[last, :] = upper_ref[last, :] - above_ref[last, :] - change


def second_fill_kernel(
    info_ref, inverse_ref, left_ref, sep_ref, own_ref, pair_ref, tip_ref, log_ref, log_two_ref,
    out_ref, sums_ref, vh, vl, bh, bl, xh, xl,
):
    even = info_ref[1] == 1
    effects = tip_ref.shape[0]
    sums_ref[...] = jnp.zeros_like(sums_ref)

    @pl.when(even)
    def _():
        out_ref[0] = own_ref[...]
        tip = tip_ref[...] + arrow_form(separator_arrow(sep_ref), inverse_ref)
        sums_ref[0:effects, 0:effects] = tip
        sums_ref[effects:, :] = log_ref[...] + log_two_ref[...]

    @pl.when(jnp.logical_not(even))
    def _():
        sums_ref[0:effects, 0:effects] = tip_ref[...]
        sums_ref[effects:, :] = log_ref[...]
        split_rows(inverse_ref, vh, vl)
        split_rows(left_ref, bh, bl)
        solve_into((vh, vl), split_two(pair_ref[...]), (xh, xl), 0)

        def part(r, carry):
            rows = block_span(r)
            out_ref[0, rows, :] = -times((bh[rows, :], bl[rows, :]), (xh[...], xl[...]))
            return carry

        lax.fori_loop(0, bh.shape[0] // BLOCK, part, 0)


def meet(devices):
    barrier = pltpu.get_barrier_semaphore()
    for device in devices:
        pl.semaphore_signal(barrier, inc=1, device_id=device, device_id_type=pl.DeviceIdType.MESH)
    pl.semaphore_wait(barrier, len(devices))


def gather_kernel(diag_ref, out_ref, local_sem, send_sem, recv_sem):
    core = lax.axis_index("blk")
    peer = {"blk": 1 - core}
    half = diag_ref.shape[2]
    rows = diag_ref.shape[1] // COPIES
    own = pl.ds(pl.multiple_of(core * half, half), half)
    local = pltpu.make_async_copy(diag_ref.at[0], out_ref.at[:, own], local_sem)
    local.start()
    meet([peer])
    copies = []
    for k in range(COPIES):
        span = pl.ds(k * rows, rows)
        copies.append(
            pltpu.make_async_remote_copy(
                src_ref=diag_ref.at[0, span, :],
                dst_ref=out_ref.at[span, own],
                send_sem=send_sem.at[k],
                recv_sem=recv_sem.at[k],
                device_id=peer,
                device_id_type=pl.DeviceIdType.MESH,
            )
        )
        copies[-1].start()
    local.wait()
    for copy in copies:
        copy.wait()


def combine_kernel(other_ref, upper_ref, lower_ref, out_ref, sum_ref, local_sem, send_sem, recv_sem):
    core = lax.axis_index("blk")
    even = lax.axis_index("tm") % 2 == 0
    peer = {"blk": 1 - core}
    other = other_ref[...]
    sum_ref[...] = jnp.where(even, upper_ref[...] - other, other - lower_ref[...])
    local = pltpu.make_async_copy(sum_ref, out_ref.at[core], local_sem)
    local.start()
    meet([peer])
    copies = []
    rows = sum_ref.shape[0] // COPIES
    for k in range(COPIES):
        span = pl.ds(k * rows, rows)
        copies.append(
            pltpu.make_async_remote_copy(
                src_ref=sum_ref.at[span, :],
                dst_ref=out_ref.at[core, span, :],
                send_sem=send_sem.at[k],
                recv_sem=recv_sem.at[k],
                device_id=peer,
                device_id_type=pl.DeviceIdType.MESH,
            )
        )
        copies[-1].start()
    local.wait()
    for copy in copies:
        copy.wait()


def finish_kernel(kept_ref, above_ref, out_ref, peer_ref, send_sem, recv_sem):
    core = lax.axis_index("blk")
    peer = {"blk": 1 - core}
    out_ref[...] = kept_ref[...] - above_ref[...]
    meet([peer])
    copies = []
    for slot, block in enumerate((2 - 2 * core, 4 - 3 * core)):
        copies.append(
            pltpu.make_async_remote_copy(
                src_ref=out_ref.at[block_span(block), :],
                dst_ref=peer_ref.at[pl.ds(slot * BLOCK, BLOCK), :],
                send_sem=send_sem.at[slot],
                recv_sem=recv_sem.at[slot],
                device_id=peer,
                device_id_type=pl.DeviceIdType.MESH,
            )
        )
        copies[-1].start()
    for copy in copies:
        copy.wait()


def place_kernel(info_ref, packed_ref, peer_ref, separator_ref, out_ref):
    core, even = info_ref[0], info_ref[1] == 1

    @pl.when(even)
    def _():
        out_ref[0] = separator_ref[...]

    def packed(k):
        return packed_ref[k * BLOCK : (k + 1) * BLOCK, :]

    def put(row, column, value):
        out_ref[0, row * BLOCK : (row + 1) * BLOCK, column * BLOCK : (column + 1) * BLOCK] = value

    first, second = peer_ref[:BLOCK, :], peer_ref[BLOCK:, :]
    odd = jnp.logical_not(even)

    @pl.when(odd & (core == 0))
    def _():
        for row, column, value in (
            (0, 0, packed(0)), (1, 0, packed(1)), (2, 0, packed(2)), (3, 0, first.T),
            (0, 1, packed(1).T), (1, 1, packed(3)), (2, 1, packed(4)), (3, 1, second.T),
        ):
            put(row, column, value)

    @pl.when(odd & (core == 1))
    def _():
        for row, column, value in (
            (0, 0, first.T), (1, 0, second.T), (2, 0, packed(4)), (3, 0, packed(2).T),
            (0, 1, packed(0)), (1, 1, packed(1)), (2, 1, packed(2)), (3, 1, packed(3)),
        ):
            put(row, column, value)


def reduce_kernel(sides, value_ref, out_ref, parts_ref, send_sem, recv_sem):
    me = lax.axis_index("tm")
    stages = []
    stride = 1
    for side in reversed(sides):
        place = (me // stride) % side
        stages.append((side, place, stride))
        stride = stride * side

    def other(stage, step):
        side, place, stride = stages[stage]
        return me + ((place + step) % side - place) * stride

    meet([{"tm": other(s, d)} for s in range(len(stages)) for d in range(1, stages[s][0])])
    out_ref[...] = value_ref[...]
    for s, (side, place, _) in enumerate(stages):
        parts_ref[s, place] = out_ref[...]
        copies = []
        for d in range(1, side):
            copies.append(
                pltpu.make_async_remote_copy(
                    src_ref=out_ref,
                    dst_ref=parts_ref.at[s, place],
                    send_sem=send_sem.at[s, d],
                    recv_sem=recv_sem.at[s, d],
                    device_id={"tm": other(s, d)},
                    device_id_type=pl.DeviceIdType.MESH,
                )
            )
            copies[-1].start()
        for copy in copies:
            copy.wait()
        total = parts_ref[s, 0]
        for k in range(1, side):
            total = total + parts_ref[s, k]
        out_ref[...] = total


def vmem(count):
    return [pl.BlockSpec(memory_space=pltpu.VMEM)] * count


def shape_of(*sizes, dtype=F32):
    return jax.ShapeDtypeStruct(sizes, dtype)


SMEM_SPEC = pl.BlockSpec(memory_space=pltpu.SMEM)
ANY_SPEC = pl.BlockSpec(memory_space=pl.ANY)


def local_call(kernel, name, flops, **kwargs):
    return pl.pallas_call(
        kernel,
        compiler_params=pltpu.CompilerParams(vmem_limit_bytes=56 * 2**20),
        cost_estimate=pl.CostEstimate(flops=flops, bytes_accessed=2**23, transcendentals=0),
        name=name,
        **kwargs,
    )


def remote_call(kernel, name, identity, **kwargs):
    return pl.pallas_call(
        kernel,
        compiler_params=pltpu.CompilerParams(
            collective_id=identity, has_side_effects=True, vmem_limit_bytes=24 * 2**20
        ),
        name=name,
        **kwargs,
    )


def dma_sems(*shape):
    return pltpu.SemaphoreType.DMA(shape)


def whole(shape, index):
    return pl.BlockSpec(shape, lambda i: index, pipeline_mode=pl.Buffered(1))


def on_device(diag_blocks, sub_blocks, arrow_blocks, tip_block):
    partition = lax.axis_index("tm")
    parts = lax.axis_size("tm")
    order, half = diag_blocks.shape[1:]
    effects = arrow_blocks.shape[1]
    packed_rows = PACKED * BLOCK + effects * half // BLOCK
    evens = range(0, parts, 2)
    down = [(p, p - 1) for p in evens if p > 0]
    core = lax.axis_index("blk")
    info = jnp.stack([core, (partition % 2 == 0).astype(core.dtype), (partition > 0).astype(core.dtype)])
    square, tall = (order, order), (order, half)
    big = [pltpu.VMEM(square, BF16)] * 2
    thin = [pltpu.VMEM(tall, BF16)] * 2

    pivot = remote_call(
        gather_kernel, "gather_pivot", 1,
        out_shape=shape_of(*square), in_specs=[ANY_SPEC], out_specs=ANY_SPEC,
        scratch_shapes=[pltpu.SemaphoreType.DMA, dma_sems(COPIES), dma_sems(COPIES)],
    )(diag_blocks)
    sub_full = lax.all_gather(sub_blocks, "blk", axis=2, tiled=True)
    arrow_full = lax.all_gather(arrow_blocks, "blk", axis=2, tiled=True)
    inverse, log_first = inverse_and_log(pivot)

    packed_shape = shape_of(packed_rows, BLOCK)
    swap, lower, upper, x_high, x_low = local_call(
        first_products_kernel, "first_products", 10 * order**3,
        grid=(1,),
        out_shape=[packed_shape] * 3 + [shape_of(*tall, dtype=BF16)] * 2,
        in_specs=[SMEM_SPEC, *vmem(3), whole((1, *tall), (1, 0, 0)), whole((1, effects, half), (1, 0, 0))],
        out_specs=vmem(5),
        scratch_shapes=big * 3 + thin,
    )(info, inverse, sub_full, arrow_full, diag_blocks, arrow_blocks)
    pairs = [(p, p + 1) for p in evens]
    other = lax.ppermute(swap, "tm", pairs + [(b, a) for a, b in pairs])
    left_own, tip_first = local_call(
        first_fill_kernel, "first_fill", 3 * order**3,
        grid=(1,),
        out_shape=[shape_of(*tall), shape_of(effects, effects)],
        in_specs=[SMEM_SPEC, *vmem(1), whole((1, *square), (1, 0, 0)), whole((1, effects, order), (0, 0, 0)), *vmem(2)],
        out_specs=vmem(2),
        scratch_shapes=big,
    )(info, inverse, sub_full, arrow_full, x_high, x_low)
    lower_above = lax.ppermute(lower, "tm", down)
    left_pair = lax.ppermute(left_own, "tm", pairs)
    left_full = lax.all_gather(left_own, "blk", axis=1, tiled=True)

    both = remote_call(
        combine_kernel, "gather_separator", 2,
        out_shape=shape_of(2, packed_rows, BLOCK), in_specs=vmem(3), out_specs=ANY_SPEC,
        scratch_shapes=[
            pltpu.VMEM((packed_rows, BLOCK), F32),
            pltpu.SemaphoreType.DMA, dma_sems(COPIES), dma_sems(COPIES),
        ],
    )(other, upper, lower)
    inverse, log_second, separator = inverse_of_packed(info, both, order, half)
    product = local_call(
        second_products_kernel, "second_products", 5 * order**3,
        out_shape=packed_shape,
        in_specs=[SMEM_SPEC, *vmem(5)],
        out_specs=vmem(1)[0],
        scratch_shapes=big * 2 + thin,
    )(info, inverse, left_full, both, upper, lower_above)
    above = lax.ppermute(product, "tm", down)
    left_result, sums = local_call(
        second_fill_kernel, "second_fill", 6 * order**3,
        out_shape=[shape_of(1, *tall), shape_of(effects + 8, TILE)],
        in_specs=[SMEM_SPEC, *vmem(8)],
        out_specs=vmem(2),
        scratch_shapes=big * 2 + thin,
    )(info, inverse, left_full, both, left_own, left_pair, tip_first, log_first, log_second)
    sides = side_lengths(parts)
    totals = remote_call(
        functools.partial(reduce_kernel, sides), "reduce_terms", 3,
        out_shape=shape_of(effects + 8, TILE), in_specs=vmem(1), out_specs=vmem(1)[0],
        scratch_shapes=[
            pltpu.VMEM((len(sides), max(sides), effects + 8, TILE), F32),
            dma_sems(len(sides), max(sides)), dma_sems(len(sides), max(sides)),
        ],
    )(sums)
    packed, swapped = remote_call(
        finish_kernel, "finish_blocks", 4,
        out_shape=[packed_shape, shape_of(2 * BLOCK, BLOCK)], in_specs=vmem(2), out_specs=vmem(2),
        scratch_shapes=[dma_sems(2), dma_sems(2)],
    )(product, above)
    diag_result = local_call(
        place_kernel, "place_blocks", 2**20,
        out_shape=shape_of(1, *tall), in_specs=[SMEM_SPEC, *vmem(3)], out_specs=vmem(1)[0],
    )(info, packed, swapped, separator)
    last = PACKED * BLOCK
    own_arrow = lax.dynamic_index_in_dim(both[:, last:], core, 0, keepdims=False)
    arrow_result = arrow_unpack(jnp.where(info[1] == 1, own_arrow, packed[last:]))
    return (
        diag_result,
        left_result,
        arrow_result[None],
        tip_block - totals[:effects, :effects],
        jnp.sum(totals[effects]),
    )


def side_lengths(parts):
    sides = []
    while parts > 1:
        side = 4 if parts % 4 == 0 else parts
        sides.append(side)
        parts //= side
    return tuple(sides)


def solution(mesh):
    in_specs = (P("tm", None, "blk"), P("tm", None, "blk"), P("tm", None, "blk"), P())
    out_specs = (P("tm", None, "blk"), P("tm", None, "blk"), P("tm", None, "blk"), P(), P())
    return jax.shard_map(
        on_device, mesh=mesh, in_specs=in_specs, out_specs=out_specs, check_vma=False
    )
```

```python
import functools

import jax
import jax.numpy as jnp
from jax import lax
from jax.experimental import pallas as pl
from jax.experimental.pallas import tpu as pltpu
from jax.sharding import PartitionSpec as P

F32 = jnp.float32
BF16 = jnp.bfloat16
TILE = 128
BLOCK = 256
PACKED = 5
COPIES = 4
GROUP = 2
SLOTS = TILE // (8 * GROUP)


def row_of(value, index):
    return jnp.broadcast_to(value[index : index + 1, :], (8, value.shape[1]))


def column_of(value, index):
    return jnp.broadcast_to(value[:, index : index + 1], (8, TILE))


def split_three(value):
    high = value.astype(BF16).astype(F32)
    rest = value - high
    middle = rest.astype(BF16).astype(F32)
    return high, middle, rest - middle


def split_two(value):
    high = value.astype(BF16)
    return high, (value - high.astype(F32)).astype(BF16)


def left_pieces(value):
    high, low = split_two(value)
    return jnp.concatenate([high, low, high], axis=1)


def right_pieces(value):
    high, low = split_two(value)
    return jnp.concatenate([high, high, low], axis=0)


def outer_product(rows_a, rows_b):
    ah, am, al = split_three(rows_a)
    bh, bm, bl = split_three(rows_b)
    left = jnp.concatenate([ah, am, ah, am, al, ah], axis=0).astype(BF16)
    right = jnp.concatenate([bh, bh, bm, bm, bh, bl], axis=0).astype(BF16)
    return lax.dot_general(left, right, (((0,), (0,)), ((), ())), preferred_element_type=F32)


def sweep_rows(rows, first, pivots, lane, sub):
    count = 8 * len(rows)
    columns = [[column_of(row, first + c) for c in range(count)] for row in rows]
    inside = (lane >= first) & (lane < first + count)
    solved = [
        jnp.where(lane == sub + first + 8 * h, -1.0, jnp.where(inside, 0.0, row)) for h, row in enumerate(rows)
    ]
    for c in range(count):
        group, place = c // 8, c % 8
        pivot = row_of(columns[group][c], place)
        scale = 1.0 / pivot
        pivots = jnp.where(lane == first + c, pivot, pivots)
        pivot_row = row_of(solved[group], place) * scale
        for h in range(len(rows)):
            value = solved[h] - columns[h][c] * pivot_row
            solved[h] = jnp.where(sub == place, pivot_row, value) if h == group else value
        for d in range(c + 1, count):
            entry = row_of(columns[group][d], place) * scale
            for h in range(len(rows)):
                value = columns[h][d] - columns[h][c] * entry
                columns[h][d] = jnp.where(sub == place, entry, value) if h == group else value
    return solved, pivots


def sweep_tile(tile, beside=None):
    lane = lax.broadcasted_iota(jnp.int32, (8, TILE), 1)
    sub = lax.broadcasted_iota(jnp.int32, (8, TILE), 0)
    pivots = jnp.ones((8, TILE), F32)
    width = 8 * GROUP
    rows = [tile[8 * i : 8 * i + 8, :] for i in range(TILE // 8)]
    for i in range(TILE // width):
        source = rows[GROUP * i : GROUP * i + GROUP]
        inside = (lane >= width * i) & (lane < width * i + width)
        solved, pivots = sweep_rows(source, width * i, pivots, lane, sub)
        update = outer_product(jnp.concatenate(source, axis=0), jnp.concatenate(solved, axis=0))
        for k in range(TILE // 8):
            if k // GROUP == i:
                continue
            kept = jnp.where(inside, 0.0, rows[k])
            if k == GROUP * (i + 1):
                for c in range(width):
                    kept = kept - column_of(rows[k], width * i + c) * row_of(solved[c // 8], c % 8)
                rows[k] = kept
            else:
                rows[k] = kept - update[8 * k : 8 * k + 8, :]
        rows[GROUP * i : GROUP * i + GROUP] = solved
        if beside is not None:
            beside(i)
    return jnp.concatenate(rows, axis=0), pivots


def tile_span(index):
    return pl.ds(pl.multiple_of(index * TILE, TILE), TILE)


def close_tile(order, matrix_ref, left_ref, swept_ref, tile_ref, j, swept):
    count = order // TILE
    here, there = tile_span(j), tile_span(lax.rem(j + 1, count))
    swept_ref[...] = swept
    solved = jnp.dot(left_pieces(swept), right_pieces(matrix_ref[here, there]), preferred_element_type=F32)
    tile_ref[...] = matrix_ref[there, there] + jnp.dot(
        left_pieces(matrix_ref[there, here]), right_pieces(solved), preferred_element_type=F32
    )
    matrix_ref[here, here] = jnp.zeros((TILE, TILE), F32)
    for r in range(count):
        span = slice(r * TILE, (r + 1) * TILE)
        left_ref[span, :] = left_pieces(matrix_ref[span, here])
    matrix_ref[:, here] = jnp.zeros((order, TILE), F32)
    matrix_ref[here, here] = swept


def solve_tile_rows(order, matrix_ref, swept_ref, right_ref, j):
    here = tile_span(j)
    rows = matrix_ref[here, :]
    lane = lax.broadcasted_iota(jnp.int32, (TILE, order), 1)
    inside = (lane >= j * TILE) & (lane < j * TILE + TILE)
    solved = -jnp.dot(left_pieces(swept_ref[...]), right_pieces(rows), preferred_element_type=F32)
    solved = jnp.where(inside, rows, solved)
    right_ref[...] = right_pieces(solved)
    matrix_ref[here, :] = solved


def update_rows(matrix_ref, left_ref, right_ref, span):
    matrix_ref[span, :] = matrix_ref[span, :] - jnp.dot(
        left_ref[span, :], right_ref[...], preferred_element_type=F32
    )


def eliminate_all(order, matrix_ref, log_ref, left_ref, right_ref, swept_ref, tile_ref):
    count = order // TILE
    swept, pivots = sweep_tile(matrix_ref[0:TILE, 0:TILE])
    close_tile(order, matrix_ref, left_ref, swept_ref, tile_ref, 0, swept)

    def step(j, logs):
        def beside(i):
            if i == 0:
                solve_tile_rows(order, matrix_ref, swept_ref, right_ref, j - 1)
                return
            first = (i - 1) * count // (SLOTS - 1)
            for r in range(first, i * count // (SLOTS - 1)):
                update_rows(matrix_ref, left_ref, right_ref, slice(r * TILE, (r + 1) * TILE))

        swept, pivots = sweep_tile(tile_ref[...], beside)
        close_tile(order, matrix_ref, left_ref, swept_ref, tile_ref, j, swept)
        return logs + jnp.log(pivots)

    log_ref[...] = lax.fori_loop(1, count, step, jnp.log(pivots))
    solve_tile_rows(order, matrix_ref, swept_ref, right_ref, count - 1)

    def update(r, carry):
        update_rows(matrix_ref, left_ref, right_ref, tile_span(r))
        return carry

    lax.fori_loop(0, count, update, 0)


def inverse_kernel(source_ref, inverse_ref, log_ref, *scratch):
    order = source_ref.shape[0]

    def take(r, carry):
        inverse_ref[tile_span(r), :] = source_ref[tile_span(r), :]
        return carry

    lax.fori_loop(0, order // TILE, take, 0)
    eliminate_all(order, inverse_ref, log_ref, *scratch)


def packed_inverse_kernel(info_ref, both_ref, inverse_ref, log_ref, own_ref, *scratch):
    order, half = own_ref.shape
    places = (((0, 0), (1, 0), (2, 0), (1, 1), (2, 1)), ((0, 3), (1, 3), (2, 3), (3, 3), (2, 2)))
    for source in range(2):
        for k, (row, column) in enumerate(places[source]):
            value = both_ref[source, k * BLOCK : (k + 1) * BLOCK, :]
            rows = slice(row * BLOCK, (row + 1) * BLOCK)
            columns = slice(column * BLOCK, (column + 1) * BLOCK)
            inverse_ref[rows, columns] = value
            if row != column:
                inverse_ref[columns, rows] = value.T
    own = pl.ds(pl.multiple_of(info_ref[0] * half, half), half)
    own_ref[...] = inverse_ref[:, own]
    eliminate_all(order, inverse_ref, log_ref, *scratch)


def inverse_scratch(order):
    return [
        pltpu.VMEM((order, 3 * TILE), BF16),
        pltpu.VMEM((3 * TILE, order), BF16),
        pltpu.VMEM((TILE, TILE), F32),
        pltpu.VMEM((TILE, TILE), F32),
    ]


def inverse_and_log(matrix):
    order = matrix.shape[0]
    return local_call(
        inverse_kernel, "first_inverse", 24 * order**3, 16,
        out_shape=[shape_of(order, order), shape_of(8, TILE)],
        in_specs=vmem(1), out_specs=vmem(2), scratch_shapes=inverse_scratch(order),
    )(matrix)


def inverse_of_packed(info, both, order, half):
    return local_call(
        packed_inverse_kernel, "second_inverse", 24 * order**3, 20,
        out_shape=[shape_of(order, order), shape_of(8, TILE), shape_of(order, half)],
        in_specs=[SMEM_SPEC, *vmem(1)], out_specs=vmem(3), scratch_shapes=inverse_scratch(order),
    )(info, both)


def times(left, right, left_dim=1, right_dim=0):
    dims = (((left_dim,), (right_dim,)), ((), ()))

    def dot(a, b):
        return lax.dot_general(a, b, dims, preferred_element_type=F32)

    return dot(left[0], right[0]) + (dot(left[0], right[1]) + dot(left[1], right[0]))


def split_rows(source, high_ref, low_ref, sign=1):
    def part(r, carry):
        high, low = split_two(sign * source[tile_span(r), :])
        high_ref[tile_span(r), :] = high
        low_ref[tile_span(r), :] = low
        return carry

    lax.fori_loop(0, high_ref.shape[0] // TILE, part, 0)


def block_span(index):
    return pl.ds(pl.multiple_of(index * BLOCK, BLOCK), BLOCK)


def packed_place(core, k):
    row = jnp.where(core == 0, jnp.where(k < 3, k, k - 2), jnp.where(k < 4, k, 2))
    column = jnp.where(core == 0, jnp.where(k < 3, 0, 1), jnp.where(k < 4, 1, 0))
    return row, column


def solve_into(inverse, right, out, right_dim):
    def part(r, carry):
        rows = block_span(r)
        value = times((inverse[0][rows, :], inverse[1][rows, :]), right, 1, right_dim)
        out[0][rows, :], out[1][rows, :] = split_two(value)
        return carry

    lax.fori_loop(0, inverse[0].shape[0] // BLOCK, part, 0)


def packed_gram(core, former, solved, left_dim, store):
    def part(k, carry):
        row, column = packed_place(core, k)
        if left_dim == 0:
            left = (former[0][:, block_span(row)], former[1][:, block_span(row)])
        else:
            left = (former[0][block_span(row), :], former[1][block_span(row), :])
        right = (solved[0][:, block_span(column)], solved[1][:, block_span(column)])
        store(k, row, column, times(left, right, left_dim, 0))
        return carry

    lax.fori_loop(0, PACKED, part, 0)


def arrow_pack(value):
    return jnp.concatenate([value[:, :BLOCK], value[:, BLOCK:]], axis=0)


def arrow_unpack(value):
    effects = value.shape[0] // 2
    return jnp.concatenate([value[:effects], value[effects:]], axis=1)


def first_products_kernel(
    info_ref, inverse_ref, sub_ref, arrow_ref, diag_ref, own_arrow_ref,
    swap_ref, lower_ref, upper_ref, xh_ref, xl_ref,
    vh, vl, bh, bl, sh, sl, yh, yl,
):
    core, even = info_ref[0], info_ref[1] == 1
    half = diag_ref.shape[2]
    own = pl.ds(pl.multiple_of(core * half, half), half)
    split_rows(inverse_ref, vh, vl, -1)
    split_rows(sub_ref.at[0], bh, bl)
    split_rows(sub_ref.at[1], sh, sl)
    solve_into((vh, vl), (bh[:, own], bl[:, own]), (xh_ref, xl_ref), 0)
    solve_into((vh, vl), (sh[own, :], sl[own, :]), (yh, yl), 1)

    def store_lower(k, row, column, value):
        lower_ref[block_span(k), :] = value

    def store_upper(k, row, column, value):
        value = diag_ref[0, block_span(row), block_span(column)] - value
        upper_ref[block_span(k), :] = value
        swap_ref[block_span(k), :] = jnp.where(even, value, lower_ref[block_span(k), :])

    packed_gram(core, (bh, bl), (xh_ref, xl_ref), 0, store_lower)
    packed_gram(core, (sh, sl), (yh, yl), 1, store_upper)
    rows = split_two(arrow_ref[0])
    lower_arrow = arrow_pack(times(rows, (xh_ref[...], xl_ref[...])))
    upper_arrow = arrow_pack(own_arrow_ref[0] - times(rows, (yh[...], yl[...])))
    last = slice(PACKED * BLOCK, None)
    lower_ref[last, :] = lower_arrow
    upper_ref[last, :] = upper_arrow
    swap_ref[last, :] = jnp.where(even, upper_arrow, lower_arrow)


def arrow_form(rows, inverse_ref):
    pieces = split_two(rows)
    through = -times(pieces, split_two(inverse_ref[...]))
    return times(split_two(through), pieces, 1, 1)


def first_fill_kernel(info_ref, inverse_ref, sub_ref, arrow_ref, xh_ref, xl_ref, left_ref, tip_ref, sh, sl):
    keep = info_ref[2] == 1
    split_rows(sub_ref.at[0], sh, sl)

    def part(r, carry):
        rows = block_span(r)
        value = -times((sh[rows, :], sl[rows, :]), (xh_ref[...], xl_ref[...]))
        left_ref[rows, :] = jnp.where(keep, value, 0.0)
        return carry

    lax.fori_loop(0, sh.shape[0] // BLOCK, part, 0)
    tip_ref[...] = arrow_form(arrow_ref[0], inverse_ref)


def separator_arrow(sep_ref):
    last = slice(PACKED * BLOCK, None)
    return jnp.concatenate([arrow_unpack(sep_ref[0, last, :]), arrow_unpack(sep_ref[1, last, :])], axis=1)


def second_products_kernel(
    info_ref, inverse_ref, left_ref, sep_ref, upper_ref, above_ref, out_ref, vh, vl, bh, bl, xh, xl
):
    core, even = info_ref[0], info_ref[1] == 1
    half = xh.shape[1]
    own = pl.ds(pl.multiple_of(core * half, half), half)
    split_rows(inverse_ref, vh, vl, -1)
    split_rows(left_ref, bh, bl)
    rows = split_two(separator_arrow(sep_ref))
    last = slice(PACKED * BLOCK, None)

    @pl.when(even)
    def _():
        solve_into((vh, vl), (bh[:, own], bl[:, own]), (xh, xl), 0)

        def store(k, row, column, value):
            out_ref[block_span(k), :] = value

        packed_gram(core, (bh, bl), (xh, xl), 0, store)
        out_ref[last, :] = arrow_pack(times(rows, (xh[...], xl[...])))

    @pl.when(jnp.logical_not(even))
    def _():
        solve_into((vh, vl), (bh[own, :], bl[own, :]), (xh, xl), 1)

        def store(k, row, column, value):
            span = block_span(k)
            out_ref[span, :] = upper_ref[span, :] - above_ref[span, :] - value

        packed_gram(core, (bh, bl), (xh, xl), 1, store)
        change = arrow_pack(times(rows, (xh[...], xl[...])))
        out_ref[last, :] = upper_ref[last, :] - above_ref[last, :] - change


def second_fill_kernel(
    info_ref, inverse_ref, left_ref, sep_ref, own_ref, pair_ref, tip_ref, log_ref, log_two_ref,
    out_ref, sums_ref, vh, vl, bh, bl, xh, xl,
):
    even = info_ref[1] == 1
    effects = tip_ref.shape[0]
    sums_ref[...] = jnp.zeros_like(sums_ref)

    @pl.when(even)
    def _():
        out_ref[0] = own_ref[...]
        tip = tip_ref[...] + arrow_form(separator_arrow(sep_ref), inverse_ref)
        sums_ref[0:effects, 0:effects] = tip
        sums_ref[effects:, :] = log_ref[...] + log_two_ref[...]

    @pl.when(jnp.logical_not(even))
    def _():
        sums_ref[0:effects, 0:effects] = tip_ref[...]
        sums_ref[effects:, :] = log_ref[...]
        split_rows(inverse_ref, vh, vl, -1)
        split_rows(left_ref, bh, bl)
        solve_into((vh, vl), split_two(pair_ref[...]), (xh, xl), 0)

        def part(r, carry):
            rows = block_span(r)
            out_ref[0, rows, :] = -times((bh[rows, :], bl[rows, :]), (xh[...], xl[...]))
            return carry

        lax.fori_loop(0, bh.shape[0] // BLOCK, part, 0)


def meet(devices):
    barrier = pltpu.get_barrier_semaphore()
    for device in devices:
        pl.semaphore_signal(barrier, inc=1, device_id=device, device_id_type=pl.DeviceIdType.MESH)
    pl.semaphore_wait(barrier, len(devices))


def gather_kernel(diag_ref, out_ref, local_sem, send_sem, recv_sem):
    core = lax.axis_index("blk")
    peer = {"blk": 1 - core}
    half = diag_ref.shape[2]
    rows = diag_ref.shape[1] // COPIES
    own = pl.ds(pl.multiple_of(core * half, half), half)
    local = pltpu.make_async_copy(diag_ref.at[0], out_ref.at[:, own], local_sem)
    local.start()
    meet([peer])
    copies = []
    for k in range(COPIES):
        span = pl.ds(k * rows, rows)
        copies.append(
            pltpu.make_async_remote_copy(
                src_ref=diag_ref.at[0, span, :],
                dst_ref=out_ref.at[span, own],
                send_sem=send_sem.at[k],
                recv_sem=recv_sem.at[k],
                device_id=peer,
                device_id_type=pl.DeviceIdType.MESH,
            )
        )
        copies[-1].start()
    local.wait()
    for copy in copies:
        copy.wait()


def combine_kernel(other_ref, upper_ref, lower_ref, out_ref, sum_ref, local_sem, send_sem, recv_sem):
    core = lax.axis_index("blk")
    even = lax.axis_index("tm") % 2 == 0
    peer = {"blk": 1 - core}
    other = other_ref[...]
    sum_ref[...] = jnp.where(even, upper_ref[...] - other, other - lower_ref[...])
    local = pltpu.make_async_copy(sum_ref, out_ref.at[core], local_sem)
    local.start()
    meet([peer])
    copies = []
    rows = sum_ref.shape[0] // COPIES
    for k in range(COPIES):
        span = pl.ds(k * rows, rows)
        copies.append(
            pltpu.make_async_remote_copy(
                src_ref=sum_ref.at[span, :],
                dst_ref=out_ref.at[core, span, :],
                send_sem=send_sem.at[k],
                recv_sem=recv_sem.at[k],
                device_id=peer,
                device_id_type=pl.DeviceIdType.MESH,
            )
        )
        copies[-1].start()
    local.wait()
    for copy in copies:
        copy.wait()


def finish_kernel(kept_ref, above_ref, out_ref, peer_ref, send_sem, recv_sem):
    core = lax.axis_index("blk")
    peer = {"blk": 1 - core}
    out_ref[...] = kept_ref[...] - above_ref[...]
    meet([peer])
    copies = []
    for slot, block in enumerate((2 - 2 * core, 4 - 3 * core)):
        copies.append(
            pltpu.make_async_remote_copy(
                src_ref=out_ref.at[block_span(block), :],
                dst_ref=peer_ref.at[pl.ds(slot * BLOCK, BLOCK), :],
                send_sem=send_sem.at[slot],
                recv_sem=recv_sem.at[slot],
                device_id=peer,
                device_id_type=pl.DeviceIdType.MESH,
            )
        )
        copies[-1].start()
    for copy in copies:
        copy.wait()


def place_kernel(info_ref, packed_ref, peer_ref, separator_ref, out_ref):
    core, even = info_ref[0], info_ref[1] == 1

    @pl.when(even)
    def _():
        out_ref[0] = separator_ref[...]

    def packed(k):
        return packed_ref[k * BLOCK : (k + 1) * BLOCK, :]

    def put(row, column, value):
        out_ref[0, row * BLOCK : (row + 1) * BLOCK, column * BLOCK : (column + 1) * BLOCK] = value

    first, second = peer_ref[:BLOCK, :], peer_ref[BLOCK:, :]
    odd = jnp.logical_not(even)

    @pl.when(odd & (core == 0))
    def _():
        for row, column, value in (
            (0, 0, packed(0)), (1, 0, packed(1)), (2, 0, packed(2)), (3, 0, first.T),
            (0, 1, packed(1).T), (1, 1, packed(3)), (2, 1, packed(4)), (3, 1, second.T),
        ):
            put(row, column, value)

    @pl.when(odd & (core == 1))
    def _():
        for row, column, value in (
            (0, 0, first.T), (1, 0, second.T), (2, 0, packed(4)), (3, 0, packed(2).T),
            (0, 1, packed(0)), (1, 1, packed(1)), (2, 1, packed(2)), (3, 1, packed(3)),
        ):
            put(row, column, value)


def reduce_kernel(sides, value_ref, out_ref, parts_ref, send_sem, recv_sem):
    me = lax.axis_index("tm")
    stages = []
    stride = 1
    for side in reversed(sides):
        place = (me // stride) % side
        stages.append((side, place, stride))
        stride = stride * side

    def other(stage, step):
        side, place, stride = stages[stage]
        return me + ((place + step) % side - place) * stride

    meet([{"tm": other(s, d)} for s in range(len(stages)) for d in range(1, stages[s][0])])
    out_ref[...] = value_ref[...]
    for s, (side, place, _) in enumerate(stages):
        parts_ref[s, place] = out_ref[...]
        copies = []
        for d in range(1, side):
            copies.append(
                pltpu.make_async_remote_copy(
                    src_ref=out_ref,
                    dst_ref=parts_ref.at[s, place],
                    send_sem=send_sem.at[s, d],
                    recv_sem=recv_sem.at[s, d],
                    device_id={"tm": other(s, d)},
                    device_id_type=pl.DeviceIdType.MESH,
                )
            )
            copies[-1].start()
        for copy in copies:
            copy.wait()
        total = parts_ref[s, 0]
        for k in range(1, side):
            total = total + parts_ref[s, k]
        out_ref[...] = total


def vmem(count):
    return [pl.BlockSpec(memory_space=pltpu.VMEM)] * count


def shape_of(*sizes, dtype=F32):
    return jax.ShapeDtypeStruct(sizes, dtype)


SMEM_SPEC = pl.BlockSpec(memory_space=pltpu.SMEM)
ANY_SPEC = pl.BlockSpec(memory_space=pl.ANY)


def local_call(kernel, name, flops, mebibytes, **kwargs):
    return pl.pallas_call(
        kernel,
        compiler_params=pltpu.CompilerParams(vmem_limit_bytes=mebibytes * 2**20),
        cost_estimate=pl.CostEstimate(flops=flops, bytes_accessed=2**23, transcendentals=0),
        name=name,
        **kwargs,
    )


def remote_call(kernel, name, identity, **kwargs):
    return pl.pallas_call(
        kernel,
        compiler_params=pltpu.CompilerParams(
            collective_id=identity, has_side_effects=True, vmem_limit_bytes=24 * 2**20
        ),
        name=name,
        **kwargs,
    )


def dma_sems(*shape):
    return pltpu.SemaphoreType.DMA(shape)


def whole(shape, index):
    return pl.BlockSpec(shape, lambda i: index, pipeline_mode=pl.Buffered(1))


def on_device(diag_blocks, sub_blocks, arrow_blocks, tip_block):
    partition = lax.axis_index("tm")
    parts = lax.axis_size("tm")
    order, half = diag_blocks.shape[1:]
    effects = arrow_blocks.shape[1]
    packed_rows = PACKED * BLOCK + effects * half // BLOCK
    evens = range(0, parts, 2)
    down = [(p, p - 1) for p in evens if p > 0]
    core = lax.axis_index("blk")
    info = jnp.stack([core, (partition % 2 == 0).astype(core.dtype), (partition > 0).astype(core.dtype)])
    square, tall = (order, order), (order, half)
    big = [pltpu.VMEM(square, BF16)] * 2
    thin = [pltpu.VMEM(tall, BF16)] * 2

    pivot = remote_call(
        gather_kernel, "gather_pivot", 1,
        out_shape=shape_of(*square), in_specs=[ANY_SPEC], out_specs=ANY_SPEC,
        scratch_shapes=[pltpu.SemaphoreType.DMA, dma_sems(COPIES), dma_sems(COPIES)],
    )(diag_blocks)
    sub_full = lax.all_gather(sub_blocks, "blk", axis=2, tiled=True)
    arrow_full = lax.all_gather(arrow_blocks, "blk", axis=2, tiled=True)
    inverse, log_first = inverse_and_log(pivot)

    packed_shape = shape_of(packed_rows, BLOCK)
    swap, lower, upper, x_high, x_low = local_call(
        first_products_kernel, "first_products", 10 * order**3, 44,
        grid=(1,),
        out_shape=[packed_shape] * 3 + [shape_of(*tall, dtype=BF16)] * 2,
        in_specs=[SMEM_SPEC, *vmem(3), whole((1, *tall), (1, 0, 0)), whole((1, effects, half), (1, 0, 0))],
        out_specs=vmem(5),
        scratch_shapes=big * 3 + thin,
    )(info, inverse, sub_full, arrow_full, diag_blocks, arrow_blocks)
    pairs = [(p, p + 1) for p in evens]
    other = lax.ppermute(swap, "tm", pairs + [(b, a) for a, b in pairs])
    left_own, tip_first = local_call(
        first_fill_kernel, "first_fill", 3 * order**3, 32,
        grid=(1,),
        out_shape=[shape_of(*tall), shape_of(effects, effects)],
        in_specs=[SMEM_SPEC, *vmem(1), whole((1, *square), (1, 0, 0)), whole((1, effects, order), (0, 0, 0)), *vmem(2)],
        out_specs=vmem(2),
        scratch_shapes=big,
    )(info, inverse, sub_full, arrow_full, x_high, x_low)
    lower_above = lax.ppermute(lower, "tm", down)
    left_pair = lax.ppermute(left_own, "tm", pairs)
    left_full = lax.all_gather(left_own, "blk", axis=1, tiled=True)

    both = remote_call(
        combine_kernel, "gather_separator", 2,
        out_shape=shape_of(2, packed_rows, BLOCK), in_specs=vmem(3), out_specs=ANY_SPEC,
        scratch_shapes=[
            pltpu.VMEM((packed_rows, BLOCK), F32),
            pltpu.SemaphoreType.DMA, dma_sems(COPIES), dma_sems(COPIES),
        ],
    )(other, upper, lower)
    inverse, log_second, separator = inverse_of_packed(info, both, order, half)
    product = local_call(
        second_products_kernel, "second_products", 5 * order**3, 40,
        out_shape=packed_shape,
        in_specs=[SMEM_SPEC, *vmem(5)],
        out_specs=vmem(1)[0],
        scratch_shapes=big * 2 + thin,
    )(info, inverse, left_full, both, upper, lower_above)
    above = lax.ppermute(product, "tm", down)
    left_result, sums = local_call(
        second_fill_kernel, "second_fill", 6 * order**3, 44,
        out_shape=[shape_of(1, *tall), shape_of(effects + 8, TILE)],
        in_specs=[SMEM_SPEC, *vmem(8)],
        out_specs=vmem(2),
        scratch_shapes=big * 2 + thin,
    )(info, inverse, left_full, both, left_own, left_pair, tip_first, log_first, log_second)
    sides = side_lengths(parts)
    totals = remote_call(
        functools.partial(reduce_kernel, sides), "reduce_terms", 3,
        out_shape=shape_of(effects + 8, TILE), in_specs=vmem(1), out_specs=vmem(1)[0],
        scratch_shapes=[
            pltpu.VMEM((len(sides), max(sides), effects + 8, TILE), F32),
            dma_sems(len(sides), max(sides)), dma_sems(len(sides), max(sides)),
        ],
    )(sums)
    packed, swapped = remote_call(
        finish_kernel, "finish_blocks", 4,
        out_shape=[packed_shape, shape_of(2 * BLOCK, BLOCK)], in_specs=vmem(2), out_specs=vmem(2),
        scratch_shapes=[dma_sems(2), dma_sems(2)],
    )(product, above)
    diag_result = local_call(
        place_kernel, "place_blocks", 2**20, 12,
        out_shape=shape_of(1, *tall), in_specs=[SMEM_SPEC, *vmem(3)], out_specs=vmem(1)[0],
    )(info, packed, swapped, separator)
    last = PACKED * BLOCK
    own_arrow = lax.dynamic_index_in_dim(both[:, last:], core, 0, keepdims=False)
    arrow_result = arrow_unpack(jnp.where(info[1] == 1, own_arrow, packed[last:]))
    return (
        diag_result,
        left_result,
        arrow_result[None],
        tip_block - totals[:effects, :effects],
        jnp.sum(totals[effects]),
    )


def side_lengths(parts):
    sides = []
    while parts > 1:
        side = 4 if parts % 4 == 0 else parts
        sides.append(side)
        parts //= side
    return tuple(sides)


def solution(mesh):
    in_specs = (P("tm", None, "blk"), P("tm", None, "blk"), P("tm", None, "blk"), P())
    out_specs = (P("tm", None, "blk"), P("tm", None, "blk"), P("tm", None, "blk"), P(), P())
    return jax.shard_map(
        on_device, mesh=mesh, in_specs=in_specs, out_specs=out_specs, check_vma=False
    )
```

```python
import functools

import jax
import jax.numpy as jnp
from jax import lax
from jax.experimental import pallas as pl
from jax.experimental.pallas import tpu as pltpu
from jax.sharding import PartitionSpec as P

F32 = jnp.float32
BF16 = jnp.bfloat16
TILE = 128
BLOCK = 256
PACKED = 5
COPIES = 4
GROUP = 2
SLOTS = TILE // (8 * GROUP)


def row_of(value, index):
    return jnp.broadcast_to(value[index : index + 1, :], (8, value.shape[1]))


def column_of(value, index):
    return jnp.broadcast_to(value[:, index : index + 1], (8, TILE))


def split_three(value):
    high = value.astype(BF16).astype(F32)
    rest = value - high
    middle = rest.astype(BF16).astype(F32)
    return high, middle, rest - middle


def split_two(value):
    high = value.astype(BF16)
    return high, (value - high.astype(F32)).astype(BF16)


def left_pieces(value):
    high, low = split_two(value)
    return jnp.concatenate([high, low, high], axis=1)


def right_pieces(value):
    high, low = split_two(value)
    return jnp.concatenate([high, high, low], axis=0)


def outer_product(rows_a, rows_b):
    ah, am, al = split_three(rows_a)
    bh, bm, bl = split_three(rows_b)
    left = jnp.concatenate([ah, am, ah, am, al, ah], axis=0).astype(BF16)
    right = jnp.concatenate([bh, bh, bm, bm, bh, bl], axis=0).astype(BF16)
    return lax.dot_general(left, right, (((0,), (0,)), ((), ())), preferred_element_type=F32)


def sweep_rows(rows, first, pivots, lane, sub):
    count = 8 * len(rows)
    columns = [[column_of(row, first + c) for c in range(count)] for row in rows]
    inside = (lane >= first) & (lane < first + count)
    solved = [
        jnp.where(lane == sub + first + 8 * h, -1.0, jnp.where(inside, 0.0, row)) for h, row in enumerate(rows)
    ]
    for c in range(count):
        group, place = c // 8, c % 8
        pivot = row_of(columns[group][c], place)
        scale = 1.0 / pivot
        pivots = jnp.where(lane == first + c, pivot, pivots)
        pivot_row = row_of(solved[group], place) * scale
        for h in range(len(rows)):
            value = solved[h] - columns[h][c] * pivot_row
            solved[h] = jnp.where(sub == place, pivot_row, value) if h == group else value
        for d in range(c + 1, count):
            entry = row_of(columns[group][d], place) * scale
            for h in range(len(rows)):
                value = columns[h][d] - columns[h][c] * entry
                columns[h][d] = jnp.where(sub == place, entry, value) if h == group else value
    return solved, pivots


def sweep_tile(tile, beside=None):
    lane = lax.broadcasted_iota(jnp.int32, (8, TILE), 1)
    sub = lax.broadcasted_iota(jnp.int32, (8, TILE), 0)
    pivots = jnp.ones((8, TILE), F32)
    width = 8 * GROUP
    rows = [tile[8 * i : 8 * i + 8, :] for i in range(TILE // 8)]
    for i in range(TILE // width):
        source = rows[GROUP * i : GROUP * i + GROUP]
        inside = (lane >= width * i) & (lane < width * i + width)
        solved, pivots = sweep_rows(source, width * i, pivots, lane, sub)
        update = outer_product(jnp.concatenate(source, axis=0), jnp.concatenate(solved, axis=0))
        for k in range(TILE // 8):
            if k // GROUP == i:
                continue
            kept = jnp.where(inside, 0.0, rows[k])
            if k == GROUP * (i + 1):
                for c in range(width):
                    kept = kept - column_of(rows[k], width * i + c) * row_of(solved[c // 8], c % 8)
                rows[k] = kept
            else:
                rows[k] = kept - update[8 * k : 8 * k + 8, :]
        rows[GROUP * i : GROUP * i + GROUP] = solved
        if beside is not None:
            beside(i)
    return jnp.concatenate(rows, axis=0), pivots


def tile_span(index):
    return pl.ds(pl.multiple_of(index * TILE, TILE), TILE)


def close_tile(order, matrix_ref, left_ref, swept_ref, tile_ref, j, swept):
    count = order // TILE
    here, there = tile_span(j), tile_span(lax.rem(j + 1, count))
    swept_ref[...] = swept
    solved = jnp.dot(left_pieces(swept), right_pieces(matrix_ref[here, there]), preferred_element_type=F32)
    tile_ref[...] = matrix_ref[there, there] + jnp.dot(
        left_pieces(matrix_ref[there, here]), right_pieces(solved), preferred_element_type=F32
    )
    matrix_ref[here, here] = jnp.zeros((TILE, TILE), F32)
    for r in range(count):
        span = slice(r * TILE, (r + 1) * TILE)
        left_ref[span, :] = left_pieces(matrix_ref[span, here])
    matrix_ref[:, here] = jnp.zeros((order, TILE), F32)
    matrix_ref[here, here] = swept


def solve_tile_rows(order, matrix_ref, swept_ref, right_ref, j):
    here = tile_span(j)
    rows = matrix_ref[here, :]
    lane = lax.broadcasted_iota(jnp.int32, (TILE, order), 1)
    inside = (lane >= j * TILE) & (lane < j * TILE + TILE)
    solved = -jnp.dot(left_pieces(swept_ref[...]), right_pieces(rows), preferred_element_type=F32)
    solved = jnp.where(inside, rows, solved)
    right_ref[...] = right_pieces(solved)
    matrix_ref[here, :] = solved


def update_rows(matrix_ref, left_ref, right_ref, span):
    matrix_ref[span, :] = matrix_ref[span, :] - jnp.dot(
        left_ref[span, :], right_ref[...], preferred_element_type=F32
    )


def eliminate_all(order, matrix_ref, log_ref, left_ref, right_ref, swept_ref, tile_ref):
    count = order // TILE
    swept, pivots = sweep_tile(matrix_ref[0:TILE, 0:TILE])
    close_tile(order, matrix_ref, left_ref, swept_ref, tile_ref, 0, swept)

    def step(j, logs):
        def beside(i):
            if i == 0:
                solve_tile_rows(order, matrix_ref, swept_ref, right_ref, j - 1)
                return
            first = (i - 1) * count // (SLOTS - 1)
            for r in range(first, i * count // (SLOTS - 1)):
                update_rows(matrix_ref, left_ref, right_ref, slice(r * TILE, (r + 1) * TILE))

        swept, pivots = sweep_tile(tile_ref[...], beside)
        close_tile(order, matrix_ref, left_ref, swept_ref, tile_ref, j, swept)
        return logs + jnp.log(pivots)

    log_ref[...] = lax.fori_loop(1, count, step, jnp.log(pivots))
    solve_tile_rows(order, matrix_ref, swept_ref, right_ref, count - 1)

    def update(r, carry):
        update_rows(matrix_ref, left_ref, right_ref, tile_span(r))
        return carry

    lax.fori_loop(0, count, update, 0)


def inverse_kernel(source_ref, inverse_ref, log_ref, *scratch):
    order = source_ref.shape[0]

    def take(r, carry):
        inverse_ref[tile_span(r), :] = source_ref[tile_span(r), :]
        return carry

    lax.fori_loop(0, order // TILE, take, 0)
    eliminate_all(order, inverse_ref, log_ref, *scratch)


def packed_inverse_kernel(info_ref, both_ref, inverse_ref, log_ref, own_ref, *scratch):
    order, half = own_ref.shape
    places = (((0, 0), (1, 0), (2, 0), (1, 1), (2, 1)), ((0, 3), (1, 3), (2, 3), (3, 3), (2, 2)))
    for source in range(2):
        for k, (row, column) in enumerate(places[source]):
            value = both_ref[source, k * BLOCK : (k + 1) * BLOCK, :]
            rows = slice(row * BLOCK, (row + 1) * BLOCK)
            columns = slice(column * BLOCK, (column + 1) * BLOCK)
            inverse_ref[rows, columns] = value
            if row != column:
                inverse_ref[columns, rows] = value.T
    own = pl.ds(pl.multiple_of(info_ref[0] * half, half), half)
    own_ref[...] = inverse_ref[:, own]
    eliminate_all(order, inverse_ref, log_ref, *scratch)


def inverse_scratch(order):
    return [
        pltpu.VMEM((order, 3 * TILE), BF16),
        pltpu.VMEM((3 * TILE, order), BF16),
        pltpu.VMEM((TILE, TILE), F32),
        pltpu.VMEM((TILE, TILE), F32),
    ]


def inverse_and_log(matrix):
    order = matrix.shape[0]
    return local_call(
        inverse_kernel, "first_inverse", 24 * order**3, 16,
        out_shape=[shape_of(order, order), shape_of(8, TILE)],
        in_specs=vmem(1), out_specs=vmem(2), scratch_shapes=inverse_scratch(order),
    )(matrix)


def inverse_of_packed(info, both, order, half):
    return local_call(
        packed_inverse_kernel, "second_inverse", 24 * order**3, 20,
        out_shape=[shape_of(order, order), shape_of(8, TILE), shape_of(order, half)],
        in_specs=[SMEM_SPEC, *vmem(1)], out_specs=vmem(3), scratch_shapes=inverse_scratch(order),
    )(info, both)


def times(left, right, left_dim=1, right_dim=0):
    dims = (((left_dim,), (right_dim,)), ((), ()))

    def dot(a, b):
        return lax.dot_general(a, b, dims, preferred_element_type=F32)

    return dot(left[0], right[0]) + (dot(left[0], right[1]) + dot(left[1], right[0]))


def split_rows(source, high_ref, low_ref, sign=1):
    def part(r, carry):
        high, low = split_two(sign * source[tile_span(r), :])
        high_ref[tile_span(r), :] = high
        low_ref[tile_span(r), :] = low
        return carry

    lax.fori_loop(0, high_ref.shape[0] // TILE, part, 0)


def block_span(index):
    return pl.ds(pl.multiple_of(index * BLOCK, BLOCK), BLOCK)


def packed_place(core, k):
    row = jnp.where(core == 0, jnp.where(k < 3, k, k - 2), jnp.where(k < 4, k, 2))
    column = jnp.where(core == 0, jnp.where(k < 3, 0, 1), jnp.where(k < 4, 1, 0))
    return row, column


def solve_into(inverse, right, out, right_dim):
    def part(r, carry):
        rows = block_span(r)
        value = times((inverse[0][rows, :], inverse[1][rows, :]), right, 1, right_dim)
        out[0][rows, :], out[1][rows, :] = split_two(value)
        return carry

    lax.fori_loop(0, inverse[0].shape[0] // BLOCK, part, 0)


def packed_gram(core, former, solved, left_dim, store):
    def part(k, carry):
        row, column = packed_place(core, k)
        if left_dim == 0:
            left = (former[0][:, block_span(row)], former[1][:, block_span(row)])
        else:
            left = (former[0][block_span(row), :], former[1][block_span(row), :])
        right = (solved[0][:, block_span(column)], solved[1][:, block_span(column)])
        store(k, row, column, times(left, right, left_dim, 0))
        return carry

    lax.fori_loop(0, PACKED, part, 0)


def arrow_pack(value):
    return jnp.concatenate([value[:, :BLOCK], value[:, BLOCK:]], axis=0)


def arrow_unpack(value):
    effects = value.shape[0] // 2
    return jnp.concatenate([value[:effects], value[effects:]], axis=1)


def fetch(pairs, sems):
    copies = [pltpu.make_async_copy(source, target, sems.at[k]) for k, (source, target) in enumerate(pairs)]
    for copy in copies:
        copy.start()
    return copies


def first_products_kernel(
    info_ref, arrow_ref, inverse_hbm, sub_hbm, diag_hbm, own_arrow_hbm,
    swap_ref, rest_ref, xh_ref, xl_ref,
    inverse_ref, left_ref, right_ref, diag_ref, own_arrow_ref, sems, vh, vl, bh, bl, sh, sl, yh, yl,
):
    core, even = info_ref[0], info_ref[1] == 1
    half = diag_ref.shape[1]
    own = pl.ds(pl.multiple_of(core * half, half), half)
    copies = fetch(
        (
            (inverse_hbm, inverse_ref),
            (sub_hbm.at[0], left_ref),
            (sub_hbm.at[1], right_ref),
            (diag_hbm.at[1], diag_ref),
            (own_arrow_hbm.at[1], own_arrow_ref),
        ),
        sems,
    )
    copies[0].wait()
    split_rows(inverse_ref, vh, vl, -1)
    copies[1].wait()
    split_rows(left_ref, bh, bl)
    solve_into((vh, vl), (bh[:, own], bl[:, own]), (xh_ref, xl_ref), 0)
    copies[2].wait()
    split_rows(right_ref, sh, sl)
    solve_into((vh, vl), (sh[own, :], sl[own, :]), (yh, yl), 1)
    copies[3].wait()
    copies[4].wait()

    def keep(span, lower, upper):
        swap_ref[span, :] = jnp.where(even, upper, lower)
        rest_ref[span, :] = jnp.where(even, lower, upper)

    def part(k, carry):
        row, column = packed_place(core, k)
        rows, columns = block_span(row), block_span(column)
        lower = times((bh[:, rows], bl[:, rows]), (xh_ref[:, columns], xl_ref[:, columns]), 0, 0)
        change = times((sh[rows, :], sl[rows, :]), (yh[:, columns], yl[:, columns]))
        keep(block_span(k), lower, diag_ref[rows, columns] - change)
        return carry

    lax.fori_loop(0, PACKED, part, 0)
    rows = split_two(arrow_ref[0])
    keep(
        slice(PACKED * BLOCK, None),
        arrow_pack(times(rows, (xh_ref[...], xl_ref[...]))),
        arrow_pack(own_arrow_ref[...] - times(rows, (yh[...], yl[...]))),
    )


def arrow_form(rows, inverse_ref):
    pieces = split_two(rows)
    through = -times(pieces, split_two(inverse_ref[...]))
    return times(split_two(through), pieces, 1, 1)


def separator_arrow(packed):
    return jnp.concatenate([arrow_unpack(packed[0]), arrow_unpack(packed[1])], axis=1)


def second_products_kernel(
    info_ref, inverse_hbm, left_hbm, both_hbm, rest_hbm, above_hbm, out_ref,
    inverse_ref, left_ref, arrow_ref, rest_ref, above_ref, sems, vh, vl, bh, bl, xh, xl,
):
    core, even = info_ref[0], info_ref[1] == 1
    half = xh.shape[1]
    own = pl.ds(pl.multiple_of(core * half, half), half)
    last = slice(PACKED * BLOCK, None)
    copies = fetch(
        (
            (inverse_hbm, inverse_ref),
            (left_hbm, left_ref),
            (both_hbm.at[:, pl.ds(PACKED * BLOCK, arrow_ref.shape[1]), :], arrow_ref),
            (rest_hbm, rest_ref),
            (above_hbm, above_ref),
        ),
        sems,
    )
    copies[0].wait()
    split_rows(inverse_ref, vh, vl, -1)
    copies[1].wait()
    split_rows(left_ref, bh, bl)
    for copy in copies[2:]:
        copy.wait()
    rows = split_two(separator_arrow(arrow_ref[...]))

    @pl.when(even)
    def _():
        solve_into((vh, vl), (bh[:, own], bl[:, own]), (xh, xl), 0)

        def store(k, row, column, value):
            out_ref[block_span(k), :] = value

        packed_gram(core, (bh, bl), (xh, xl), 0, store)
        out_ref[last, :] = arrow_pack(times(rows, (xh[...], xl[...])))

    @pl.when(jnp.logical_not(even))
    def _():
        solve_into((vh, vl), (bh[own, :], bl[own, :]), (xh, xl), 1)

        def store(k, row, column, value):
            span = block_span(k)
            out_ref[span, :] = rest_ref[span, :] - above_ref[span, :] - value

        packed_gram(core, (bh, bl), (xh, xl), 1, store)
        change = arrow_pack(times(rows, (xh[...], xl[...])))
        out_ref[last, :] = rest_ref[last, :] - above_ref[last, :] - change


def second_fill_kernel(
    info_ref, inverse_ref, left_ref, sep_ref, own_ref, pair_ref, tip_ref, log_ref, log_two_ref,
    out_ref, sums_ref, vh, vl, bh, bl, xh, xl,
):
    even = info_ref[1] == 1
    effects = tip_ref.shape[0]
    sums_ref[...] = jnp.zeros_like(sums_ref)

    @pl.when(even)
    def _():
        out_ref[0] = own_ref[...]
        tip = tip_ref[...] + arrow_form(separator_arrow(sep_ref[:, PACKED * BLOCK :, :]), inverse_ref)
        sums_ref[0:effects, 0:effects] = tip
        sums_ref[effects:, :] = log_ref[...] + log_two_ref[...]

    @pl.when(jnp.logical_not(even))
    def _():
        sums_ref[0:effects, 0:effects] = tip_ref[...]
        sums_ref[effects:, :] = log_ref[...]
        split_rows(inverse_ref, vh, vl, -1)
        split_rows(left_ref, bh, bl)
        solve_into((vh, vl), split_two(pair_ref[...]), (xh, xl), 0)

        def part(r, carry):
            rows = block_span(r)
            out_ref[0, rows, :] = -times((bh[rows, :], bl[rows, :]), (xh[...], xl[...]))
            return carry

        lax.fori_loop(0, bh.shape[0] // BLOCK, part, 0)


def meet(devices):
    barrier = pltpu.get_barrier_semaphore()
    for device in devices:
        pl.semaphore_signal(barrier, inc=1, device_id=device, device_id_type=pl.DeviceIdType.MESH)
    pl.semaphore_wait(barrier, len(devices))


def exchange(parts, peer, send_sem, recv_sem):
    copies = []
    for k, (source, target) in enumerate(parts):
        copies.append(
            pltpu.make_async_remote_copy(
                src_ref=source,
                dst_ref=target,
                send_sem=send_sem.at[k],
                recv_sem=recv_sem.at[k],
                device_id=peer,
                device_id_type=pl.DeviceIdType.MESH,
            )
        )
        copies[-1].start()
    return copies


def gather_kernel(diag_ref, arrow_ref, out_ref, arrow_out_ref, local_sems, send_sem, recv_sem):
    core = lax.axis_index("blk")
    peer = {"blk": 1 - core}
    half = diag_ref.shape[2]
    rows = diag_ref.shape[1] // COPIES
    own = pl.ds(pl.multiple_of(core * half, half), half)
    local = pltpu.make_async_copy(diag_ref.at[0], out_ref.at[:, own], local_sems.at[0])
    local.start()
    local_arrow = pltpu.make_async_copy(arrow_ref.at[0], arrow_out_ref.at[0, :, own], local_sems.at[1])
    local_arrow.start()
    meet([peer])
    spans = [pl.ds(k * rows, rows) for k in range(COPIES)]
    parts = [(diag_ref.at[0, span, :], out_ref.at[span, own]) for span in spans]
    parts.append((arrow_ref.at[0], arrow_out_ref.at[0, :, own]))
    copies = exchange(parts, peer, send_sem, recv_sem)
    local.wait()
    local_arrow.wait()
    for copy in copies:
        copy.wait()


def pair_kernel(
    swap_hbm, inverse_hbm, sub_hbm, arrow_hbm, xh_hbm, xl_hbm, both_hbm, left_ref, tip_ref,
    own_ref, other_ref, sum_ref, inverse_ref, right_ref, arrow_ref, xh, xl, sh, sl,
    sems, local_sems, swap_send, swap_recv, send_sem, recv_sem,
):
    core, me = lax.axis_index("blk"), lax.axis_index("tm")
    even = me % 2 == 0
    peer, partner = {"blk": 1 - core}, {"tm": me + 1 - 2 * (me % 2)}
    meet([peer, partner])
    rows = sum_ref.shape[0] // COPIES
    spans = [pl.ds(k * rows, rows) for k in range(COPIES)]
    swaps = exchange(
        [(swap_hbm.at[span, :], other_ref.at[span, :]) for span in spans], partner, swap_send, swap_recv
    )
    copies = fetch(
        (
            (sub_hbm.at[1], right_ref),
            (xh_hbm, xh),
            (xl_hbm, xl),
            (inverse_hbm, inverse_ref),
            (arrow_hbm.at[0], arrow_ref),
            (swap_hbm, own_ref),
        ),
        sems,
    )
    for copy in copies:
        copy.wait()
    split_rows(right_ref, sh, sl)

    def part(r, carry):
        span = block_span(r)
        value = -times((sh[span, :], sl[span, :]), (xh[...], xl[...]))
        left_ref[span, :] = jnp.where(me > 0, value, 0.0)
        return carry

    lax.fori_loop(0, sh.shape[0] // BLOCK, part, 0)
    tip_ref[...] = arrow_form(arrow_ref[...], inverse_ref)
    shares = []
    for k, span in enumerate(spans):
        swaps[k].wait()
        difference = own_ref[span, :] - other_ref[span, :]
        sum_ref[span, :] = jnp.where(even, difference, -difference)
        local = pltpu.make_async_copy(sum_ref.at[span, :], both_hbm.at[core, span, :], local_sems.at[k])
        local.start()
        shares.append(local)
        shares += exchange(
            [(sum_ref.at[span, :], both_hbm.at[core, span, :])], peer, send_sem.at[pl.ds(k, 1)], recv_sem.at[pl.ds(k, 1)]
        )
    for copy in shares:
        copy.wait()


def finish_kernel(kept_ref, above_ref, out_ref, peer_ref, send_sem, recv_sem):
    core = lax.axis_index("blk")
    peer = {"blk": 1 - core}
    out_ref[...] = kept_ref[...] - above_ref[...]
    meet([peer])
    copies = []
    for slot, block in enumerate((2 - 2 * core, 4 - 3 * core)):
        copies.append(
            pltpu.make_async_remote_copy(
                src_ref=out_ref.at[block_span(block), :],
                dst_ref=peer_ref.at[pl.ds(slot * BLOCK, BLOCK), :],
                send_sem=send_sem.at[slot],
                recv_sem=recv_sem.at[slot],
                device_id=peer,
                device_id_type=pl.DeviceIdType.MESH,
            )
        )
        copies[-1].start()
    for copy in copies:
        copy.wait()


def place_kernel(info_ref, packed_ref, peer_ref, separator_ref, out_ref):
    core, even = info_ref[0], info_ref[1] == 1

    @pl.when(even)
    def _():
        out_ref[0] = separator_ref[...]

    def packed(k):
        return packed_ref[k * BLOCK : (k + 1) * BLOCK, :]

    def put(row, column, value):
        out_ref[0, row * BLOCK : (row + 1) * BLOCK, column * BLOCK : (column + 1) * BLOCK] = value

    first, second = peer_ref[:BLOCK, :], peer_ref[BLOCK:, :]
    odd = jnp.logical_not(even)

    @pl.when(odd & (core == 0))
    def _():
        for row, column, value in (
            (0, 0, packed(0)), (1, 0, packed(1)), (2, 0, packed(2)), (3, 0, first.T),
            (0, 1, packed(1).T), (1, 1, packed(3)), (2, 1, packed(4)), (3, 1, second.T),
        ):
            put(row, column, value)

    @pl.when(odd & (core == 1))
    def _():
        for row, column, value in (
            (0, 0, first.T), (1, 0, second.T), (2, 0, packed(4)), (3, 0, packed(2).T),
            (0, 1, packed(0)), (1, 1, packed(1)), (2, 1, packed(2)), (3, 1, packed(3)),
        ):
            put(row, column, value)


def reduce_kernel(sides, value_ref, out_ref, parts_ref, send_sem, recv_sem):
    me = lax.axis_index("tm")
    stages = []
    stride = 1
    for side in reversed(sides):
        place = (me // stride) % side
        stages.append((side, place, stride))
        stride = stride * side

    def other(stage, step):
        side, place, stride = stages[stage]
        return me + ((place + step) % side - place) * stride

    meet([{"tm": other(s, d)} for s in range(len(stages)) for d in range(1, stages[s][0])])
    out_ref[...] = value_ref[...]
    for s in reversed(range(len(stages))):
        side, place, _ = stages[s]
        parts_ref[s, place] = out_ref[...]
        copies = []
        for d in range(1, side):
            copies.append(
                pltpu.make_async_remote_copy(
                    src_ref=out_ref,
                    dst_ref=parts_ref.at[s, place],
                    send_sem=send_sem.at[s, d],
                    recv_sem=recv_sem.at[s, d],
                    device_id={"tm": other(s, d)},
                    device_id_type=pl.DeviceIdType.MESH,
                )
            )
            copies[-1].start()
        for copy in copies:
            copy.wait()
        total = parts_ref[s, 0]
        for k in range(1, side):
            total = total + parts_ref[s, k]
        out_ref[...] = total


def vmem(count):
    return [pl.BlockSpec(memory_space=pltpu.VMEM)] * count


def shape_of(*sizes, dtype=F32):
    return jax.ShapeDtypeStruct(sizes, dtype)


SMEM_SPEC = pl.BlockSpec(memory_space=pltpu.SMEM)
ANY_SPEC = pl.BlockSpec(memory_space=pl.ANY)
HBM_SPEC = pl.BlockSpec(memory_space=pltpu.HBM)


def local_call(kernel, name, flops, mebibytes, **kwargs):
    return pl.pallas_call(
        kernel,
        compiler_params=pltpu.CompilerParams(vmem_limit_bytes=mebibytes * 2**20),
        cost_estimate=pl.CostEstimate(flops=flops, bytes_accessed=2**23, transcendentals=0),
        name=name,
        **kwargs,
    )


def remote_call(kernel, name, identity, mebibytes=24, **kwargs):
    return pl.pallas_call(
        kernel,
        compiler_params=pltpu.CompilerParams(
            collective_id=identity, has_side_effects=True, vmem_limit_bytes=mebibytes * 2**20
        ),
        name=name,
        **kwargs,
    )


def dma_sems(*shape):
    return pltpu.SemaphoreType.DMA(shape)


def whole(shape, index):
    return pl.BlockSpec(shape, lambda i: index, pipeline_mode=pl.Buffered(1))


def on_device(diag_blocks, sub_blocks, arrow_blocks, tip_block):
    partition = lax.axis_index("tm")
    parts = lax.axis_size("tm")
    order, half = diag_blocks.shape[1:]
    effects = arrow_blocks.shape[1]
    packed_rows = PACKED * BLOCK + effects * half // BLOCK
    evens = range(0, parts, 2)
    down = [(p, p - 1) for p in evens if p > 0]
    core = lax.axis_index("blk")
    info = jnp.stack([core, (partition % 2 == 0).astype(core.dtype), (partition > 0).astype(core.dtype)])
    square, tall = (order, order), (order, half)
    big = [pltpu.VMEM(square, BF16)] * 2
    thin = [pltpu.VMEM(tall, BF16)] * 2

    pivot, arrow_full = remote_call(
        gather_kernel, "gather_pivot", 1, 58,
        out_shape=[shape_of(*square), shape_of(1, effects, order)],
        in_specs=[HBM_SPEC] * 2, out_specs=[ANY_SPEC] * 2,
        scratch_shapes=[dma_sems(2), dma_sems(COPIES + 1), dma_sems(COPIES + 1)],
    )(diag_blocks, arrow_blocks)
    sub_full = lax.all_gather(sub_blocks, "blk", axis=2, tiled=True)
    inverse, log_first = inverse_and_log(pivot)

    packed_shape = shape_of(packed_rows, BLOCK)
    packed_scratch = pltpu.VMEM((packed_rows, BLOCK), F32)
    swap, rest, x_high, x_low = local_call(
        first_products_kernel, "first_products", 10 * order**3, 58,
        out_shape=[packed_shape] * 2 + [shape_of(*tall, dtype=BF16)] * 2,
        in_specs=[SMEM_SPEC, *vmem(1), *[ANY_SPEC] * 4],
        out_specs=vmem(4),
        scratch_shapes=[pltpu.VMEM(square, F32)] * 3
        + [pltpu.VMEM(tall, F32), pltpu.VMEM((effects, half), F32), dma_sems(5)]
        + big * 3
        + thin,
    )(info, arrow_full, inverse, sub_full, diag_blocks, arrow_blocks)
    pairs = [(p, p + 1) for p in evens]
    both, left_own, tip_first = remote_call(
        pair_kernel, "swap_and_fill", 2, 58,
        out_shape=[shape_of(2, packed_rows, BLOCK), shape_of(*tall), shape_of(effects, effects)],
        in_specs=[ANY_SPEC] * 6,
        out_specs=[ANY_SPEC, *vmem(2)],
        scratch_shapes=[packed_scratch] * 3
        + [pltpu.VMEM(square, F32)] * 2
        + [pltpu.VMEM((effects, order), F32)]
        + thin
        + big
        + [dma_sems(6), dma_sems(COPIES), dma_sems(COPIES), dma_sems(COPIES), dma_sems(COPIES), dma_sems(COPIES)],
    )(swap, inverse, sub_full, arrow_full, x_high, x_low)
    lower_above = lax.ppermute(rest, "tm", down)
    left_pair = lax.ppermute(left_own, "tm", pairs)
    left_full = lax.all_gather(left_own, "blk", axis=1, tiled=True)

    inverse, log_second, separator = inverse_of_packed(info, both, order, half)
    product = local_call(
        second_products_kernel, "second_products", 5 * order**3, 58,
        out_shape=packed_shape,
        in_specs=[SMEM_SPEC, *[ANY_SPEC] * 5],
        out_specs=vmem(1)[0],
        scratch_shapes=[pltpu.VMEM(square, F32)] * 2
        + [pltpu.VMEM((2, packed_rows - PACKED * BLOCK, BLOCK), F32), packed_scratch, packed_scratch, dma_sems(5)]
        + big * 2
        + thin,
    )(info, inverse, left_full, both, rest, lower_above)
    above = lax.ppermute(product, "tm", down)
    left_result, sums = local_call(
        second_fill_kernel, "second_fill", 6 * order**3, 58,
        out_shape=[shape_of(1, *tall), shape_of(effects + 8, TILE)],
        in_specs=[SMEM_SPEC, *vmem(8)],
        out_specs=vmem(2),
        scratch_shapes=big * 2 + thin,
    )(info, inverse, left_full, both, left_own, left_pair, tip_first, log_first, log_second)
    sides = side_lengths(parts)
    totals = remote_call(
        functools.partial(reduce_kernel, sides), "reduce_terms", 3,
        out_shape=shape_of(effects + 8, TILE), in_specs=vmem(1), out_specs=vmem(1)[0],
        scratch_shapes=[
            pltpu.VMEM((len(sides), max(sides), effects + 8, TILE), F32),
            dma_sems(len(sides), max(sides)), dma_sems(len(sides), max(sides)),
        ],
    )(sums)
    packed, swapped = remote_call(
        finish_kernel, "finish_blocks", 4,
        out_shape=[packed_shape, shape_of(2 * BLOCK, BLOCK)], in_specs=vmem(2), out_specs=vmem(2),
        scratch_shapes=[dma_sems(2), dma_sems(2)],
    )(product, above)
    diag_result = local_call(
        place_kernel, "place_blocks", 2**20, 12,
        out_shape=shape_of(1, *tall), in_specs=[SMEM_SPEC, *vmem(3)], out_specs=vmem(1)[0],
    )(info, packed, swapped, separator)
    last = PACKED * BLOCK
    own_arrow = lax.dynamic_index_in_dim(both[:, last:], core, 0, keepdims=False)
    arrow_result = arrow_unpack(jnp.where(info[1] == 1, own_arrow, packed[last:]))
    return (
        diag_result,
        left_result,
        arrow_result[None],
        tip_block - totals[:effects, :effects],
        jnp.sum(totals[effects]),
    )


def side_lengths(parts):
    sides = []
    while parts > 1:
        side = 4 if parts % 4 == 0 else parts
        sides.append(side)
        parts //= side
    return tuple(sides)


def solution(mesh):
    in_specs = (P("tm", None, "blk"), P("tm", None, "blk"), P("tm", None, "blk"), P())
    out_specs = (P("tm", None, "blk"), P("tm", None, "blk"), P("tm", None, "blk"), P(), P())
    return jax.shard_map(
        on_device, mesh=mesh, in_specs=in_specs, out_specs=out_specs, check_vma=False
    )
```

```python
import functools

import jax
import jax.numpy as jnp
from jax import lax
from jax.experimental import pallas as pl
from jax.experimental.pallas import tpu as pltpu
from jax.sharding import PartitionSpec as P

F32 = jnp.float32
BF16 = jnp.bfloat16
TILE = 128
BLOCK = 256
PACKED = 5
COPIES = 4
SIDE = 4
GROUP = 2
SLOTS = TILE // (8 * GROUP)


def row_of(value, index):
    return jnp.broadcast_to(value[index : index + 1, :], (8, value.shape[1]))


def column_of(value, index):
    return jnp.broadcast_to(value[:, index : index + 1], (8, TILE))


def split_three(value):
    high = value.astype(BF16).astype(F32)
    rest = value - high
    middle = rest.astype(BF16).astype(F32)
    return high, middle, rest - middle


def split_two(value):
    high = value.astype(BF16)
    return high, (value - high.astype(F32)).astype(BF16)


def left_pieces(value):
    high, low = split_two(value)
    return jnp.concatenate([high, low, high], axis=1)


def right_pieces(value):
    high, low = split_two(value)
    return jnp.concatenate([high, high, low], axis=0)


def outer_product(rows_a, rows_b):
    ah, am, al = split_three(rows_a)
    bh, bm, bl = split_three(rows_b)
    left = jnp.concatenate([ah, am, ah, am, al, ah], axis=0).astype(BF16)
    right = jnp.concatenate([bh, bh, bm, bm, bh, bl], axis=0).astype(BF16)
    return lax.dot_general(left, right, (((0,), (0,)), ((), ())), preferred_element_type=F32)


def sweep_rows(rows, first, pivots, lane, sub):
    count = 8 * len(rows)
    columns = [[column_of(row, first + c) for c in range(count)] for row in rows]
    inside = (lane >= first) & (lane < first + count)
    solved = [
        jnp.where(lane == sub + first + 8 * h, -1.0, jnp.where(inside, 0.0, row)) for h, row in enumerate(rows)
    ]
    for c in range(count):
        group, place = c // 8, c % 8
        pivot = row_of(columns[group][c], place)
        scale = 1.0 / pivot
        pivots = jnp.where(lane == first + c, pivot, pivots)
        pivot_row = row_of(solved[group], place) * scale
        for h in range(len(rows)):
            value = solved[h] - columns[h][c] * pivot_row
            solved[h] = jnp.where(sub == place, pivot_row, value) if h == group else value
        for d in range(c + 1, count):
            entry = row_of(columns[group][d], place) * scale
            for h in range(len(rows)):
                value = columns[h][d] - columns[h][c] * entry
                columns[h][d] = jnp.where(sub == place, entry, value) if h == group else value
    return solved, pivots


def sweep_tile(tile, beside=None):
    lane = lax.broadcasted_iota(jnp.int32, (8, TILE), 1)
    sub = lax.broadcasted_iota(jnp.int32, (8, TILE), 0)
    pivots = jnp.ones((8, TILE), F32)
    width = 8 * GROUP
    rows = [tile[8 * i : 8 * i + 8, :] for i in range(TILE // 8)]
    for i in range(TILE // width):
        source = rows[GROUP * i : GROUP * i + GROUP]
        inside = (lane >= width * i) & (lane < width * i + width)
        solved, pivots = sweep_rows(source, width * i, pivots, lane, sub)
        update = outer_product(jnp.concatenate(source, axis=0), jnp.concatenate(solved, axis=0))
        for k in range(TILE // 8):
            if k // GROUP == i:
                continue
            kept = jnp.where(inside, 0.0, rows[k])
            if k == GROUP * (i + 1):
                for c in range(width):
                    kept = kept - column_of(rows[k], width * i + c) * row_of(solved[c // 8], c % 8)
                rows[k] = kept
            else:
                rows[k] = kept - update[8 * k : 8 * k + 8, :]
        rows[GROUP * i : GROUP * i + GROUP] = solved
        if beside is not None:
            beside(i)
    return jnp.concatenate(rows, axis=0), pivots


def tile_span(index):
    return pl.ds(pl.multiple_of(index * TILE, TILE), TILE)


def close_tile(order, matrix_ref, left_ref, swept_ref, tile_ref, j, swept):
    count = order // TILE
    here, there = tile_span(j), tile_span(lax.rem(j + 1, count))
    swept_ref[...] = swept
    solved = jnp.dot(left_pieces(swept), right_pieces(matrix_ref[here, there]), preferred_element_type=F32)
    tile_ref[...] = matrix_ref[there, there] + jnp.dot(
        left_pieces(matrix_ref[there, here]), right_pieces(solved), preferred_element_type=F32
    )
    matrix_ref[here, here] = jnp.zeros((TILE, TILE), F32)
    for r in range(count):
        span = slice(r * TILE, (r + 1) * TILE)
        left_ref[span, :] = left_pieces(matrix_ref[span, here])
    matrix_ref[:, here] = jnp.zeros((order, TILE), F32)
    matrix_ref[here, here] = swept


def solve_tile_rows(order, matrix_ref, swept_ref, right_ref, j):
    here = tile_span(j)
    rows = matrix_ref[here, :]
    lane = lax.broadcasted_iota(jnp.int32, (TILE, order), 1)
    inside = (lane >= j * TILE) & (lane < j * TILE + TILE)
    solved = -jnp.dot(left_pieces(swept_ref[...]), right_pieces(rows), preferred_element_type=F32)
    solved = jnp.where(inside, rows, solved)
    right_ref[...] = right_pieces(solved)
    matrix_ref[here, :] = solved


def update_rows(matrix_ref, left_ref, right_ref, span):
    matrix_ref[span, :] = matrix_ref[span, :] - jnp.dot(
        left_ref[span, :], right_ref[...], preferred_element_type=F32
    )


def eliminate_all(order, matrix_ref, log_ref, left_ref, right_ref, swept_ref, tile_ref):
    count = order // TILE
    swept, pivots = sweep_tile(matrix_ref[0:TILE, 0:TILE])
    close_tile(order, matrix_ref, left_ref, swept_ref, tile_ref, 0, swept)

    def step(j, logs):
        def beside(i):
            if i == 0:
                solve_tile_rows(order, matrix_ref, swept_ref, right_ref, j - 1)
                return
            first = (i - 1) * count // (SLOTS - 1)
            for r in range(first, i * count // (SLOTS - 1)):
                update_rows(matrix_ref, left_ref, right_ref, slice(r * TILE, (r + 1) * TILE))

        swept, pivots = sweep_tile(tile_ref[...], beside)
        close_tile(order, matrix_ref, left_ref, swept_ref, tile_ref, j, swept)
        return logs + jnp.log(pivots)

    log_ref[...] = lax.fori_loop(1, count, step, jnp.log(pivots))
    solve_tile_rows(order, matrix_ref, swept_ref, right_ref, count - 1)

    def update(r, carry):
        update_rows(matrix_ref, left_ref, right_ref, tile_span(r))
        return carry

    lax.fori_loop(0, count, update, 0)


def inverse_kernel(source_ref, inverse_ref, log_ref, *scratch):
    order = source_ref.shape[0]

    def take(r, carry):
        inverse_ref[tile_span(r), :] = source_ref[tile_span(r), :]
        return carry

    lax.fori_loop(0, order // TILE, take, 0)
    eliminate_all(order, inverse_ref, log_ref, *scratch)


def packed_inverse_kernel(info_ref, both_ref, inverse_ref, log_ref, own_ref, *scratch):
    order, half = own_ref.shape
    places = (((0, 0), (1, 0), (2, 0), (1, 1), (2, 1)), ((0, 3), (1, 3), (2, 3), (3, 3), (2, 2)))
    for source in range(2):
        for k, (row, column) in enumerate(places[source]):
            value = both_ref[source, k * BLOCK : (k + 1) * BLOCK, :]
            rows = slice(row * BLOCK, (row + 1) * BLOCK)
            columns = slice(column * BLOCK, (column + 1) * BLOCK)
            inverse_ref[rows, columns] = value
            if row != column:
                inverse_ref[columns, rows] = value.T
    own = pl.ds(pl.multiple_of(info_ref[0] * half, half), half)
    own_ref[...] = inverse_ref[:, own]
    eliminate_all(order, inverse_ref, log_ref, *scratch)


def inverse_scratch(order):
    return [
        pltpu.VMEM((order, 3 * TILE), BF16),
        pltpu.VMEM((3 * TILE, order), BF16),
        pltpu.VMEM((TILE, TILE), F32),
        pltpu.VMEM((TILE, TILE), F32),
    ]


def inverse_and_log(matrix):
    order = matrix.shape[0]
    return local_call(
        inverse_kernel, "first_inverse", 24 * order**3, 16,
        out_shape=[shape_of(order, order), shape_of(8, TILE)],
        in_specs=vmem(1), out_specs=vmem(2), scratch_shapes=inverse_scratch(order),
    )(matrix)


def inverse_of_packed(info, both, order, half):
    return local_call(
        packed_inverse_kernel, "second_inverse", 24 * order**3, 20,
        out_shape=[shape_of(order, order), shape_of(8, TILE), shape_of(order, half)],
        in_specs=[SMEM_SPEC, *vmem(1)], out_specs=vmem(3), scratch_shapes=inverse_scratch(order),
    )(info, both)


def times(left, right, left_dim=1, right_dim=0):
    dims = (((left_dim,), (right_dim,)), ((), ()))

    def dot(a, b):
        return lax.dot_general(a, b, dims, preferred_element_type=F32)

    return dot(left[0], right[0]) + (dot(left[0], right[1]) + dot(left[1], right[0]))


def split_rows(source, high_ref, low_ref, sign=1):
    def part(r, carry):
        high, low = split_two(sign * source[tile_span(r), :])
        high_ref[tile_span(r), :] = high
        low_ref[tile_span(r), :] = low
        return carry

    lax.fori_loop(0, high_ref.shape[0] // TILE, part, 0)


def block_span(index):
    return pl.ds(pl.multiple_of(index * BLOCK, BLOCK), BLOCK)


def packed_place(core, k):
    row = jnp.where(core == 0, jnp.where(k < 3, k, k - 2), jnp.where(k < 4, k, 2))
    column = jnp.where(core == 0, jnp.where(k < 3, 0, 1), jnp.where(k < 4, 1, 0))
    return row, column


def solve_into(inverse, right, out, right_dim):
    def part(r, carry):
        rows = block_span(r)
        value = times((inverse[0][rows, :], inverse[1][rows, :]), right, 1, right_dim)
        out[0][rows, :], out[1][rows, :] = split_two(value)
        return carry

    lax.fori_loop(0, inverse[0].shape[0] // BLOCK, part, 0)


def packed_gram(core, former, solved, left_dim, store):
    def part(k, carry):
        row, column = packed_place(core, k)
        if left_dim == 0:
            left = (former[0][:, block_span(row)], former[1][:, block_span(row)])
        else:
            left = (former[0][block_span(row), :], former[1][block_span(row), :])
        right = (solved[0][:, block_span(column)], solved[1][:, block_span(column)])
        store(k, row, column, times(left, right, left_dim, 0))
        return carry

    lax.fori_loop(0, PACKED, part, 0)


def arrow_pack(value):
    return jnp.concatenate([value[:, :BLOCK], value[:, BLOCK:]], axis=0)


def arrow_unpack(value):
    effects = value.shape[0] // 2
    return jnp.concatenate([value[:effects], value[effects:]], axis=1)


def fetch(pairs, sems):
    copies = [pltpu.make_async_copy(source, target, sems.at[k]) for k, (source, target) in enumerate(pairs)]
    for copy in copies:
        copy.start()
    return copies


def first_products_kernel(
    info_ref, arrow_ref, inverse_hbm, sub_hbm, diag_hbm, own_arrow_hbm,
    swap_ref, rest_ref, xh_ref, xl_ref,
    inverse_ref, left_ref, right_ref, diag_ref, own_arrow_ref, sems, vh, vl, bh, bl, sh, sl, yh, yl,
):
    core, even = info_ref[0], info_ref[1] == 1
    half = diag_ref.shape[1]
    own = pl.ds(pl.multiple_of(core * half, half), half)
    copies = fetch(
        (
            (inverse_hbm, inverse_ref),
            (sub_hbm.at[0], left_ref),
            (sub_hbm.at[1], right_ref),
            (diag_hbm.at[1], diag_ref),
            (own_arrow_hbm.at[1], own_arrow_ref),
        ),
        sems,
    )
    copies[0].wait()
    split_rows(inverse_ref, vh, vl, -1)
    copies[1].wait()
    split_rows(left_ref, bh, bl)
    solve_into((vh, vl), (bh[:, own], bl[:, own]), (xh_ref, xl_ref), 0)
    copies[2].wait()
    split_rows(right_ref, sh, sl)
    solve_into((vh, vl), (sh[own, :], sl[own, :]), (yh, yl), 1)
    copies[3].wait()
    copies[4].wait()

    def keep(span, lower, upper):
        swap_ref[span, :] = jnp.where(even, upper, lower)
        rest_ref[span, :] = jnp.where(even, lower, upper)

    def part(k, carry):
        row, column = packed_place(core, k)
        rows, columns = block_span(row), block_span(column)
        lower = times((bh[:, rows], bl[:, rows]), (xh_ref[:, columns], xl_ref[:, columns]), 0, 0)
        change = times((sh[rows, :], sl[rows, :]), (yh[:, columns], yl[:, columns]))
        keep(block_span(k), lower, diag_ref[rows, columns] - change)
        return carry

    lax.fori_loop(0, PACKED, part, 0)
    rows = split_two(arrow_ref[0])
    keep(
        slice(PACKED * BLOCK, None),
        arrow_pack(times(rows, (xh_ref[...], xl_ref[...]))),
        arrow_pack(own_arrow_ref[...] - times(rows, (yh[...], yl[...]))),
    )


def arrow_form(rows, inverse_ref):
    pieces = split_two(rows)
    through = -times(pieces, split_two(inverse_ref[...]))
    return times(split_two(through), pieces, 1, 1)


def separator_arrow(packed):
    return jnp.concatenate([arrow_unpack(packed[0]), arrow_unpack(packed[1])], axis=1)


def second_products_kernel(
    info_ref, inverse_hbm, left_hbm, both_hbm, rest_hbm, out_ref,
    inverse_ref, left_ref, arrow_ref, rest_ref, sems, vh, vl, bh, bl, xh, xl,
):
    core, even = info_ref[0], info_ref[1] == 1
    half = xh.shape[1]
    own = pl.ds(pl.multiple_of(core * half, half), half)
    last = slice(PACKED * BLOCK, None)
    copies = fetch(
        (
            (inverse_hbm, inverse_ref),
            (left_hbm, left_ref),
            (both_hbm.at[:, pl.ds(PACKED * BLOCK, arrow_ref.shape[1]), :], arrow_ref),
            (rest_hbm, rest_ref),
        ),
        sems,
    )
    copies[0].wait()
    split_rows(inverse_ref, vh, vl, -1)
    copies[1].wait()
    split_rows(left_ref, bh, bl)
    for copy in copies[2:]:
        copy.wait()
    rows = split_two(separator_arrow(arrow_ref[...]))

    @pl.when(even)
    def _():
        solve_into((vh, vl), (bh[:, own], bl[:, own]), (xh, xl), 0)

        def store(k, row, column, value):
            out_ref[block_span(k), :] = rest_ref[block_span(k), :] + value

        packed_gram(core, (bh, bl), (xh, xl), 0, store)
        out_ref[last, :] = rest_ref[last, :] + arrow_pack(times(rows, (xh[...], xl[...])))

    @pl.when(jnp.logical_not(even))
    def _():
        solve_into((vh, vl), (bh[own, :], bl[own, :]), (xh, xl), 1)

        def store(k, row, column, value):
            span = block_span(k)
            out_ref[span, :] = rest_ref[span, :] - value

        packed_gram(core, (bh, bl), (xh, xl), 1, store)
        change = arrow_pack(times(rows, (xh[...], xl[...])))
        out_ref[last, :] = rest_ref[last, :] - change


def second_fill_kernel(
    info_ref, inverse_ref, left_ref, sep_ref, own_ref, pair_ref, pair_sums_ref, log_ref,
    out_ref, sums_ref, vh, vl, bh, bl, xh, xl,
):
    even = info_ref[1] == 1

    @pl.when(even)
    def _():
        out_ref[0] = own_ref[...]
        sums_ref[...] = pair_sums_ref[...]

    @pl.when(jnp.logical_not(even))
    def _():
        put_sums(sums_ref, arrow_form(separator_arrow(sep_ref[:, PACKED * BLOCK :, :]), inverse_ref), log_ref[...])
        sums_ref[...] = sums_ref[...] + pair_sums_ref[...]
        split_rows(inverse_ref, vh, vl, -1)
        split_rows(left_ref, bh, bl)
        solve_into((vh, vl), split_two(pair_ref[...]), (xh, xl), 0)

        def part(r, carry):
            rows = block_span(r)
            out_ref[0, rows, :] = -times((bh[rows, :], bl[rows, :]), (xh[...], xl[...]))
            return carry

        lax.fori_loop(0, bh.shape[0] // BLOCK, part, 0)


def meet(devices):
    barrier = pltpu.get_barrier_semaphore()
    for device in devices:
        pl.semaphore_signal(barrier, inc=1, device_id=device, device_id_type=pl.DeviceIdType.MESH)
    pl.semaphore_wait(barrier, len(devices))


def exchange(parts, peer, send_sem, recv_sem):
    copies = []
    for k, (source, target) in enumerate(parts):
        copies.append(
            pltpu.make_async_remote_copy(
                src_ref=source,
                dst_ref=target,
                send_sem=send_sem.at[k],
                recv_sem=recv_sem.at[k],
                device_id=peer,
                device_id_type=pl.DeviceIdType.MESH,
            )
        )
        copies[-1].start()
    return copies


def gather_kernel(diag_ref, arrow_ref, out_ref, arrow_out_ref, local_sems, send_sem, recv_sem):
    core = lax.axis_index("blk")
    peer = {"blk": 1 - core}
    half = diag_ref.shape[2]
    rows = diag_ref.shape[1] // COPIES
    own = pl.ds(pl.multiple_of(core * half, half), half)
    local = pltpu.make_async_copy(diag_ref.at[0], out_ref.at[:, own], local_sems.at[0])
    local.start()
    local_arrow = pltpu.make_async_copy(arrow_ref.at[0], arrow_out_ref.at[0, :, own], local_sems.at[1])
    local_arrow.start()
    meet([peer])
    spans = [pl.ds(k * rows, rows) for k in range(COPIES)]
    parts = [(diag_ref.at[0, span, :], out_ref.at[span, own]) for span in spans]
    parts.append((arrow_ref.at[0], arrow_out_ref.at[0, :, own]))
    copies = exchange(parts, peer, send_sem, recv_sem)
    local.wait()
    local_arrow.wait()
    for copy in copies:
        copy.wait()


def put_sums(sums_ref, tip, logs):
    effects = tip.shape[0]
    sums_ref[...] = jnp.zeros_like(sums_ref)
    sums_ref[0:effects, 0:effects] = tip
    sums_ref[effects:, :] = logs


def pair_kernel(
    swap_hbm, inverse_hbm, sub_hbm, arrow_hbm, xh_hbm, xl_hbm, log_ref, both_hbm, left_ref, pair_sums_ref,
    own_ref, other_ref, sum_ref, own_sums_ref, other_sums_ref, inverse_ref, right_ref, arrow_ref, xh, xl, sh, sl,
    sems, local_sems, swap_send, swap_recv, send_sem, recv_sem, sums_send, sums_recv,
):
    core, me = lax.axis_index("blk"), lax.axis_index("tm")
    even = me % 2 == 0
    peer, partner = {"blk": 1 - core}, {"tm": me + 1 - 2 * (me % 2)}
    meet([peer, partner])
    rows = sum_ref.shape[0] // COPIES
    spans = [pl.ds(k * rows, rows) for k in range(COPIES)]
    swaps = exchange(
        [(swap_hbm.at[span, :], other_ref.at[span, :]) for span in spans], partner, swap_send, swap_recv
    )
    copies = fetch(
        (
            (sub_hbm.at[1], right_ref),
            (xh_hbm, xh),
            (xl_hbm, xl),
            (inverse_hbm, inverse_ref),
            (arrow_hbm.at[0], arrow_ref),
            (swap_hbm, own_ref),
        ),
        sems,
    )
    for copy in copies:
        copy.wait()
    split_rows(right_ref, sh, sl)

    def part(r, carry):
        span = block_span(r)
        value = -times((sh[span, :], sl[span, :]), (xh[...], xl[...]))
        left_ref[span, :] = jnp.where(me > 0, value, 0.0)
        return carry

    lax.fori_loop(0, sh.shape[0] // BLOCK, part, 0)
    put_sums(own_sums_ref, arrow_form(arrow_ref[...], inverse_ref), log_ref[...])
    sums = exchange([(own_sums_ref, other_sums_ref)], partner, sums_send, sums_recv)
    shares = []
    for k, span in enumerate(spans):
        swaps[k].wait()
        difference = own_ref[span, :] - other_ref[span, :]
        sum_ref[span, :] = jnp.where(even, difference, -difference)
        local = pltpu.make_async_copy(sum_ref.at[span, :], both_hbm.at[core, span, :], local_sems.at[k])
        local.start()
        shares.append(local)
        shares += exchange(
            [(sum_ref.at[span, :], both_hbm.at[core, span, :])], peer, send_sem.at[pl.ds(k, 1)], recv_sem.at[pl.ds(k, 1)]
        )
    for copy in shares + sums:
        copy.wait()
    pair_sums_ref[...] = own_sums_ref[...] + other_sums_ref[...]


def finish_kernel(kept_ref, above_ref, out_ref, peer_ref, send_sem, recv_sem):
    core = lax.axis_index("blk")
    peer = {"blk": 1 - core}
    out_ref[...] = kept_ref[...] - above_ref[...]
    meet([peer])
    copies = []
    for slot, block in enumerate((2 - 2 * core, 4 - 3 * core)):
        copies.append(
            pltpu.make_async_remote_copy(
                src_ref=out_ref.at[block_span(block), :],
                dst_ref=peer_ref.at[pl.ds(slot * BLOCK, BLOCK), :],
                send_sem=send_sem.at[slot],
                recv_sem=recv_sem.at[slot],
                device_id=peer,
                device_id_type=pl.DeviceIdType.MESH,
            )
        )
        copies[-1].start()
    for copy in copies:
        copy.wait()


def place_kernel(info_ref, packed_ref, peer_ref, separator_ref, out_ref):
    core, even = info_ref[0], info_ref[1] == 1

    @pl.when(even)
    def _():
        out_ref[0] = separator_ref[...]

    def packed(k):
        return packed_ref[k * BLOCK : (k + 1) * BLOCK, :]

    def put(row, column, value):
        out_ref[0, row * BLOCK : (row + 1) * BLOCK, column * BLOCK : (column + 1) * BLOCK] = value

    first, second = peer_ref[:BLOCK, :], peer_ref[BLOCK:, :]
    odd = jnp.logical_not(even)

    @pl.when(odd & (core == 0))
    def _():
        for row, column, value in (
            (0, 0, packed(0)), (1, 0, packed(1)), (2, 0, packed(2)), (3, 0, first.T),
            (0, 1, packed(1).T), (1, 1, packed(3)), (2, 1, packed(4)), (3, 1, second.T),
        ):
            put(row, column, value)

    @pl.when(odd & (core == 1))
    def _():
        for row, column, value in (
            (0, 0, first.T), (1, 0, second.T), (2, 0, packed(4)), (3, 0, packed(2).T),
            (0, 1, packed(0)), (1, 1, packed(1)), (2, 1, packed(2)), (3, 1, packed(3)),
        ):
            put(row, column, value)


def reduce_kernel(side, value_ref, out_ref, parts_ref, send_sem, recv_sem, last_send, last_recv):
    me = lax.axis_index("tm")
    odd = me % 2 == 1
    stages = [(side, (me // side) % side, side), (side, (me // side**2) % side, side**2), (2, (me // 2) % 2, 2)]

    def other(stage, step):
        count, place, stride = stages[stage]
        return me + ((place + step) % count - place) * stride

    def hand(partner):
        return pltpu.make_async_remote_copy(
            src_ref=out_ref,
            dst_ref=out_ref,
            send_sem=last_send,
            recv_sem=last_recv,
            device_id={"tm": partner},
            device_id_type=pl.DeviceIdType.MESH,
        )

    @pl.when(odd)
    def _():
        others = [{"tm": other(s, d)} for s in range(len(stages)) for d in range(1, stages[s][0])]
        meet(others + [{"tm": me - 1}])
        out_ref[...] = value_ref[...]
        for s, (count, place, _) in enumerate(stages):
            parts_ref[s, place] = out_ref[...]
            copies = []
            for d in range(1, count):
                copies += exchange(
                    [(out_ref, parts_ref.at[s, place])],
                    {"tm": other(s, d)},
                    send_sem.at[s, pl.ds(d, 1)],
                    recv_sem.at[s, pl.ds(d, 1)],
                )
            for copy in copies:
                copy.wait()
            total = parts_ref[s, 0]
            for k in range(1, count):
                total = total + parts_ref[s, k]
            out_ref[...] = total
        copy = hand(me - 1)
        copy.start()
        copy.wait_send()

    @pl.when(jnp.logical_not(odd))
    def _():
        meet([{"tm": me + 1}])
        hand(me + 1).wait_recv()


def vmem(count):
    return [pl.BlockSpec(memory_space=pltpu.VMEM)] * count


def shape_of(*sizes, dtype=F32):
    return jax.ShapeDtypeStruct(sizes, dtype)


SMEM_SPEC = pl.BlockSpec(memory_space=pltpu.SMEM)
ANY_SPEC = pl.BlockSpec(memory_space=pl.ANY)
HBM_SPEC = pl.BlockSpec(memory_space=pltpu.HBM)


def local_call(kernel, name, flops, mebibytes, **kwargs):
    return pl.pallas_call(
        kernel,
        compiler_params=pltpu.CompilerParams(vmem_limit_bytes=mebibytes * 2**20),
        cost_estimate=pl.CostEstimate(flops=flops, bytes_accessed=2**23, transcendentals=0),
        name=name,
        **kwargs,
    )


def remote_call(kernel, name, identity, mebibytes=24, **kwargs):
    return pl.pallas_call(
        kernel,
        compiler_params=pltpu.CompilerParams(
            collective_id=identity, has_side_effects=True, vmem_limit_bytes=mebibytes * 2**20
        ),
        name=name,
        **kwargs,
    )


def dma_sems(*shape):
    return pltpu.SemaphoreType.DMA(shape)


def whole(shape, index):
    return pl.BlockSpec(shape, lambda i: index, pipeline_mode=pl.Buffered(1))


def on_device(diag_blocks, sub_blocks, arrow_blocks, tip_block):
    partition = lax.axis_index("tm")
    parts = lax.axis_size("tm")
    order, half = diag_blocks.shape[1:]
    effects = arrow_blocks.shape[1]
    packed_rows = PACKED * BLOCK + effects * half // BLOCK
    evens = range(0, parts, 2)
    down = [(p, p - 1) for p in evens if p > 0]
    core = lax.axis_index("blk")
    info = jnp.stack([core, (partition % 2 == 0).astype(core.dtype), (partition > 0).astype(core.dtype)])
    square, tall = (order, order), (order, half)
    big = [pltpu.VMEM(square, BF16)] * 2
    thin = [pltpu.VMEM(tall, BF16)] * 2

    pivot, arrow_full = remote_call(
        gather_kernel, "gather_pivot", 1,
        out_shape=[shape_of(*square), shape_of(1, effects, order)],
        in_specs=[HBM_SPEC] * 2, out_specs=[ANY_SPEC] * 2,
        scratch_shapes=[dma_sems(2), dma_sems(COPIES + 1), dma_sems(COPIES + 1)],
    )(diag_blocks, arrow_blocks)
    sub_full = lax.all_gather(sub_blocks, "blk", axis=2, tiled=True)
    inverse, log_first = inverse_and_log(pivot)

    packed_shape = shape_of(packed_rows, BLOCK)
    packed_scratch = pltpu.VMEM((packed_rows, BLOCK), F32)
    swap, rest, x_high, x_low = local_call(
        first_products_kernel, "first_products", 10 * order**3, 58,
        out_shape=[packed_shape] * 2 + [shape_of(*tall, dtype=BF16)] * 2,
        in_specs=[SMEM_SPEC, *vmem(1), *[ANY_SPEC] * 4],
        out_specs=vmem(4),
        scratch_shapes=[pltpu.VMEM(square, F32)] * 3
        + [pltpu.VMEM(tall, F32), pltpu.VMEM((effects, half), F32), dma_sems(5)]
        + big * 3
        + thin,
    )(info, arrow_full, inverse, sub_full, diag_blocks, arrow_blocks)
    pairs = [(p, p + 1) for p in evens]
    both, left_own, pair_sums = remote_call(
        pair_kernel, "swap_and_fill", 2, 58,
        out_shape=[shape_of(2, packed_rows, BLOCK), shape_of(*tall), shape_of(effects + 8, TILE)],
        in_specs=[*[ANY_SPEC] * 6, *vmem(1)],
        out_specs=[ANY_SPEC, *vmem(2)],
        scratch_shapes=[packed_scratch] * 3
        + [pltpu.VMEM((effects + 8, TILE), F32)] * 2
        + [pltpu.VMEM(square, F32)] * 2
        + [pltpu.VMEM((effects, order), F32)]
        + thin
        + big
        + [dma_sems(6), *[dma_sems(COPIES)] * 5, dma_sems(1), dma_sems(1)],
    )(swap, inverse, sub_full, arrow_full, x_high, x_low, log_first)
    left_pair = lax.ppermute(left_own, "tm", pairs)
    left_full = lax.all_gather(left_own, "blk", axis=1, tiled=True)

    inverse, log_second, separator = inverse_of_packed(info, both, order, half)
    product = local_call(
        second_products_kernel, "second_products", 5 * order**3, 58,
        out_shape=packed_shape,
        in_specs=[SMEM_SPEC, *[ANY_SPEC] * 4],
        out_specs=vmem(1)[0],
        scratch_shapes=[pltpu.VMEM(square, F32)] * 2
        + [pltpu.VMEM((2, packed_rows - PACKED * BLOCK, BLOCK), F32), packed_scratch, dma_sems(4)]
        + big * 2
        + thin,
    )(info, inverse, left_full, both, rest)
    above = lax.ppermute(product, "tm", down)
    left_result, sums = local_call(
        second_fill_kernel, "second_fill", 6 * order**3, 58,
        out_shape=[shape_of(1, *tall), shape_of(effects + 8, TILE)],
        in_specs=[SMEM_SPEC, *vmem(7)],
        out_specs=vmem(2),
        scratch_shapes=big * 2 + thin,
    )(info, inverse, left_full, both, left_own, left_pair, pair_sums, log_second)
    totals = remote_call(
        functools.partial(reduce_kernel, SIDE), "reduce_terms", 3,
        out_shape=shape_of(effects + 8, TILE), in_specs=vmem(1), out_specs=vmem(1)[0],
        scratch_shapes=[
            pltpu.VMEM((3, SIDE, effects + 8, TILE), F32),
            dma_sems(3, SIDE), dma_sems(3, SIDE), pltpu.SemaphoreType.DMA, pltpu.SemaphoreType.DMA,
        ],
    )(sums)
    packed, swapped = remote_call(
        finish_kernel, "finish_blocks", 4,
        out_shape=[packed_shape, shape_of(2 * BLOCK, BLOCK)], in_specs=vmem(2), out_specs=vmem(2),
        scratch_shapes=[dma_sems(2), dma_sems(2)],
    )(product, above)
    diag_result = local_call(
        place_kernel, "place_blocks", 2**20, 12,
        out_shape=shape_of(1, *tall), in_specs=[SMEM_SPEC, *vmem(3)], out_specs=vmem(1)[0],
    )(info, packed, swapped, separator)
    last = PACKED * BLOCK
    own_arrow = lax.dynamic_index_in_dim(both[:, last:], core, 0, keepdims=False)
    arrow_result = arrow_unpack(jnp.where(info[1] == 1, own_arrow, packed[last:]))
    return (
        diag_result,
        left_result,
        arrow_result[None],
        tip_block - totals[:effects, :effects],
        jnp.sum(totals[effects]),
    )


def solution(mesh):
    in_specs = (P("tm", None, "blk"), P("tm", None, "blk"), P("tm", None, "blk"), P())
    out_specs = (P("tm", None, "blk"), P("tm", None, "blk"), P("tm", None, "blk"), P(), P())
    return jax.shard_map(
        on_device, mesh=mesh, in_specs=in_specs, out_specs=out_specs, check_vma=False
    )
```

```python
import functools

import jax
import jax.numpy as jnp
from jax import lax
from jax.experimental import pallas as pl
from jax.experimental.pallas import tpu as pltpu
from jax.sharding import PartitionSpec as P

F32 = jnp.float32
BF16 = jnp.bfloat16
TILE = 128
BLOCK = 256
PACKED = 5
COPIES = 4
SIDE = 4
GROUP = 2
SLOTS = TILE // (8 * GROUP)


def row_of(value, index):
    return jnp.broadcast_to(value[index : index + 1, :], (8, value.shape[1]))


def column_of(value, index):
    return jnp.broadcast_to(value[:, index : index + 1], (8, TILE))


def split_three(value):
    high = value.astype(BF16).astype(F32)
    rest = value - high
    middle = rest.astype(BF16).astype(F32)
    return high, middle, rest - middle


def split_two(value):
    high = value.astype(BF16)
    return high, (value - high.astype(F32)).astype(BF16)


def left_pieces(value):
    high, low = split_two(value)
    return jnp.concatenate([high, low, high], axis=1)


def right_pieces(value):
    high, low = split_two(value)
    return jnp.concatenate([high, high, low], axis=0)


def outer_product(rows_a, rows_b):
    ah, am, al = split_three(rows_a)
    bh, bm, bl = split_three(rows_b)
    left = jnp.concatenate([ah, am, ah, am, al, ah], axis=0).astype(BF16)
    right = jnp.concatenate([bh, bh, bm, bm, bh, bl], axis=0).astype(BF16)
    return lax.dot_general(left, right, (((0,), (0,)), ((), ())), preferred_element_type=F32)


def sweep_rows(rows, first, pivots, lane, sub):
    count = 8 * len(rows)
    columns = [[column_of(row, first + c) for c in range(count)] for row in rows]
    inside = (lane >= first) & (lane < first + count)
    solved = [
        jnp.where(lane == sub + first + 8 * h, -1.0, jnp.where(inside, 0.0, row)) for h, row in enumerate(rows)
    ]
    for c in range(count):
        group, place = c // 8, c % 8
        pivot = row_of(columns[group][c], place)
        scale = 1.0 / pivot
        pivots = jnp.where(lane == first + c, pivot, pivots)
        pivot_row = row_of(solved[group], place) * scale
        for h in range(len(rows)):
            value = solved[h] - columns[h][c] * pivot_row
            solved[h] = jnp.where(sub == place, pivot_row, value) if h == group else value
        for d in range(c + 1, count):
            entry = row_of(columns[group][d], place) * scale
            for h in range(len(rows)):
                value = columns[h][d] - columns[h][c] * entry
                columns[h][d] = jnp.where(sub == place, entry, value) if h == group else value
    return solved, pivots


def sweep_tile(tile, beside=None):
    lane = lax.broadcasted_iota(jnp.int32, (8, TILE), 1)
    sub = lax.broadcasted_iota(jnp.int32, (8, TILE), 0)
    pivots = jnp.ones((8, TILE), F32)
    width = 8 * GROUP
    rows = [tile[8 * i : 8 * i + 8, :] for i in range(TILE // 8)]
    for i in range(TILE // width):
        source = rows[GROUP * i : GROUP * i + GROUP]
        inside = (lane >= width * i) & (lane < width * i + width)
        solved, pivots = sweep_rows(source, width * i, pivots, lane, sub)
        update = outer_product(jnp.concatenate(source, axis=0), jnp.concatenate(solved, axis=0))
        for k in range(TILE // 8):
            if k // GROUP == i:
                continue
            kept = jnp.where(inside, 0.0, rows[k])
            if k == GROUP * (i + 1):
                for c in range(width):
                    kept = kept - column_of(rows[k], width * i + c) * row_of(solved[c // 8], c % 8)
                rows[k] = kept
            else:
                rows[k] = kept - update[8 * k : 8 * k + 8, :]
        rows[GROUP * i : GROUP * i + GROUP] = solved
        if beside is not None:
            beside(i)
    return jnp.concatenate(rows, axis=0), pivots


def tile_span(index):
    return pl.ds(pl.multiple_of(index * TILE, TILE), TILE)


def close_tile(order, matrix_ref, left_ref, swept_ref, tile_ref, j, swept):
    count = order // TILE
    here, there = tile_span(j), tile_span(lax.rem(j + 1, count))
    swept_ref[...] = swept
    solved = jnp.dot(left_pieces(swept), right_pieces(matrix_ref[here, there]), preferred_element_type=F32)
    tile_ref[...] = matrix_ref[there, there] + jnp.dot(
        left_pieces(matrix_ref[there, here]), right_pieces(solved), preferred_element_type=F32
    )
    matrix_ref[here, here] = jnp.zeros((TILE, TILE), F32)
    for r in range(count):
        span = slice(r * TILE, (r + 1) * TILE)
        left_ref[span, :] = left_pieces(matrix_ref[span, here])
    matrix_ref[:, here] = jnp.zeros((order, TILE), F32)
    matrix_ref[here, here] = swept


def solve_tile_rows(order, matrix_ref, swept_ref, right_ref, j):
    here = tile_span(j)
    rows = matrix_ref[here, :]
    lane = lax.broadcasted_iota(jnp.int32, (TILE, order), 1)
    inside = (lane >= j * TILE) & (lane < j * TILE + TILE)
    solved = -jnp.dot(left_pieces(swept_ref[...]), right_pieces(rows), preferred_element_type=F32)
    solved = jnp.where(inside, rows, solved)
    right_ref[...] = right_pieces(solved)
    matrix_ref[here, :] = solved


def update_rows(matrix_ref, left_ref, right_ref, span):
    matrix_ref[span, :] = matrix_ref[span, :] - jnp.dot(
        left_ref[span, :], right_ref[...], preferred_element_type=F32
    )


def eliminate_all(order, matrix_ref, log_ref, left_ref, right_ref, swept_ref, tile_ref):
    count = order // TILE
    swept, pivots = sweep_tile(matrix_ref[0:TILE, 0:TILE])
    close_tile(order, matrix_ref, left_ref, swept_ref, tile_ref, 0, swept)

    def step(j, logs):
        def beside(i):
            if i == 0:
                solve_tile_rows(order, matrix_ref, swept_ref, right_ref, j - 1)
                return
            first = (i - 1) * count // (SLOTS - 1)
            for r in range(first, i * count // (SLOTS - 1)):
                update_rows(matrix_ref, left_ref, right_ref, slice(r * TILE, (r + 1) * TILE))

        swept, pivots = sweep_tile(tile_ref[...], beside)
        close_tile(order, matrix_ref, left_ref, swept_ref, tile_ref, j, swept)
        return logs + jnp.log(pivots)

    log_ref[...] = lax.fori_loop(1, count, step, jnp.log(pivots))
    solve_tile_rows(order, matrix_ref, swept_ref, right_ref, count - 1)

    def update(r, carry):
        update_rows(matrix_ref, left_ref, right_ref, tile_span(r))
        return carry

    lax.fori_loop(0, count, update, 0)


def inverse_kernel(source_ref, inverse_ref, log_ref, *scratch):
    order = source_ref.shape[0]

    def take(r, carry):
        inverse_ref[tile_span(r), :] = source_ref[tile_span(r), :]
        return carry

    lax.fori_loop(0, order // TILE, take, 0)
    eliminate_all(order, inverse_ref, log_ref, *scratch)


def packed_inverse_kernel(info_ref, both_ref, inverse_ref, log_ref, own_ref, *scratch):
    order, half = own_ref.shape
    places = (((0, 0), (1, 0), (2, 0), (1, 1), (2, 1)), ((0, 3), (1, 3), (2, 3), (3, 3), (2, 2)))
    for source in range(2):
        for k, (row, column) in enumerate(places[source]):
            value = both_ref[source, k * BLOCK : (k + 1) * BLOCK, :]
            rows = slice(row * BLOCK, (row + 1) * BLOCK)
            columns = slice(column * BLOCK, (column + 1) * BLOCK)
            inverse_ref[rows, columns] = value
            if row != column:
                inverse_ref[columns, rows] = value.T
    own = pl.ds(pl.multiple_of(info_ref[0] * half, half), half)
    own_ref[...] = inverse_ref[:, own]
    eliminate_all(order, inverse_ref, log_ref, *scratch)


def inverse_scratch(order):
    return [
        pltpu.VMEM((order, 3 * TILE), BF16),
        pltpu.VMEM((3 * TILE, order), BF16),
        pltpu.VMEM((TILE, TILE), F32),
        pltpu.VMEM((TILE, TILE), F32),
    ]


def inverse_and_log(matrix):
    order = matrix.shape[0]
    return local_call(
        inverse_kernel, "first_inverse", 24 * order**3, 16,
        out_shape=[shape_of(order, order), shape_of(8, TILE)],
        in_specs=vmem(1), out_specs=vmem(2), scratch_shapes=inverse_scratch(order),
    )(matrix)


def inverse_of_packed(info, both, order, half):
    return local_call(
        packed_inverse_kernel, "second_inverse", 24 * order**3, 20,
        out_shape=[shape_of(order, order), shape_of(8, TILE), shape_of(order, half)],
        in_specs=[SMEM_SPEC, *vmem(1)], out_specs=vmem(3), scratch_shapes=inverse_scratch(order),
    )(info, both)


def times(left, right, left_dim=1, right_dim=0):
    dims = (((left_dim,), (right_dim,)), ((), ()))

    def dot(a, b):
        return lax.dot_general(a, b, dims, preferred_element_type=F32)

    return dot(left[0], right[0]) + (dot(left[0], right[1]) + dot(left[1], right[0]))


def split_rows(source, high_ref, low_ref, sign=1):
    def part(r, carry):
        high, low = split_two(sign * source[tile_span(r), :])
        high_ref[tile_span(r), :] = high
        low_ref[tile_span(r), :] = low
        return carry

    lax.fori_loop(0, high_ref.shape[0] // TILE, part, 0)


def block_span(index):
    return pl.ds(pl.multiple_of(index * BLOCK, BLOCK), BLOCK)


def packed_place(core, k):
    row = jnp.where(core == 0, jnp.where(k < 3, k, k - 2), jnp.where(k < 4, k, 2))
    column = jnp.where(core == 0, jnp.where(k < 3, 0, 1), jnp.where(k < 4, 1, 0))
    return row, column


def solve_into(inverse, right, out, right_dim):
    def part(r, carry):
        rows = block_span(r)
        value = times((inverse[0][rows, :], inverse[1][rows, :]), right, 1, right_dim)
        out[0][rows, :], out[1][rows, :] = split_two(value)
        return carry

    lax.fori_loop(0, inverse[0].shape[0] // BLOCK, part, 0)


def packed_gram(core, former, solved, left_dim, store):
    def part(k, carry):
        row, column = packed_place(core, k)
        if left_dim == 0:
            left = (former[0][:, block_span(row)], former[1][:, block_span(row)])
        else:
            left = (former[0][block_span(row), :], former[1][block_span(row), :])
        right = (solved[0][:, block_span(column)], solved[1][:, block_span(column)])
        store(k, row, column, times(left, right, left_dim, 0))
        return carry

    lax.fori_loop(0, PACKED, part, 0)


def arrow_pack(value):
    return jnp.concatenate([value[:, :BLOCK], value[:, BLOCK:]], axis=0)


def arrow_unpack(value):
    effects = value.shape[0] // 2
    return jnp.concatenate([value[:effects], value[effects:]], axis=1)


def fetch(pairs, sems):
    copies = [pltpu.make_async_copy(source, target, sems.at[k]) for k, (source, target) in enumerate(pairs)]
    for copy in copies:
        copy.start()
    return copies


def arrow_form(rows, inverse_ref):
    pieces = split_two(rows)
    through = -times(pieces, split_two(inverse_ref[...]))
    return times(split_two(through), pieces, 1, 1)


def separator_arrow(packed):
    return jnp.concatenate([arrow_unpack(packed[0]), arrow_unpack(packed[1])], axis=1)


def second_products_kernel(
    info_ref, inverse_hbm, left_hbm, both_hbm, rest_hbm, out_ref,
    inverse_ref, left_ref, arrow_ref, rest_ref, sems, vh, vl, bh, bl, xh, xl,
):
    core, even = info_ref[0], info_ref[1] == 1
    half = xh.shape[1]
    own = pl.ds(pl.multiple_of(core * half, half), half)
    last = slice(PACKED * BLOCK, None)
    copies = fetch(
        (
            (inverse_hbm, inverse_ref),
            (left_hbm, left_ref),
            (both_hbm.at[:, pl.ds(PACKED * BLOCK, arrow_ref.shape[1]), :], arrow_ref),
            (rest_hbm, rest_ref),
        ),
        sems,
    )
    copies[0].wait()
    split_rows(inverse_ref, vh, vl, -1)
    copies[1].wait()
    split_rows(left_ref, bh, bl)
    for copy in copies[2:]:
        copy.wait()
    rows = split_two(separator_arrow(arrow_ref[...]))

    @pl.when(even)
    def _():
        solve_into((vh, vl), (bh[:, own], bl[:, own]), (xh, xl), 0)

        def store(k, row, column, value):
            out_ref[block_span(k), :] = rest_ref[block_span(k), :] + value

        packed_gram(core, (bh, bl), (xh, xl), 0, store)
        out_ref[last, :] = rest_ref[last, :] + arrow_pack(times(rows, (xh[...], xl[...])))

    @pl.when(jnp.logical_not(even))
    def _():
        solve_into((vh, vl), (bh[own, :], bl[own, :]), (xh, xl), 1)

        def store(k, row, column, value):
            span = block_span(k)
            out_ref[span, :] = rest_ref[span, :] - value

        packed_gram(core, (bh, bl), (xh, xl), 1, store)
        change = arrow_pack(times(rows, (xh[...], xl[...])))
        out_ref[last, :] = rest_ref[last, :] - change


def second_terms_kernel(info_ref, inverse_hbm, arrow_ref, pair_sums_ref, log_ref, sums_ref, inverse_ref, sem):
    sums_ref[...] = pair_sums_ref[...]

    @pl.when(info_ref[1] == 0)
    def _():
        copy = pltpu.make_async_copy(inverse_hbm, inverse_ref, sem)
        copy.start()
        copy.wait()
        put_sums(sums_ref, arrow_form(separator_arrow(arrow_ref[...]), inverse_ref), log_ref[...])
        sums_ref[...] = sums_ref[...] + pair_sums_ref[...]


def second_fill_kernel(
    info_ref, totals_ref, inverse_hbm, left_hbm, own_hbm, pair_hbm, out_ref,
    inverse_ref, left_ref, pair_ref, sems, vh, vl, bh, bl, xh, xl,
):
    even = info_ref[1] == 1

    @pl.when(even)
    def _():
        copy = pltpu.make_async_copy(own_hbm, out_ref.at[0], sems.at[0])
        copy.start()
        copy.wait()

    @pl.when(jnp.logical_not(even))
    def _():
        copies = fetch(((inverse_hbm, inverse_ref), (pair_hbm, pair_ref), (left_hbm, left_ref)), sems)
        copies[0].wait()
        split_rows(inverse_ref, vh, vl, -1)
        copies[1].wait()
        solve_into((vh, vl), split_two(pair_ref[...]), (xh, xl), 0)
        copies[2].wait()
        split_rows(left_ref, bh, bl)

        def part(r, carry):
            rows = block_span(r)
            out_ref[0, rows, :] = -times((bh[rows, :], bl[rows, :]), (xh[...], xl[...]))
            return carry

        lax.fori_loop(0, bh.shape[0] // BLOCK, part, 0)


def meet(devices):
    barrier = pltpu.get_barrier_semaphore()
    for device in devices:
        pl.semaphore_signal(barrier, inc=1, device_id=device, device_id_type=pl.DeviceIdType.MESH)
    pl.semaphore_wait(barrier, len(devices))


def exchange(parts, peer, send_sem, recv_sem):
    copies = []
    for k, (source, target) in enumerate(parts):
        copies.append(
            pltpu.make_async_remote_copy(
                src_ref=source,
                dst_ref=target,
                send_sem=send_sem.at[k],
                recv_sem=recv_sem.at[k],
                device_id=peer,
                device_id_type=pl.DeviceIdType.MESH,
            )
        )
        copies[-1].start()
    return copies


def gather_kernel(diag_ref, arrow_ref, out_ref, arrow_out_ref, local_sems, send_sem, recv_sem):
    core = lax.axis_index("blk")
    peer = {"blk": 1 - core}
    half = diag_ref.shape[2]
    rows = diag_ref.shape[1] // COPIES
    own = pl.ds(pl.multiple_of(core * half, half), half)
    local = pltpu.make_async_copy(diag_ref.at[0], out_ref.at[:, own], local_sems.at[0])
    local.start()
    local_arrow = pltpu.make_async_copy(arrow_ref.at[0], arrow_out_ref.at[0, :, own], local_sems.at[1])
    local_arrow.start()
    meet([peer])
    spans = [pl.ds(k * rows, rows) for k in range(COPIES)]
    parts = [(diag_ref.at[0, span, :], out_ref.at[span, own]) for span in spans]
    parts.append((arrow_ref.at[0], arrow_out_ref.at[0, :, own]))
    copies = exchange(parts, peer, send_sem, recv_sem)
    local.wait()
    local_arrow.wait()
    for copy in copies:
        copy.wait()


def put_sums(sums_ref, tip, logs):
    effects = tip.shape[0]
    sums_ref[...] = jnp.zeros_like(sums_ref)
    sums_ref[0:effects, 0:effects] = tip
    sums_ref[effects:, :] = logs


def pair_kernel(
    inverse_hbm, sub_hbm, diag_hbm, own_arrow_hbm, arrow_ref, log_ref,
    both_hbm, left_out_ref, rest_ref, pair_sums_ref,
    inverse_ref, left_ref, right_ref, diag_ref, own_arrow_ref, swap_ref, other_ref, sum_ref,
    own_sums_ref, other_sums_ref, vh, vl, bh, bl, sh, sl, xh, xl, yh, yl,
    sems, local_sems, swap_send, swap_recv, send_sem, recv_sem, sums_send, sums_recv,
):
    core, me = lax.axis_index("blk"), lax.axis_index("tm")
    even = me % 2 == 0
    peer, partner = {"blk": 1 - core}, {"tm": me + 1 - 2 * (me % 2)}
    half = diag_ref.shape[1]
    own = pl.ds(pl.multiple_of(core * half, half), half)
    copies = fetch(
        (
            (inverse_hbm, inverse_ref),
            (sub_hbm.at[0], left_ref),
            (sub_hbm.at[1], right_ref),
            (diag_hbm.at[1], diag_ref),
            (own_arrow_hbm.at[1], own_arrow_ref),
        ),
        sems,
    )
    copies[0].wait()
    split_rows(inverse_ref, vh, vl, -1)
    copies[1].wait()
    split_rows(left_ref, bh, bl)
    solve_into((vh, vl), (bh[:, own], bl[:, own]), (xh, xl), 0)
    copies[2].wait()
    split_rows(right_ref, sh, sl)
    solve_into((vh, vl), (sh[own, :], sl[own, :]), (yh, yl), 1)
    copies[3].wait()
    copies[4].wait()
    meet([peer, partner])

    def keep(span, lower, upper):
        swap_ref[span, :] = jnp.where(even, upper, lower)
        rest_ref[span, :] = jnp.where(even, lower, upper)

    def swap(span, k):
        return pltpu.make_async_remote_copy(
            src_ref=swap_ref.at[span, :],
            dst_ref=other_ref.at[span, :],
            send_sem=swap_send.at[k],
            recv_sem=swap_recv.at[k],
            device_id=partner,
            device_id_type=pl.DeviceIdType.MESH,
        )

    def blocks(k, carry):
        row, column = packed_place(core, k)
        rows, columns = block_span(row), block_span(column)
        lower = times((bh[:, rows], bl[:, rows]), (xh[:, columns], xl[:, columns]), 0, 0)
        change = times((sh[rows, :], sl[rows, :]), (yh[:, columns], yl[:, columns]))
        keep(block_span(k), lower, diag_ref[rows, columns] - change)
        swap(block_span(k), k).start()
        return carry

    lax.fori_loop(0, PACKED, blocks, 0)
    rows = split_two(arrow_ref[0])
    last = pl.ds(PACKED * BLOCK, swap_ref.shape[0] - PACKED * BLOCK)
    keep(
        last,
        arrow_pack(times(rows, (xh[...], xl[...]))),
        arrow_pack(own_arrow_ref[...] - times(rows, (yh[...], yl[...]))),
    )
    swap(last, PACKED).start()

    def part(r, carry):
        span = block_span(r)
        value = -times((sh[span, :], sl[span, :]), (xh[...], xl[...]))
        left_out_ref[span, :] = jnp.where(me > 0, value, 0.0)
        return carry

    lax.fori_loop(0, sh.shape[0] // BLOCK, part, 0)
    put_sums(own_sums_ref, arrow_form(arrow_ref[0], inverse_ref), log_ref[...])
    sums = exchange([(own_sums_ref, other_sums_ref)], partner, sums_send, sums_recv)
    shares = []
    for k in range(PACKED + 1):
        span = last if k == PACKED else pl.ds(k * BLOCK, BLOCK)
        swap(span, k).wait()
        difference = swap_ref[span, :] - other_ref[span, :]
        sum_ref[span, :] = jnp.where(even, difference, -difference)
        local = pltpu.make_async_copy(sum_ref.at[span, :], both_hbm.at[core, span, :], local_sems.at[k])
        local.start()
        shares.append(local)
        shares += exchange(
            [(sum_ref.at[span, :], both_hbm.at[core, span, :])], peer, send_sem.at[pl.ds(k, 1)], recv_sem.at[pl.ds(k, 1)]
        )
    for copy in shares + sums:
        copy.wait()
    pair_sums_ref[...] = own_sums_ref[...] + other_sums_ref[...]


def finish_kernel(kept_ref, above_ref, out_ref, peer_ref, send_sem, recv_sem):
    core = lax.axis_index("blk")
    peer = {"blk": 1 - core}
    out_ref[...] = kept_ref[...] - above_ref[...]
    meet([peer])
    copies = []
    for slot, block in enumerate((2 - 2 * core, 4 - 3 * core)):
        copies.append(
            pltpu.make_async_remote_copy(
                src_ref=out_ref.at[block_span(block), :],
                dst_ref=peer_ref.at[pl.ds(slot * BLOCK, BLOCK), :],
                send_sem=send_sem.at[slot],
                recv_sem=recv_sem.at[slot],
                device_id=peer,
                device_id_type=pl.DeviceIdType.MESH,
            )
        )
        copies[-1].start()
    for copy in copies:
        copy.wait()


def place_kernel(info_ref, packed_ref, peer_ref, separator_ref, out_ref):
    core, even = info_ref[0], info_ref[1] == 1

    @pl.when(even)
    def _():
        out_ref[0] = separator_ref[...]

    def packed(k):
        return packed_ref[k * BLOCK : (k + 1) * BLOCK, :]

    def put(row, column, value):
        out_ref[0, row * BLOCK : (row + 1) * BLOCK, column * BLOCK : (column + 1) * BLOCK] = value

    first, second = peer_ref[:BLOCK, :], peer_ref[BLOCK:, :]
    odd = jnp.logical_not(even)

    @pl.when(odd & (core == 0))
    def _():
        for row, column, value in (
            (0, 0, packed(0)), (1, 0, packed(1)), (2, 0, packed(2)), (3, 0, first.T),
            (0, 1, packed(1).T), (1, 1, packed(3)), (2, 1, packed(4)), (3, 1, second.T),
        ):
            put(row, column, value)

    @pl.when(odd & (core == 1))
    def _():
        for row, column, value in (
            (0, 0, first.T), (1, 0, second.T), (2, 0, packed(4)), (3, 0, packed(2).T),
            (0, 1, packed(0)), (1, 1, packed(1)), (2, 1, packed(2)), (3, 1, packed(3)),
        ):
            put(row, column, value)


def reduce_kernel(side, value_ref, out_ref, parts_ref, send_sem, recv_sem, last_send, last_recv):
    me = lax.axis_index("tm")
    odd = me % 2 == 1
    stages = [(side, (me // side) % side, side), (side, (me // side**2) % side, side**2), (2, (me // 2) % 2, 2)]

    def other(stage, step):
        count, place, stride = stages[stage]
        return me + ((place + step) % count - place) * stride

    def hand(partner):
        return pltpu.make_async_remote_copy(
            src_ref=out_ref,
            dst_ref=out_ref,
            send_sem=last_send,
            recv_sem=last_recv,
            device_id={"tm": partner},
            device_id_type=pl.DeviceIdType.MESH,
        )

    @pl.when(odd)
    def _():
        others = [{"tm": other(s, d)} for s in range(len(stages)) for d in range(1, stages[s][0])]
        meet(others + [{"tm": me - 1}])
        out_ref[...] = value_ref[...]
        for s, (count, place, _) in enumerate(stages):
            parts_ref[s, place] = out_ref[...]
            copies = []
            for d in range(1, count):
                copies += exchange(
                    [(out_ref, parts_ref.at[s, place])],
                    {"tm": other(s, d)},
                    send_sem.at[s, pl.ds(d, 1)],
                    recv_sem.at[s, pl.ds(d, 1)],
                )
            for copy in copies:
                copy.wait()
            total = parts_ref[s, 0]
            for k in range(1, count):
                total = total + parts_ref[s, k]
            out_ref[...] = total
        copy = hand(me - 1)
        copy.start()
        copy.wait_send()

    @pl.when(jnp.logical_not(odd))
    def _():
        meet([{"tm": me + 1}])
        hand(me + 1).wait_recv()


def vmem(count):
    return [pl.BlockSpec(memory_space=pltpu.VMEM)] * count


def shape_of(*sizes, dtype=F32):
    return jax.ShapeDtypeStruct(sizes, dtype)


SMEM_SPEC = pl.BlockSpec(memory_space=pltpu.SMEM)
ANY_SPEC = pl.BlockSpec(memory_space=pl.ANY)
HBM_SPEC = pl.BlockSpec(memory_space=pltpu.HBM)


def local_call(kernel, name, flops, mebibytes, **kwargs):
    return pl.pallas_call(
        kernel,
        compiler_params=pltpu.CompilerParams(vmem_limit_bytes=mebibytes * 2**20),
        cost_estimate=pl.CostEstimate(flops=flops, bytes_accessed=2**23, transcendentals=0),
        name=name,
        **kwargs,
    )


def remote_call(kernel, name, identity, mebibytes=24, **kwargs):
    return pl.pallas_call(
        kernel,
        compiler_params=pltpu.CompilerParams(
            collective_id=identity, has_side_effects=True, vmem_limit_bytes=mebibytes * 2**20
        ),
        name=name,
        **kwargs,
    )


def dma_sems(*shape):
    return pltpu.SemaphoreType.DMA(shape)


def whole(shape, index):
    return pl.BlockSpec(shape, lambda i: index, pipeline_mode=pl.Buffered(1))


def on_device(diag_blocks, sub_blocks, arrow_blocks, tip_block):
    partition = lax.axis_index("tm")
    parts = lax.axis_size("tm")
    order, half = diag_blocks.shape[1:]
    effects = arrow_blocks.shape[1]
    packed_rows = PACKED * BLOCK + effects * half // BLOCK
    evens = range(0, parts, 2)
    down = [(p, p - 1) for p in evens if p > 0]
    core = lax.axis_index("blk")
    info = jnp.stack([core, (partition % 2 == 0).astype(core.dtype), (partition > 0).astype(core.dtype)])
    square, tall = (order, order), (order, half)
    big = [pltpu.VMEM(square, BF16)] * 2
    thin = [pltpu.VMEM(tall, BF16)] * 2

    pivot, arrow_full = remote_call(
        gather_kernel, "gather_pivot", 1,
        out_shape=[shape_of(*square), shape_of(1, effects, order)],
        in_specs=[HBM_SPEC] * 2, out_specs=[ANY_SPEC] * 2,
        scratch_shapes=[dma_sems(2), dma_sems(COPIES + 1), dma_sems(COPIES + 1)],
    )(diag_blocks, arrow_blocks)
    sub_full = lax.all_gather(sub_blocks, "blk", axis=2, tiled=True)
    inverse, log_first = inverse_and_log(pivot)

    packed_shape = shape_of(packed_rows, BLOCK)
    packed_scratch = pltpu.VMEM((packed_rows, BLOCK), F32)
    pairs = [(p, p + 1) for p in evens]
    both, left_own, rest, pair_sums = remote_call(
        pair_kernel, "products_and_swap", 2, 58,
        out_shape=[shape_of(2, packed_rows, BLOCK), shape_of(*tall), packed_shape, shape_of(effects + 8, TILE)],
        in_specs=[*[ANY_SPEC] * 4, *vmem(2)],
        out_specs=[ANY_SPEC, *vmem(3)],
        scratch_shapes=[pltpu.VMEM(square, F32)] * 3
        + [pltpu.VMEM(tall, F32), pltpu.VMEM((effects, half), F32)]
        + [packed_scratch] * 3
        + [pltpu.VMEM((effects + 8, TILE), F32)] * 2
        + big * 3
        + thin * 2
        + [dma_sems(5), *[dma_sems(PACKED + 1)] * 5, dma_sems(1), dma_sems(1)],
    )(inverse, sub_full, diag_blocks, arrow_blocks, arrow_full, log_first)
    left_pair = lax.ppermute(left_own, "tm", pairs)
    left_full = lax.all_gather(left_own, "blk", axis=1, tiled=True)

    inverse, log_second, separator = inverse_of_packed(info, both, order, half)
    product = local_call(
        second_products_kernel, "second_products", 5 * order**3, 58,
        out_shape=packed_shape,
        in_specs=[SMEM_SPEC, *[ANY_SPEC] * 4],
        out_specs=vmem(1)[0],
        scratch_shapes=[pltpu.VMEM(square, F32)] * 2
        + [pltpu.VMEM((2, packed_rows - PACKED * BLOCK, BLOCK), F32), packed_scratch, dma_sems(4)]
        + big * 2
        + thin,
    )(info, inverse, left_full, both, rest)
    above = lax.ppermute(product, "tm", down)
    sums = local_call(
        second_terms_kernel, "second_terms", order**3 // 2, 24,
        out_shape=shape_of(effects + 8, TILE),
        in_specs=[SMEM_SPEC, ANY_SPEC, *vmem(3)],
        out_specs=vmem(1)[0],
        scratch_shapes=[pltpu.VMEM(square, F32), pltpu.SemaphoreType.DMA],
    )(info, inverse, both[:, PACKED * BLOCK :], pair_sums, log_second)
    totals = remote_call(
        functools.partial(reduce_kernel, SIDE), "reduce_terms", 3,
        out_shape=shape_of(effects + 8, TILE), in_specs=vmem(1), out_specs=vmem(1)[0],
        scratch_shapes=[
            pltpu.VMEM((3, SIDE, effects + 8, TILE), F32),
            dma_sems(3, SIDE), dma_sems(3, SIDE), pltpu.SemaphoreType.DMA, pltpu.SemaphoreType.DMA,
        ],
    )(sums)
    left_result = local_call(
        second_fill_kernel, "second_fill", 6 * order**3, 58,
        out_shape=shape_of(1, *tall),
        in_specs=[SMEM_SPEC, *vmem(1), *[ANY_SPEC] * 4],
        out_specs=vmem(1)[0],
        scratch_shapes=[pltpu.VMEM(square, F32)] * 2 + [pltpu.VMEM(tall, F32), dma_sems(3)] + big * 2 + thin,
    )(info, totals, inverse, left_full, left_own, left_pair)
    packed, swapped = remote_call(
        finish_kernel, "finish_blocks", 4,
        out_shape=[packed_shape, shape_of(2 * BLOCK, BLOCK)], in_specs=vmem(2), out_specs=vmem(2),
        scratch_shapes=[dma_sems(2), dma_sems(2)],
    )(product, above)
    diag_result = local_call(
        place_kernel, "place_blocks", 2**20, 12,
        out_shape=shape_of(1, *tall), in_specs=[SMEM_SPEC, *vmem(3)], out_specs=vmem(1)[0],
    )(info, packed, swapped, separator)
    last = PACKED * BLOCK
    own_arrow = lax.dynamic_index_in_dim(both[:, last:], core, 0, keepdims=False)
    arrow_result = arrow_unpack(jnp.where(info[1] == 1, own_arrow, packed[last:]))
    return (
        diag_result,
        left_result,
        arrow_result[None],
        tip_block - totals[:effects, :effects],
        jnp.sum(totals[effects]),
    )


def solution(mesh):
    in_specs = (P("tm", None, "blk"), P("tm", None, "blk"), P("tm", None, "blk"), P())
    out_specs = (P("tm", None, "blk"), P("tm", None, "blk"), P("tm", None, "blk"), P(), P())
    return jax.shard_map(
        on_device, mesh=mesh, in_specs=in_specs, out_specs=out_specs, check_vma=False
    )
```

```python
import functools

import jax
import jax.numpy as jnp
from jax import lax
from jax.experimental import pallas as pl
from jax.experimental.pallas import tpu as pltpu
from jax.sharding import PartitionSpec as P

F32 = jnp.float32
BF16 = jnp.bfloat16
TILE = 128
BLOCK = 256
PACKED = 5
COPIES = 4
SIDE = 4
GROUP = 2
SLOTS = TILE // (8 * GROUP)


def row_of(value, index):
    return jnp.broadcast_to(value[index : index + 1, :], (8, value.shape[1]))


def column_of(value, index):
    return jnp.broadcast_to(value[:, index : index + 1], (8, TILE))


def split_three(value):
    high = value.astype(BF16).astype(F32)
    rest = value - high
    middle = rest.astype(BF16).astype(F32)
    return high, middle, rest - middle


def split_two(value):
    high = value.astype(BF16)
    return high, (value - high.astype(F32)).astype(BF16)


def left_pieces(value):
    high, low = split_two(value)
    return jnp.concatenate([high, low, high], axis=1)


def right_pieces(value):
    high, low = split_two(value)
    return jnp.concatenate([high, high, low], axis=0)


def outer_product(rows_a, rows_b):
    ah, am, al = split_three(rows_a)
    bh, bm, bl = split_three(rows_b)
    left = jnp.concatenate([ah, am, ah, am, al, ah], axis=0).astype(BF16)
    right = jnp.concatenate([bh, bh, bm, bm, bh, bl], axis=0).astype(BF16)
    return lax.dot_general(left, right, (((0,), (0,)), ((), ())), preferred_element_type=F32)


def sweep_rows(rows, first, pivots, lane, sub):
    count = 8 * len(rows)
    columns = [[column_of(row, first + c) for c in range(count)] for row in rows]
    inside = (lane >= first) & (lane < first + count)
    solved = [
        jnp.where(lane == sub + first + 8 * h, -1.0, jnp.where(inside, 0.0, row)) for h, row in enumerate(rows)
    ]
    for c in range(count):
        group, place = c // 8, c % 8
        pivot = row_of(columns[group][c], place)
        scale = 1.0 / pivot
        pivots = jnp.where(lane == first + c, pivot, pivots)
        pivot_row = row_of(solved[group], place) * scale
        for h in range(len(rows)):
            value = solved[h] - columns[h][c] * pivot_row
            solved[h] = jnp.where(sub == place, pivot_row, value) if h == group else value
        for d in range(c + 1, count):
            entry = row_of(columns[group][d], place) * scale
            for h in range(len(rows)):
                value = columns[h][d] - columns[h][c] * entry
                columns[h][d] = jnp.where(sub == place, entry, value) if h == group else value
    return solved, pivots


def sweep_tile(tile, beside=None):
    lane = lax.broadcasted_iota(jnp.int32, (8, TILE), 1)
    sub = lax.broadcasted_iota(jnp.int32, (8, TILE), 0)
    pivots = jnp.ones((8, TILE), F32)
    width = 8 * GROUP
    rows = [tile[8 * i : 8 * i + 8, :] for i in range(TILE // 8)]
    for i in range(TILE // width):
        source = rows[GROUP * i : GROUP * i + GROUP]
        inside = (lane >= width * i) & (lane < width * i + width)
        solved, pivots = sweep_rows(source, width * i, pivots, lane, sub)
        update = outer_product(jnp.concatenate(source, axis=0), jnp.concatenate(solved, axis=0))
        for k in range(TILE // 8):
            if k // GROUP == i:
                continue
            kept = jnp.where(inside, 0.0, rows[k])
            if k == GROUP * (i + 1):
                for c in range(width):
                    kept = kept - column_of(rows[k], width * i + c) * row_of(solved[c // 8], c % 8)
                rows[k] = kept
            else:
                rows[k] = kept - update[8 * k : 8 * k + 8, :]
        rows[GROUP * i : GROUP * i + GROUP] = solved
        if beside is not None:
            beside(i)
    return jnp.concatenate(rows, axis=0), pivots


def tile_span(index):
    return pl.ds(pl.multiple_of(index * TILE, TILE), TILE)


def close_tile(order, matrix_ref, left_ref, swept_ref, tile_ref, j, swept):
    count = order // TILE
    here, there = tile_span(j), tile_span(lax.rem(j + 1, count))
    swept_ref[...] = swept
    solved = jnp.dot(left_pieces(swept), right_pieces(matrix_ref[here, there]), preferred_element_type=F32)
    tile_ref[...] = matrix_ref[there, there] + jnp.dot(
        left_pieces(matrix_ref[there, here]), right_pieces(solved), preferred_element_type=F32
    )
    matrix_ref[here, here] = jnp.zeros((TILE, TILE), F32)
    for r in range(count):
        span = slice(r * TILE, (r + 1) * TILE)
        left_ref[span, :] = left_pieces(matrix_ref[span, here])
    matrix_ref[:, here] = jnp.zeros((order, TILE), F32)
    matrix_ref[here, here] = swept


def solve_tile_rows(order, matrix_ref, swept_ref, right_ref, j):
    here = tile_span(j)
    rows = matrix_ref[here, :]
    lane = lax.broadcasted_iota(jnp.int32, (TILE, order), 1)
    inside = (lane >= j * TILE) & (lane < j * TILE + TILE)
    solved = -jnp.dot(left_pieces(swept_ref[...]), right_pieces(rows), preferred_element_type=F32)
    solved = jnp.where(inside, rows, solved)
    right_ref[...] = right_pieces(solved)
    matrix_ref[here, :] = solved


def update_rows(matrix_ref, left_ref, right_ref, span):
    matrix_ref[span, :] = matrix_ref[span, :] - jnp.dot(
        left_ref[span, :], right_ref[...], preferred_element_type=F32
    )


def eliminate_all(order, matrix_ref, log_ref, left_ref, right_ref, swept_ref, tile_ref):
    count = order // TILE
    swept, pivots = sweep_tile(matrix_ref[0:TILE, 0:TILE])
    close_tile(order, matrix_ref, left_ref, swept_ref, tile_ref, 0, swept)

    def step(j, logs):
        def beside(i):
            if i == 0:
                solve_tile_rows(order, matrix_ref, swept_ref, right_ref, j - 1)
                return
            first = (i - 1) * count // (SLOTS - 1)
            for r in range(first, i * count // (SLOTS - 1)):
                update_rows(matrix_ref, left_ref, right_ref, slice(r * TILE, (r + 1) * TILE))

        swept, pivots = sweep_tile(tile_ref[...], beside)
        close_tile(order, matrix_ref, left_ref, swept_ref, tile_ref, j, swept)
        return logs + jnp.log(pivots)

    log_ref[...] = lax.fori_loop(1, count, step, jnp.log(pivots))
    solve_tile_rows(order, matrix_ref, swept_ref, right_ref, count - 1)

    def update(r, carry):
        update_rows(matrix_ref, left_ref, right_ref, tile_span(r))
        return carry

    lax.fori_loop(0, count, update, 0)


def inverse_kernel(source_ref, inverse_ref, log_ref, *scratch):
    order = source_ref.shape[0]

    def take(r, carry):
        inverse_ref[tile_span(r), :] = source_ref[tile_span(r), :]
        return carry

    lax.fori_loop(0, order // TILE, take, 0)
    eliminate_all(order, inverse_ref, log_ref, *scratch)


def packed_inverse_kernel(info_ref, both_ref, inverse_ref, log_ref, own_ref, *scratch):
    order, half = own_ref.shape
    places = (((0, 0), (1, 0), (2, 0), (1, 1), (2, 1)), ((0, 3), (1, 3), (2, 3), (3, 3), (2, 2)))
    for source in range(2):
        for k, (row, column) in enumerate(places[source]):
            value = both_ref[source, k * BLOCK : (k + 1) * BLOCK, :]
            rows = slice(row * BLOCK, (row + 1) * BLOCK)
            columns = slice(column * BLOCK, (column + 1) * BLOCK)
            inverse_ref[rows, columns] = value
            if row != column:
                inverse_ref[columns, rows] = value.T
    own = pl.ds(pl.multiple_of(info_ref[0] * half, half), half)
    own_ref[...] = inverse_ref[:, own]
    eliminate_all(order, inverse_ref, log_ref, *scratch)


def inverse_scratch(order):
    return [
        pltpu.VMEM((order, 3 * TILE), BF16),
        pltpu.VMEM((3 * TILE, order), BF16),
        pltpu.VMEM((TILE, TILE), F32),
        pltpu.VMEM((TILE, TILE), F32),
    ]


def inverse_and_log(matrix):
    order = matrix.shape[0]
    return local_call(
        inverse_kernel, "first_inverse", 24 * order**3, 16,
        out_shape=[shape_of(order, order), shape_of(8, TILE)],
        in_specs=vmem(1), out_specs=vmem(2), scratch_shapes=inverse_scratch(order),
    )(matrix)


def inverse_of_packed(info, both, order, half):
    return local_call(
        packed_inverse_kernel, "second_inverse", 24 * order**3, 20,
        out_shape=[shape_of(order, order), shape_of(8, TILE), shape_of(order, half)],
        in_specs=[SMEM_SPEC, *vmem(1)], out_specs=vmem(3), scratch_shapes=inverse_scratch(order),
    )(info, both)


def times(left, right, left_dim=1, right_dim=0):
    dims = (((left_dim,), (right_dim,)), ((), ()))

    def dot(a, b):
        return lax.dot_general(a, b, dims, preferred_element_type=F32)

    return dot(left[0], right[0]) + (dot(left[0], right[1]) + dot(left[1], right[0]))


def split_rows(source, high_ref, low_ref, sign=1):
    def part(r, carry):
        high, low = split_two(sign * source[tile_span(r), :])
        high_ref[tile_span(r), :] = high
        low_ref[tile_span(r), :] = low
        return carry

    lax.fori_loop(0, high_ref.shape[0] // TILE, part, 0)


def block_span(index):
    return pl.ds(pl.multiple_of(index * BLOCK, BLOCK), BLOCK)


def packed_place(core, k):
    row = jnp.where(core == 0, jnp.where(k < 3, k, k - 2), jnp.where(k < 4, k, 2))
    column = jnp.where(core == 0, jnp.where(k < 3, 0, 1), jnp.where(k < 4, 1, 0))
    return row, column


def solve_into(inverse, right, out, right_dim):
    def part(r, carry):
        rows = block_span(r)
        value = times((inverse[0][rows, :], inverse[1][rows, :]), right, 1, right_dim)
        out[0][rows, :], out[1][rows, :] = split_two(value)
        return carry

    lax.fori_loop(0, inverse[0].shape[0] // BLOCK, part, 0)


def packed_gram(core, former, solved, left_dim, store):
    def part(k, carry):
        row, column = packed_place(core, k)
        if left_dim == 0:
            left = (former[0][:, block_span(row)], former[1][:, block_span(row)])
        else:
            left = (former[0][block_span(row), :], former[1][block_span(row), :])
        right = (solved[0][:, block_span(column)], solved[1][:, block_span(column)])
        store(k, row, column, times(left, right, left_dim, 0))
        return carry

    lax.fori_loop(0, PACKED, part, 0)


def arrow_pack(value):
    return jnp.concatenate([value[:, :BLOCK], value[:, BLOCK:]], axis=0)


def arrow_unpack(value):
    effects = value.shape[0] // 2
    return jnp.concatenate([value[:effects], value[effects:]], axis=1)


def fetch(pairs, sems):
    copies = [pltpu.make_async_copy(source, target, sems.at[k]) for k, (source, target) in enumerate(pairs)]
    for copy in copies:
        copy.start()
    return copies


def arrow_form(rows, inverse_ref):
    pieces = split_two(rows)
    through = -times(pieces, split_two(inverse_ref[...]))
    return times(split_two(through), pieces, 1, 1)


def separator_arrow(packed):
    return jnp.concatenate([arrow_unpack(packed[0]), arrow_unpack(packed[1])], axis=1)


def second_products_kernel(
    info_ref, inverse_hbm, left_hbm, both_hbm, rest_hbm, out_ref,
    inverse_ref, left_ref, arrow_ref, rest_ref, sems, vh, vl, bh, bl, xh, xl,
):
    core, even = info_ref[0], info_ref[1] == 1
    half = xh.shape[1]
    own = pl.ds(pl.multiple_of(core * half, half), half)
    last = slice(PACKED * BLOCK, None)
    copies = fetch(
        (
            (inverse_hbm, inverse_ref),
            (left_hbm, left_ref),
            (both_hbm.at[:, pl.ds(PACKED * BLOCK, arrow_ref.shape[1]), :], arrow_ref),
            (rest_hbm, rest_ref),
        ),
        sems,
    )
    copies[0].wait()
    split_rows(inverse_ref, vh, vl, -1)
    copies[1].wait()
    split_rows(left_ref, bh, bl)
    for copy in copies[2:]:
        copy.wait()
    rows = split_two(separator_arrow(arrow_ref[...]))

    @pl.when(even)
    def _():
        solve_into((vh, vl), (bh[:, own], bl[:, own]), (xh, xl), 0)

        def store(k, row, column, value):
            out_ref[block_span(k), :] = rest_ref[block_span(k), :] + value

        packed_gram(core, (bh, bl), (xh, xl), 0, store)
        out_ref[last, :] = rest_ref[last, :] + arrow_pack(times(rows, (xh[...], xl[...])))

    @pl.when(jnp.logical_not(even))
    def _():
        solve_into((vh, vl), (bh[own, :], bl[own, :]), (xh, xl), 1)

        def store(k, row, column, value):
            span = block_span(k)
            out_ref[span, :] = rest_ref[span, :] - value

        packed_gram(core, (bh, bl), (xh, xl), 1, store)
        change = arrow_pack(times(rows, (xh[...], xl[...])))
        out_ref[last, :] = rest_ref[last, :] - change


def second_terms_kernel(info_ref, inverse_hbm, arrow_ref, pair_sums_ref, log_ref, sums_ref, inverse_ref, sem):
    sums_ref[...] = pair_sums_ref[...]

    @pl.when(info_ref[1] == 0)
    def _():
        copy = pltpu.make_async_copy(inverse_hbm, inverse_ref, sem)
        copy.start()
        copy.wait()
        put_sums(sums_ref, arrow_form(separator_arrow(arrow_ref[...]), inverse_ref), log_ref[...])
        sums_ref[...] = sums_ref[...] + pair_sums_ref[...]


def second_fill_kernel(
    info_ref, totals_ref, inverse_hbm, left_hbm, own_hbm, pair_hbm, out_ref,
    inverse_ref, left_ref, pair_ref, sems, vh, vl, bh, bl, xh, xl,
):
    even = info_ref[1] == 1

    @pl.when(even)
    def _():
        copy = pltpu.make_async_copy(own_hbm, out_ref.at[0], sems.at[0])
        copy.start()
        copy.wait()

    @pl.when(jnp.logical_not(even))
    def _():
        copies = fetch(((inverse_hbm, inverse_ref), (pair_hbm, pair_ref), (left_hbm, left_ref)), sems)
        copies[0].wait()
        split_rows(inverse_ref, vh, vl, -1)
        copies[1].wait()
        solve_into((vh, vl), split_two(pair_ref[...]), (xh, xl), 0)
        copies[2].wait()
        split_rows(left_ref, bh, bl)

        def part(r, carry):
            rows = block_span(r)
            out_ref[0, rows, :] = -times((bh[rows, :], bl[rows, :]), (xh[...], xl[...]))
            return carry

        lax.fori_loop(0, bh.shape[0] // BLOCK, part, 0)


def meet(devices):
    barrier = pltpu.get_barrier_semaphore()
    for device in devices:
        pl.semaphore_signal(barrier, inc=1, device_id=device, device_id_type=pl.DeviceIdType.MESH)
    pl.semaphore_wait(barrier, len(devices))


def exchange(parts, peer, send_sem, recv_sem):
    copies = []
    for k, (source, target) in enumerate(parts):
        copies.append(
            pltpu.make_async_remote_copy(
                src_ref=source,
                dst_ref=target,
                send_sem=send_sem.at[k],
                recv_sem=recv_sem.at[k],
                device_id=peer,
                device_id_type=pl.DeviceIdType.MESH,
            )
        )
        copies[-1].start()
    return copies


def gather_kernel(diag_ref, arrow_ref, out_ref, arrow_out_ref, local_sems, send_sem, recv_sem):
    core = lax.axis_index("blk")
    peer = {"blk": 1 - core}
    half = diag_ref.shape[2]
    rows = diag_ref.shape[1] // COPIES
    own = pl.ds(pl.multiple_of(core * half, half), half)
    local = pltpu.make_async_copy(diag_ref.at[0], out_ref.at[:, own], local_sems.at[0])
    local.start()
    local_arrow = pltpu.make_async_copy(arrow_ref.at[0], arrow_out_ref.at[0, :, own], local_sems.at[1])
    local_arrow.start()
    meet([peer])
    spans = [pl.ds(k * rows, rows) for k in range(COPIES)]
    parts = [(diag_ref.at[0, span, :], out_ref.at[span, own]) for span in spans]
    parts.append((arrow_ref.at[0], arrow_out_ref.at[0, :, own]))
    copies = exchange(parts, peer, send_sem, recv_sem)
    local.wait()
    local_arrow.wait()
    for copy in copies:
        copy.wait()


def put_sums(sums_ref, tip, logs):
    effects = tip.shape[0]
    sums_ref[...] = jnp.zeros_like(sums_ref)
    sums_ref[0:effects, 0:effects] = tip
    sums_ref[effects:, :] = logs


def pair_kernel(
    inverse_hbm, sub_hbm, diag_hbm, own_arrow_hbm, arrow_ref, log_ref,
    both_hbm, left_out_ref, rest_ref, pair_sums_ref,
    inverse_ref, left_ref, right_ref, diag_ref, own_arrow_ref, swap_ref, other_ref, sum_ref,
    own_sums_ref, other_sums_ref, vh, vl, bh, bl, sh, sl, xh, xl, yh, yl,
    sems, local_sems, swap_send, swap_recv, send_sem, recv_sem, sums_send, sums_recv,
):
    core, me = lax.axis_index("blk"), lax.axis_index("tm")
    even = me % 2 == 0
    peer, partner = {"blk": 1 - core}, {"tm": me + 1 - 2 * (me % 2)}
    half = diag_ref.shape[1]
    own = pl.ds(pl.multiple_of(core * half, half), half)
    copies = fetch(
        (
            (inverse_hbm, inverse_ref),
            (sub_hbm.at[0], left_ref),
            (sub_hbm.at[1], right_ref),
            (diag_hbm.at[1], diag_ref),
            (own_arrow_hbm.at[1], own_arrow_ref),
        ),
        sems,
    )
    copies[0].wait()
    split_rows(inverse_ref, vh, vl, -1)
    copies[1].wait()
    split_rows(left_ref, bh, bl)
    solve_into((vh, vl), (bh[:, own], bl[:, own]), (xh, xl), 0)
    copies[2].wait()
    split_rows(right_ref, sh, sl)
    solve_into((vh, vl), (sh[own, :], sl[own, :]), (yh, yl), 1)
    copies[3].wait()
    copies[4].wait()
    meet([peer, partner])

    def keep(span, lower, upper):
        swap_ref[span, :] = jnp.where(even, upper, lower)
        rest_ref[span, :] = jnp.where(even, lower, upper)

    def swap(span, k):
        return pltpu.make_async_remote_copy(
            src_ref=swap_ref.at[span, :],
            dst_ref=other_ref.at[span, :],
            send_sem=swap_send.at[k],
            recv_sem=swap_recv.at[k],
            device_id=partner,
            device_id_type=pl.DeviceIdType.MESH,
        )

    def blocks(k, carry):
        row, column = packed_place(core, k)
        rows, columns = block_span(row), block_span(column)
        lower = times((bh[:, rows], bl[:, rows]), (xh[:, columns], xl[:, columns]), 0, 0)
        change = times((sh[rows, :], sl[rows, :]), (yh[:, columns], yl[:, columns]))
        keep(block_span(k), lower, diag_ref[rows, columns] - change)
        swap(block_span(k), k).start()
        return carry

    lax.fori_loop(0, PACKED, blocks, 0)
    rows = split_two(arrow_ref[0])
    last = pl.ds(PACKED * BLOCK, swap_ref.shape[0] - PACKED * BLOCK)
    keep(
        last,
        arrow_pack(times(rows, (xh[...], xl[...]))),
        arrow_pack(own_arrow_ref[...] - times(rows, (yh[...], yl[...]))),
    )
    swap(last, PACKED).start()

    def part(r, carry):
        span = block_span(r)
        value = -times((sh[span, :], sl[span, :]), (xh[...], xl[...]))
        left_out_ref[span, :] = jnp.where(me > 0, value, 0.0)
        return carry

    lax.fori_loop(0, sh.shape[0] // BLOCK, part, 0)
    put_sums(own_sums_ref, arrow_form(arrow_ref[0], inverse_ref), log_ref[...])
    sums = exchange([(own_sums_ref, other_sums_ref)], partner, sums_send, sums_recv)
    shares = []
    for k in range(PACKED + 1):
        span = last if k == PACKED else pl.ds(k * BLOCK, BLOCK)
        swap(span, k).wait()
        difference = swap_ref[span, :] - other_ref[span, :]
        sum_ref[span, :] = jnp.where(even, difference, -difference)
        local = pltpu.make_async_copy(sum_ref.at[span, :], both_hbm.at[core, span, :], local_sems.at[k])
        local.start()
        shares.append(local)
        shares += exchange(
            [(sum_ref.at[span, :], both_hbm.at[core, span, :])], peer, send_sem.at[pl.ds(k, 1)], recv_sem.at[pl.ds(k, 1)]
        )
    for copy in shares + sums:
        copy.wait()
    pair_sums_ref[...] = own_sums_ref[...] + other_sums_ref[...]


def finish_kernel(kept_ref, above_ref, out_ref, peer_ref, send_sem, recv_sem):
    core = lax.axis_index("blk")
    peer = {"blk": 1 - core}
    out_ref[...] = kept_ref[...] - above_ref[...]
    meet([peer])
    copies = []
    for slot, block in enumerate((2 - 2 * core, 4 - 3 * core)):
        copies.append(
            pltpu.make_async_remote_copy(
                src_ref=out_ref.at[block_span(block), :],
                dst_ref=peer_ref.at[pl.ds(slot * BLOCK, BLOCK), :],
                send_sem=send_sem.at[slot],
                recv_sem=recv_sem.at[slot],
                device_id=peer,
                device_id_type=pl.DeviceIdType.MESH,
            )
        )
        copies[-1].start()
    for copy in copies:
        copy.wait()


def place_kernel(info_ref, packed_ref, peer_ref, separator_ref, out_ref):
    core, even = info_ref[0], info_ref[1] == 1

    @pl.when(even)
    def _():
        out_ref[0] = separator_ref[...]

    def packed(k):
        return packed_ref[k * BLOCK : (k + 1) * BLOCK, :]

    def put(row, column, value):
        out_ref[0, row * BLOCK : (row + 1) * BLOCK, column * BLOCK : (column + 1) * BLOCK] = value

    first, second = peer_ref[:BLOCK, :], peer_ref[BLOCK:, :]
    odd = jnp.logical_not(even)

    @pl.when(odd & (core == 0))
    def _():
        for row, column, value in (
            (0, 0, packed(0)), (1, 0, packed(1)), (2, 0, packed(2)), (3, 0, first.T),
            (0, 1, packed(1).T), (1, 1, packed(3)), (2, 1, packed(4)), (3, 1, second.T),
        ):
            put(row, column, value)

    @pl.when(odd & (core == 1))
    def _():
        for row, column, value in (
            (0, 0, first.T), (1, 0, second.T), (2, 0, packed(4)), (3, 0, packed(2).T),
            (0, 1, packed(0)), (1, 1, packed(1)), (2, 1, packed(2)), (3, 1, packed(3)),
        ):
            put(row, column, value)


def reduce_kernel(side, value_ref, out_ref, parts_ref, first_sems, send_sem, recv_sem, last_send, last_recv):
    me = lax.axis_index("tm")
    place_y = me % side
    root = me - place_y + 1
    stages = [((me // side) % side, side), ((me // side**2) % side, side**2)]

    def other(stage, step):
        place, stride = stages[stage]
        return me + ((place + step) % side - place) * stride

    def hand(source, target, send, recv, device):
        return pltpu.make_async_remote_copy(
            src_ref=source,
            dst_ref=target,
            send_sem=send,
            recv_sem=recv,
            device_id={"tm": device},
            device_id_type=pl.DeviceIdType.MESH,
        )

    slot = parts_ref.at[len(stages), 0]

    @pl.when(place_y == 1)
    def _():
        row = (me - 1, me + 1, me + 2)
        meet([{"tm": other(s, d)} for s in range(len(stages)) for d in range(1, side)] + [{"tm": k} for k in row])
        hand(value_ref, slot, first_sems.at[0], first_sems.at[1], me + 2).wait_recv()
        out_ref[...] = value_ref[...] + parts_ref[len(stages), 0]
        for s, (place, _) in enumerate(stages):
            parts_ref[s, place] = out_ref[...]
            copies = []
            for d in range(1, side):
                copies += exchange(
                    [(out_ref, parts_ref.at[s, place])],
                    {"tm": other(s, d)},
                    send_sem.at[s, pl.ds(d, 1)],
                    recv_sem.at[s, pl.ds(d, 1)],
                )
            for copy in copies:
                copy.wait()
            total = parts_ref[s, 0]
            for k in range(1, side):
                total = total + parts_ref[s, k]
            out_ref[...] = total
        copies = [hand(out_ref, out_ref, last_send.at[k], last_recv, device) for k, device in enumerate(row)]
        for copy in copies:
            copy.start()
        for copy in copies:
            copy.wait_send()

    @pl.when(place_y != 1)
    def _():
        meet([{"tm": root}])

        @pl.when(place_y == 3)
        def _():
            copy = hand(value_ref, slot, first_sems.at[0], first_sems.at[1], root)
            copy.start()
            copy.wait_send()

        hand(out_ref, out_ref, last_send.at[0], last_recv, root).wait_recv()


def vmem(count):
    return [pl.BlockSpec(memory_space=pltpu.VMEM)] * count


def shape_of(*sizes, dtype=F32):
    return jax.ShapeDtypeStruct(sizes, dtype)


SMEM_SPEC = pl.BlockSpec(memory_space=pltpu.SMEM)
ANY_SPEC = pl.BlockSpec(memory_space=pl.ANY)
HBM_SPEC = pl.BlockSpec(memory_space=pltpu.HBM)


def local_call(kernel, name, flops, mebibytes, **kwargs):
    return pl.pallas_call(
        kernel,
        compiler_params=pltpu.CompilerParams(vmem_limit_bytes=mebibytes * 2**20),
        cost_estimate=pl.CostEstimate(flops=flops, bytes_accessed=2**23, transcendentals=0),
        name=name,
        **kwargs,
    )


def remote_call(kernel, name, identity, mebibytes=24, **kwargs):
    return pl.pallas_call(
        kernel,
        compiler_params=pltpu.CompilerParams(
            collective_id=identity, has_side_effects=True, vmem_limit_bytes=mebibytes * 2**20
        ),
        name=name,
        **kwargs,
    )


def dma_sems(*shape):
    return pltpu.SemaphoreType.DMA(shape)


def whole(shape, index):
    return pl.BlockSpec(shape, lambda i: index, pipeline_mode=pl.Buffered(1))


def on_device(diag_blocks, sub_blocks, arrow_blocks, tip_block):
    partition = lax.axis_index("tm")
    parts = lax.axis_size("tm")
    order, half = diag_blocks.shape[1:]
    effects = arrow_blocks.shape[1]
    packed_rows = PACKED * BLOCK + effects * half // BLOCK
    evens = range(0, parts, 2)
    down = [(p, p - 1) for p in evens if p > 0]
    core = lax.axis_index("blk")
    info = jnp.stack([core, (partition % 2 == 0).astype(core.dtype), (partition > 0).astype(core.dtype)])
    square, tall = (order, order), (order, half)
    big = [pltpu.VMEM(square, BF16)] * 2
    thin = [pltpu.VMEM(tall, BF16)] * 2

    pivot, arrow_full = remote_call(
        gather_kernel, "gather_pivot", 1,
        out_shape=[shape_of(*square), shape_of(1, effects, order)],
        in_specs=[HBM_SPEC] * 2, out_specs=[ANY_SPEC] * 2,
        scratch_shapes=[dma_sems(2), dma_sems(COPIES + 1), dma_sems(COPIES + 1)],
    )(diag_blocks, arrow_blocks)
    sub_full = lax.all_gather(sub_blocks, "blk", axis=2, tiled=True)
    inverse, log_first = inverse_and_log(pivot)

    packed_shape = shape_of(packed_rows, BLOCK)
    packed_scratch = pltpu.VMEM((packed_rows, BLOCK), F32)
    pairs = [(p, p + 1) for p in evens]
    both, left_own, rest, pair_sums = remote_call(
        pair_kernel, "products_and_swap", 2, 58,
        out_shape=[shape_of(2, packed_rows, BLOCK), shape_of(*tall), packed_shape, shape_of(effects + 8, TILE)],
        in_specs=[*[ANY_SPEC] * 4, *vmem(2)],
        out_specs=[ANY_SPEC, *vmem(3)],
        scratch_shapes=[pltpu.VMEM(square, F32)] * 3
        + [pltpu.VMEM(tall, F32), pltpu.VMEM((effects, half), F32)]
        + [packed_scratch] * 3
        + [pltpu.VMEM((effects + 8, TILE), F32)] * 2
        + big * 3
        + thin * 2
        + [dma_sems(5), *[dma_sems(PACKED + 1)] * 5, dma_sems(1), dma_sems(1)],
    )(inverse, sub_full, diag_blocks, arrow_blocks, arrow_full, log_first)
    left_pair = lax.ppermute(left_own, "tm", pairs)
    left_full = lax.all_gather(left_own, "blk", axis=1, tiled=True)

    inverse, log_second, separator = inverse_of_packed(info, both, order, half)
    product = local_call(
        second_products_kernel, "second_products", 5 * order**3, 58,
        out_shape=packed_shape,
        in_specs=[SMEM_SPEC, *[ANY_SPEC] * 4],
        out_specs=vmem(1)[0],
        scratch_shapes=[pltpu.VMEM(square, F32)] * 2
        + [pltpu.VMEM((2, packed_rows - PACKED * BLOCK, BLOCK), F32), packed_scratch, dma_sems(4)]
        + big * 2
        + thin,
    )(info, inverse, left_full, both, rest)
    above = lax.ppermute(product, "tm", down)
    sums = local_call(
        second_terms_kernel, "second_terms", order**3 // 2, 24,
        out_shape=shape_of(effects + 8, TILE),
        in_specs=[SMEM_SPEC, ANY_SPEC, *vmem(3)],
        out_specs=vmem(1)[0],
        scratch_shapes=[pltpu.VMEM(square, F32), pltpu.SemaphoreType.DMA],
    )(info, inverse, both[:, PACKED * BLOCK :], pair_sums, log_second)
    totals = remote_call(
        functools.partial(reduce_kernel, SIDE), "reduce_terms", 3,
        out_shape=shape_of(effects + 8, TILE), in_specs=vmem(1), out_specs=vmem(1)[0],
        scratch_shapes=[
            pltpu.VMEM((3, SIDE, effects + 8, TILE), F32),
            dma_sems(2), dma_sems(2, SIDE), dma_sems(2, SIDE), dma_sems(3), pltpu.SemaphoreType.DMA,
        ],
    )(sums)
    left_result = local_call(
        second_fill_kernel, "second_fill", 6 * order**3, 58,
        out_shape=shape_of(1, *tall),
        in_specs=[SMEM_SPEC, *vmem(1), *[ANY_SPEC] * 4],
        out_specs=vmem(1)[0],
        scratch_shapes=[pltpu.VMEM(square, F32)] * 2 + [pltpu.VMEM(tall, F32), dma_sems(3)] + big * 2 + thin,
    )(info, totals, inverse, left_full, left_own, left_pair)
    packed, swapped = remote_call(
        finish_kernel, "finish_blocks", 4,
        out_shape=[packed_shape, shape_of(2 * BLOCK, BLOCK)], in_specs=vmem(2), out_specs=vmem(2),
        scratch_shapes=[dma_sems(2), dma_sems(2)],
    )(product, above)
    diag_result = local_call(
        place_kernel, "place_blocks", 2**20, 12,
        out_shape=shape_of(1, *tall), in_specs=[SMEM_SPEC, *vmem(3)], out_specs=vmem(1)[0],
    )(info, packed, swapped, separator)
    last = PACKED * BLOCK
    own_arrow = lax.dynamic_index_in_dim(both[:, last:], core, 0, keepdims=False)
    arrow_result = arrow_unpack(jnp.where(info[1] == 1, own_arrow, packed[last:]))
    return (
        diag_result,
        left_result,
        arrow_result[None],
        tip_block - totals[:effects, :effects],
        jnp.sum(totals[effects]),
    )


def solution(mesh):
    in_specs = (P("tm", None, "blk"), P("tm", None, "blk"), P("tm", None, "blk"), P())
    out_specs = (P("tm", None, "blk"), P("tm", None, "blk"), P("tm", None, "blk"), P(), P())
    return jax.shard_map(
        on_device, mesh=mesh, in_specs=in_specs, out_specs=out_specs, check_vma=False
    )
```

```python
import functools

import jax
import jax.numpy as jnp
from jax import lax
from jax.experimental import pallas as pl
from jax.experimental.pallas import tpu as pltpu
from jax.sharding import PartitionSpec as P

F32 = jnp.float32
BF16 = jnp.bfloat16
TILE = 128
BLOCK = 256
PACKED = 5
COPIES = 4
SIDE = 4
GROUP = 2
SLOTS = TILE // (8 * GROUP)


def row_of(value, index):
    return jnp.broadcast_to(value[index : index + 1, :], (8, value.shape[1]))


def column_of(value, index):
    return jnp.broadcast_to(value[:, index : index + 1], (8, TILE))


def split_three(value):
    high = value.astype(BF16).astype(F32)
    rest = value - high
    middle = rest.astype(BF16).astype(F32)
    return high, middle, rest - middle


def split_two(value):
    high = value.astype(BF16)
    return high, (value - high.astype(F32)).astype(BF16)


def left_pieces(value):
    high, low = split_two(value)
    return jnp.concatenate([high, low, high], axis=1)


def right_pieces(value):
    high, low = split_two(value)
    return jnp.concatenate([high, high, low], axis=0)


def outer_product(rows_a, rows_b):
    ah, am, al = split_three(rows_a)
    bh, bm, bl = split_three(rows_b)
    left = jnp.concatenate([ah, am, ah, am, al, ah], axis=0).astype(BF16)
    right = jnp.concatenate([bh, bh, bm, bm, bh, bl], axis=0).astype(BF16)
    return lax.dot_general(left, right, (((0,), (0,)), ((), ())), preferred_element_type=F32)


def sweep_rows(rows, first, pivots, lane, sub):
    count = 8 * len(rows)
    columns = [[column_of(row, first + c) for c in range(count)] for row in rows]
    inside = (lane >= first) & (lane < first + count)
    solved = [
        jnp.where(lane == sub + first + 8 * h, -1.0, jnp.where(inside, 0.0, row)) for h, row in enumerate(rows)
    ]
    for c in range(count):
        group, place = c // 8, c % 8
        pivot = row_of(columns[group][c], place)
        scale = 1.0 / pivot
        pivots = jnp.where(lane == first + c, pivot, pivots)
        pivot_row = row_of(solved[group], place) * scale
        for h in range(len(rows)):
            value = solved[h] - columns[h][c] * pivot_row
            solved[h] = jnp.where(sub == place, pivot_row, value) if h == group else value
        for d in range(c + 1, count):
            entry = row_of(columns[group][d], place) * scale
            for h in range(len(rows)):
                value = columns[h][d] - columns[h][c] * entry
                columns[h][d] = jnp.where(sub == place, entry, value) if h == group else value
    return solved, pivots


def sweep_tile(tile, beside=None):
    lane = lax.broadcasted_iota(jnp.int32, (8, TILE), 1)
    sub = lax.broadcasted_iota(jnp.int32, (8, TILE), 0)
    pivots = jnp.ones((8, TILE), F32)
    width = 8 * GROUP
    rows = [tile[8 * i : 8 * i + 8, :] for i in range(TILE // 8)]
    for i in range(TILE // width):
        source = rows[GROUP * i : GROUP * i + GROUP]
        inside = (lane >= width * i) & (lane < width * i + width)
        solved, pivots = sweep_rows(source, width * i, pivots, lane, sub)
        update = outer_product(jnp.concatenate(source, axis=0), jnp.concatenate(solved, axis=0))
        for k in range(TILE // 8):
            if k // GROUP == i:
                continue
            kept = jnp.where(inside, 0.0, rows[k])
            if k == GROUP * (i + 1):
                for c in range(width):
                    kept = kept - column_of(rows[k], width * i + c) * row_of(solved[c // 8], c % 8)
                rows[k] = kept
            else:
                rows[k] = kept - update[8 * k : 8 * k + 8, :]
        rows[GROUP * i : GROUP * i + GROUP] = solved
        if beside is not None:
            beside(i)
    return jnp.concatenate(rows, axis=0), pivots


def tile_span(index):
    return pl.ds(pl.multiple_of(index * TILE, TILE), TILE)


def close_tile(order, matrix_ref, left_ref, swept_ref, tile_ref, j, swept):
    count = order // TILE
    here, there = tile_span(j), tile_span(lax.rem(j + 1, count))
    swept_ref[...] = swept
    solved = jnp.dot(left_pieces(swept), right_pieces(matrix_ref[here, there]), preferred_element_type=F32)
    tile_ref[...] = matrix_ref[there, there] + jnp.dot(
        left_pieces(matrix_ref[there, here]), right_pieces(solved), preferred_element_type=F32
    )
    matrix_ref[here, here] = jnp.zeros((TILE, TILE), F32)
    for r in range(count):
        span = slice(r * TILE, (r + 1) * TILE)
        left_ref[span, :] = left_pieces(matrix_ref[span, here])
    matrix_ref[:, here] = jnp.zeros((order, TILE), F32)
    matrix_ref[here, here] = swept


def solve_tile_rows(order, matrix_ref, swept_ref, right_ref, j):
    here = tile_span(j)
    rows = matrix_ref[here, :]
    lane = lax.broadcasted_iota(jnp.int32, (TILE, order), 1)
    inside = (lane >= j * TILE) & (lane < j * TILE + TILE)
    solved = -jnp.dot(left_pieces(swept_ref[...]), right_pieces(rows), preferred_element_type=F32)
    solved = jnp.where(inside, rows, solved)
    right_ref[...] = right_pieces(solved)
    matrix_ref[here, :] = solved


def update_rows(matrix_ref, left_ref, right_ref, span):
    matrix_ref[span, :] = matrix_ref[span, :] - jnp.dot(
        left_ref[span, :], right_ref[...], preferred_element_type=F32
    )


def eliminate_all(order, matrix_ref, log_ref, left_ref, right_ref, swept_ref, tile_ref):
    count = order // TILE
    swept, pivots = sweep_tile(matrix_ref[0:TILE, 0:TILE])
    close_tile(order, matrix_ref, left_ref, swept_ref, tile_ref, 0, swept)

    def step(j, logs):
        def beside(i):
            if i == 0:
                solve_tile_rows(order, matrix_ref, swept_ref, right_ref, j - 1)
                return
            first = (i - 1) * count // (SLOTS - 1)
            for r in range(first, i * count // (SLOTS - 1)):
                update_rows(matrix_ref, left_ref, right_ref, slice(r * TILE, (r + 1) * TILE))

        swept, pivots = sweep_tile(tile_ref[...], beside)
        close_tile(order, matrix_ref, left_ref, swept_ref, tile_ref, j, swept)
        return logs + jnp.log(pivots)

    log_ref[...] = lax.fori_loop(1, count, step, jnp.log(pivots))
    solve_tile_rows(order, matrix_ref, swept_ref, right_ref, count - 1)

    def update(r, carry):
        update_rows(matrix_ref, left_ref, right_ref, tile_span(r))
        return carry

    lax.fori_loop(0, count, update, 0)


def inverse_kernel(source_ref, inverse_ref, log_ref, *scratch):
    order = source_ref.shape[0]

    def take(r, carry):
        inverse_ref[tile_span(r), :] = source_ref[tile_span(r), :]
        return carry

    lax.fori_loop(0, order // TILE, take, 0)
    eliminate_all(order, inverse_ref, log_ref, *scratch)


def packed_inverse_kernel(info_ref, both_ref, inverse_ref, log_ref, own_ref, *scratch):
    order, half = own_ref.shape
    places = (((0, 0), (1, 0), (2, 0), (1, 1), (2, 1)), ((0, 3), (1, 3), (2, 3), (3, 3), (2, 2)))
    for source in range(2):
        for k, (row, column) in enumerate(places[source]):
            value = both_ref[source, k * BLOCK : (k + 1) * BLOCK, :]
            rows = slice(row * BLOCK, (row + 1) * BLOCK)
            columns = slice(column * BLOCK, (column + 1) * BLOCK)
            inverse_ref[rows, columns] = value
            if row != column:
                inverse_ref[columns, rows] = value.T
    own = pl.ds(pl.multiple_of(info_ref[0] * half, half), half)
    own_ref[...] = inverse_ref[:, own]
    eliminate_all(order, inverse_ref, log_ref, *scratch)


def inverse_scratch(order):
    return [
        pltpu.VMEM((order, 3 * TILE), BF16),
        pltpu.VMEM((3 * TILE, order), BF16),
        pltpu.VMEM((TILE, TILE), F32),
        pltpu.VMEM((TILE, TILE), F32),
    ]


def inverse_and_log(matrix):
    order = matrix.shape[0]
    return local_call(
        inverse_kernel, "first_inverse", 24 * order**3, 16,
        out_shape=[shape_of(order, order), shape_of(8, TILE)],
        in_specs=vmem(1), out_specs=vmem(2), scratch_shapes=inverse_scratch(order),
    )(matrix)


def inverse_of_packed(info, both, order, half):
    return local_call(
        packed_inverse_kernel, "second_inverse", 24 * order**3, 20,
        out_shape=[shape_of(order, order), shape_of(8, TILE), shape_of(order, half)],
        in_specs=[SMEM_SPEC, *vmem(1)], out_specs=vmem(3), scratch_shapes=inverse_scratch(order),
    )(info, both)


def times(left, right, left_dim=1, right_dim=0):
    dims = (((left_dim,), (right_dim,)), ((), ()))

    def dot(a, b):
        return lax.dot_general(a, b, dims, preferred_element_type=F32)

    return dot(left[0], right[0]) + (dot(left[0], right[1]) + dot(left[1], right[0]))


def split_rows(source, high_ref, low_ref, sign=1):
    def part(r, carry):
        high, low = split_two(sign * source[tile_span(r), :])
        high_ref[tile_span(r), :] = high
        low_ref[tile_span(r), :] = low
        return carry

    lax.fori_loop(0, high_ref.shape[0] // TILE, part, 0)


def block_span(index):
    return pl.ds(pl.multiple_of(index * BLOCK, BLOCK), BLOCK)


def packed_place(core, k):
    row = jnp.where(core == 0, jnp.where(k < 3, k, k - 2), jnp.where(k < 4, k, 2))
    column = jnp.where(core == 0, jnp.where(k < 3, 0, 1), jnp.where(k < 4, 1, 0))
    return row, column


def solve_into(inverse, right, out, right_dim):
    def part(r, carry):
        rows = block_span(r)
        value = times((inverse[0][rows, :], inverse[1][rows, :]), right, 1, right_dim)
        out[0][rows, :], out[1][rows, :] = split_two(value)
        return carry

    lax.fori_loop(0, inverse[0].shape[0] // BLOCK, part, 0)


def packed_gram(core, former, solved, left_dim, store):
    def part(k, carry):
        row, column = packed_place(core, k)
        if left_dim == 0:
            left = (former[0][:, block_span(row)], former[1][:, block_span(row)])
        else:
            left = (former[0][block_span(row), :], former[1][block_span(row), :])
        right = (solved[0][:, block_span(column)], solved[1][:, block_span(column)])
        store(k, row, column, times(left, right, left_dim, 0))
        return carry

    lax.fori_loop(0, PACKED, part, 0)


def arrow_pack(value):
    return jnp.concatenate([value[:, :BLOCK], value[:, BLOCK:]], axis=0)


def arrow_unpack(value):
    effects = value.shape[0] // 2
    return jnp.concatenate([value[:effects], value[effects:]], axis=1)


def fetch(pairs, sems):
    copies = [pltpu.make_async_copy(source, target, sems.at[k]) for k, (source, target) in enumerate(pairs)]
    for copy in copies:
        copy.start()
    return copies


def arrow_form(rows, inverse_ref):
    pieces = split_two(rows)
    through = -times(pieces, split_two(inverse_ref[...]))
    return times(split_two(through), pieces, 1, 1)


def separator_arrow(packed):
    return jnp.concatenate([arrow_unpack(packed[0]), arrow_unpack(packed[1])], axis=1)


def second_products_kernel(
    info_ref, inverse_hbm, left_hbm, both_hbm, rest_hbm, out_ref,
    inverse_ref, left_ref, arrow_ref, rest_ref, sems, vh, vl, bh, bl, xh, xl,
):
    core, even = info_ref[0], info_ref[1] == 1
    half = xh.shape[1]
    own = pl.ds(pl.multiple_of(core * half, half), half)
    last = slice(PACKED * BLOCK, None)
    copies = fetch(
        (
            (left_hbm, left_ref),
            (inverse_hbm, inverse_ref),
            (both_hbm.at[:, pl.ds(PACKED * BLOCK, arrow_ref.shape[1]), :], arrow_ref),
            (rest_hbm, rest_ref),
        ),
        sems,
    )
    copies[0].wait()
    split_rows(left_ref, bh, bl)
    copies[1].wait()
    split_rows(inverse_ref, vh, vl, -1)
    for copy in copies[2:]:
        copy.wait()
    rows = split_two(separator_arrow(arrow_ref[...]))

    @pl.when(even)
    def _():
        solve_into((vh, vl), (bh[:, own], bl[:, own]), (xh, xl), 0)

        def store(k, row, column, value):
            out_ref[block_span(k), :] = rest_ref[block_span(k), :] + value

        packed_gram(core, (bh, bl), (xh, xl), 0, store)
        out_ref[last, :] = rest_ref[last, :] + arrow_pack(times(rows, (xh[...], xl[...])))

    @pl.when(jnp.logical_not(even))
    def _():
        solve_into((vh, vl), (bh[own, :], bl[own, :]), (xh, xl), 1)

        def store(k, row, column, value):
            span = block_span(k)
            out_ref[span, :] = rest_ref[span, :] - value

        packed_gram(core, (bh, bl), (xh, xl), 1, store)
        change = arrow_pack(times(rows, (xh[...], xl[...])))
        out_ref[last, :] = rest_ref[last, :] - change


def second_terms_kernel(
    info_ref, inverse_hbm, pair_hbm, arrow_ref, pair_sums_ref, log_ref, sums_ref, xh_ref, xl_ref,
    inverse_ref, pair_ref, sems, vh, vl,
):
    sums_ref[...] = pair_sums_ref[...]

    @pl.when(info_ref[1] == 0)
    def _():
        copies = fetch(((inverse_hbm, inverse_ref), (pair_hbm, pair_ref)), sems)
        copies[0].wait()
        put_sums(sums_ref, arrow_form(separator_arrow(arrow_ref[...]), inverse_ref), log_ref[...])
        sums_ref[...] = sums_ref[...] + pair_sums_ref[...]
        split_rows(inverse_ref, vh, vl, -1)
        copies[1].wait()
        solve_into((vh, vl), split_two(pair_ref[...]), (xh_ref, xl_ref), 0)


def second_fill_kernel(info_ref, totals_ref, left_hbm, own_hbm, xh_ref, xl_ref, out_ref, left_ref, sem, bh, bl):
    even = info_ref[1] == 1

    @pl.when(even)
    def _():
        copy = pltpu.make_async_copy(own_hbm, out_ref.at[0], sem)
        copy.start()
        copy.wait()

    @pl.when(jnp.logical_not(even))
    def _():
        copy = pltpu.make_async_copy(left_hbm, left_ref, sem)
        copy.start()
        copy.wait()
        split_rows(left_ref, bh, bl)

        def part(r, carry):
            rows = block_span(r)
            out_ref[0, rows, :] = -times((bh[rows, :], bl[rows, :]), (xh_ref[...], xl_ref[...]))
            return carry

        lax.fori_loop(0, bh.shape[0] // BLOCK, part, 0)


def meet(devices):
    barrier = pltpu.get_barrier_semaphore()
    for device in devices:
        pl.semaphore_signal(barrier, inc=1, device_id=device, device_id_type=pl.DeviceIdType.MESH)
    pl.semaphore_wait(barrier, len(devices))


def exchange(parts, peer, send_sem, recv_sem):
    copies = []
    for k, (source, target) in enumerate(parts):
        copies.append(
            pltpu.make_async_remote_copy(
                src_ref=source,
                dst_ref=target,
                send_sem=send_sem.at[k],
                recv_sem=recv_sem.at[k],
                device_id=peer,
                device_id_type=pl.DeviceIdType.MESH,
            )
        )
        copies[-1].start()
    return copies


def gather_kernel(diag_ref, arrow_ref, out_ref, arrow_out_ref, local_sems, send_sem, recv_sem):
    core = lax.axis_index("blk")
    peer = {"blk": 1 - core}
    half = diag_ref.shape[2]
    rows = diag_ref.shape[1] // COPIES
    own = pl.ds(pl.multiple_of(core * half, half), half)
    local = pltpu.make_async_copy(diag_ref.at[0], out_ref.at[:, own], local_sems.at[0])
    local.start()
    local_arrow = pltpu.make_async_copy(arrow_ref.at[0], arrow_out_ref.at[0, :, own], local_sems.at[1])
    local_arrow.start()
    meet([peer])
    spans = [pl.ds(k * rows, rows) for k in range(COPIES)]
    parts = [(diag_ref.at[0, span, :], out_ref.at[span, own]) for span in spans]
    parts.append((arrow_ref.at[0], arrow_out_ref.at[0, :, own]))
    copies = exchange(parts, peer, send_sem, recv_sem)
    local.wait()
    local_arrow.wait()
    for copy in copies:
        copy.wait()


def put_sums(sums_ref, tip, logs):
    effects = tip.shape[0]
    sums_ref[...] = jnp.zeros_like(sums_ref)
    sums_ref[0:effects, 0:effects] = tip
    sums_ref[effects:, :] = logs


def pair_kernel(
    inverse_hbm, sub_hbm, diag_hbm, own_arrow_hbm, arrow_ref, log_ref,
    both_hbm, left_out_ref, rest_ref, pair_sums_ref,
    inverse_ref, left_ref, right_ref, diag_ref, own_arrow_ref, swap_ref, other_ref, sum_ref,
    own_sums_ref, other_sums_ref, vh, vl, bh, bl, sh, sl, xh, xl, yh, yl,
    sems, local_sems, swap_send, swap_recv, send_sem, recv_sem, sums_send, sums_recv,
):
    core, me = lax.axis_index("blk"), lax.axis_index("tm")
    even = me % 2 == 0
    peer, partner = {"blk": 1 - core}, {"tm": me + 1 - 2 * (me % 2)}
    half = diag_ref.shape[1]
    own = pl.ds(pl.multiple_of(core * half, half), half)
    copies = fetch(
        (
            (sub_hbm.at[0], left_ref),
            (inverse_hbm, inverse_ref),
            (sub_hbm.at[1], right_ref),
            (diag_hbm.at[1], diag_ref),
            (own_arrow_hbm.at[1], own_arrow_ref),
        ),
        sems,
    )
    copies[0].wait()
    split_rows(left_ref, bh, bl)
    copies[1].wait()
    split_rows(inverse_ref, vh, vl, -1)
    solve_into((vh, vl), (bh[:, own], bl[:, own]), (xh, xl), 0)
    copies[2].wait()
    split_rows(right_ref, sh, sl)
    solve_into((vh, vl), (sh[own, :], sl[own, :]), (yh, yl), 1)
    copies[3].wait()
    copies[4].wait()
    meet([peer, partner])

    def keep(span, lower, upper):
        swap_ref[span, :] = jnp.where(even, upper, lower)
        rest_ref[span, :] = jnp.where(even, lower, upper)

    def swap(span, k):
        return pltpu.make_async_remote_copy(
            src_ref=swap_ref.at[span, :],
            dst_ref=other_ref.at[span, :],
            send_sem=swap_send.at[k],
            recv_sem=swap_recv.at[k],
            device_id=partner,
            device_id_type=pl.DeviceIdType.MESH,
        )

    def blocks(k, carry):
        row, column = packed_place(core, k)
        rows, columns = block_span(row), block_span(column)
        lower = times((bh[:, rows], bl[:, rows]), (xh[:, columns], xl[:, columns]), 0, 0)
        change = times((sh[rows, :], sl[rows, :]), (yh[:, columns], yl[:, columns]))
        keep(block_span(k), lower, diag_ref[rows, columns] - change)
        swap(block_span(k), k).start()
        return carry

    lax.fori_loop(0, PACKED, blocks, 0)
    rows = split_two(arrow_ref[0])
    last = pl.ds(PACKED * BLOCK, swap_ref.shape[0] - PACKED * BLOCK)
    keep(
        last,
        arrow_pack(times(rows, (xh[...], xl[...]))),
        arrow_pack(own_arrow_ref[...] - times(rows, (yh[...], yl[...]))),
    )
    swap(last, PACKED).start()

    def part(r, carry):
        span = block_span(r)
        value = -times((sh[span, :], sl[span, :]), (xh[...], xl[...]))
        left_out_ref[span, :] = jnp.where(me > 0, value, 0.0)
        return carry

    lax.fori_loop(0, sh.shape[0] // BLOCK, part, 0)
    put_sums(own_sums_ref, arrow_form(arrow_ref[0], inverse_ref), log_ref[...])
    sums = exchange([(own_sums_ref, other_sums_ref)], partner, sums_send, sums_recv)
    shares = []
    for k in range(PACKED + 1):
        span = last if k == PACKED else pl.ds(k * BLOCK, BLOCK)
        swap(span, k).wait()
        difference = swap_ref[span, :] - other_ref[span, :]
        sum_ref[span, :] = jnp.where(even, difference, -difference)
        local = pltpu.make_async_copy(sum_ref.at[span, :], both_hbm.at[core, span, :], local_sems.at[k])
        local.start()
        shares.append(local)
        shares += exchange(
            [(sum_ref.at[span, :], both_hbm.at[core, span, :])], peer, send_sem.at[pl.ds(k, 1)], recv_sem.at[pl.ds(k, 1)]
        )
    for copy in shares + sums:
        copy.wait()
    pair_sums_ref[...] = own_sums_ref[...] + other_sums_ref[...]


def finish_kernel(kept_ref, above_ref, out_ref, peer_ref, send_sem, recv_sem):
    core = lax.axis_index("blk")
    peer = {"blk": 1 - core}
    out_ref[...] = kept_ref[...] - above_ref[...]
    meet([peer])
    copies = []
    for slot, block in enumerate((2 - 2 * core, 4 - 3 * core)):
        copies.append(
            pltpu.make_async_remote_copy(
                src_ref=out_ref.at[block_span(block), :],
                dst_ref=peer_ref.at[pl.ds(slot * BLOCK, BLOCK), :],
                send_sem=send_sem.at[slot],
                recv_sem=recv_sem.at[slot],
                device_id=peer,
                device_id_type=pl.DeviceIdType.MESH,
            )
        )
        copies[-1].start()
    for copy in copies:
        copy.wait()


def place_kernel(info_ref, packed_ref, peer_ref, separator_ref, out_ref):
    core, even = info_ref[0], info_ref[1] == 1

    @pl.when(even)
    def _():
        out_ref[0] = separator_ref[...]

    def packed(k):
        return packed_ref[k * BLOCK : (k + 1) * BLOCK, :]

    def put(row, column, value):
        out_ref[0, row * BLOCK : (row + 1) * BLOCK, column * BLOCK : (column + 1) * BLOCK] = value

    first, second = peer_ref[:BLOCK, :], peer_ref[BLOCK:, :]
    odd = jnp.logical_not(even)

    @pl.when(odd & (core == 0))
    def _():
        for row, column, value in (
            (0, 0, packed(0)), (1, 0, packed(1)), (2, 0, packed(2)), (3, 0, first.T),
            (0, 1, packed(1).T), (1, 1, packed(3)), (2, 1, packed(4)), (3, 1, second.T),
        ):
            put(row, column, value)

    @pl.when(odd & (core == 1))
    def _():
        for row, column, value in (
            (0, 0, first.T), (1, 0, second.T), (2, 0, packed(4)), (3, 0, packed(2).T),
            (0, 1, packed(0)), (1, 1, packed(1)), (2, 1, packed(2)), (3, 1, packed(3)),
        ):
            put(row, column, value)


def reduce_kernel(side, value_ref, out_ref, parts_ref, first_sems, send_sem, recv_sem, last_send, last_recv):
    me = lax.axis_index("tm")
    place_y = me % side
    root = me - place_y + 1
    stages = [((me // side) % side, side), ((me // side**2) % side, side**2)]

    def other(stage, step):
        place, stride = stages[stage]
        return me + ((place + step) % side - place) * stride

    def hand(source, target, send, recv, device):
        return pltpu.make_async_remote_copy(
            src_ref=source,
            dst_ref=target,
            send_sem=send,
            recv_sem=recv,
            device_id={"tm": device},
            device_id_type=pl.DeviceIdType.MESH,
        )

    slot = parts_ref.at[len(stages), 0]

    @pl.when(place_y == 1)
    def _():
        row = (me - 1, me + 1, me + 2)
        meet([{"tm": other(s, d)} for s in range(len(stages)) for d in range(1, side)] + [{"tm": k} for k in row])
        hand(value_ref, slot, first_sems.at[0], first_sems.at[1], me + 2).wait_recv()
        out_ref[...] = value_ref[...] + parts_ref[len(stages), 0]
        for s, (place, _) in enumerate(stages):
            parts_ref[s, place] = out_ref[...]
            copies = []
            for d in range(1, side):
                copies += exchange(
                    [(out_ref, parts_ref.at[s, place])],
                    {"tm": other(s, d)},
                    send_sem.at[s, pl.ds(d, 1)],
                    recv_sem.at[s, pl.ds(d, 1)],
                )
            for copy in copies:
                copy.wait()
            total = parts_ref[s, 0]
            for k in range(1, side):
                total = total + parts_ref[s, k]
            out_ref[...] = total
        copies = [hand(out_ref, out_ref, last_send.at[k], last_recv, device) for k, device in enumerate(row)]
        for copy in copies:
            copy.start()
        for copy in copies:
            copy.wait_send()

    @pl.when(place_y != 1)
    def _():
        meet([{"tm": root}])

        @pl.when(place_y == 3)
        def _():
            copy = hand(value_ref, slot, first_sems.at[0], first_sems.at[1], root)
            copy.start()
            copy.wait_send()

        hand(out_ref, out_ref, last_send.at[0], last_recv, root).wait_recv()


def vmem(count):
    return [pl.BlockSpec(memory_space=pltpu.VMEM)] * count


def shape_of(*sizes, dtype=F32):
    return jax.ShapeDtypeStruct(sizes, dtype)


SMEM_SPEC = pl.BlockSpec(memory_space=pltpu.SMEM)
ANY_SPEC = pl.BlockSpec(memory_space=pl.ANY)
HBM_SPEC = pl.BlockSpec(memory_space=pltpu.HBM)


def local_call(kernel, name, flops, mebibytes, **kwargs):
    return pl.pallas_call(
        kernel,
        compiler_params=pltpu.CompilerParams(vmem_limit_bytes=mebibytes * 2**20),
        cost_estimate=pl.CostEstimate(flops=flops, bytes_accessed=2**23, transcendentals=0),
        name=name,
        **kwargs,
    )


def remote_call(kernel, name, identity, mebibytes=24, **kwargs):
    return pl.pallas_call(
        kernel,
        compiler_params=pltpu.CompilerParams(
            collective_id=identity, has_side_effects=True, vmem_limit_bytes=mebibytes * 2**20
        ),
        name=name,
        **kwargs,
    )


def dma_sems(*shape):
    return pltpu.SemaphoreType.DMA(shape)


def whole(shape, index):
    return pl.BlockSpec(shape, lambda i: index, pipeline_mode=pl.Buffered(1))


def on_device(diag_blocks, sub_blocks, arrow_blocks, tip_block):
    partition = lax.axis_index("tm")
    parts = lax.axis_size("tm")
    order, half = diag_blocks.shape[1:]
    effects = arrow_blocks.shape[1]
    packed_rows = PACKED * BLOCK + effects * half // BLOCK
    evens = range(0, parts, 2)
    down = [(p, p - 1) for p in evens if p > 0]
    core = lax.axis_index("blk")
    info = jnp.stack([core, (partition % 2 == 0).astype(core.dtype), (partition > 0).astype(core.dtype)])
    square, tall = (order, order), (order, half)
    big = [pltpu.VMEM(square, BF16)] * 2
    thin = [pltpu.VMEM(tall, BF16)] * 2

    pivot, arrow_full = remote_call(
        gather_kernel, "gather_pivot", 1,
        out_shape=[shape_of(*square), shape_of(1, effects, order)],
        in_specs=[HBM_SPEC] * 2, out_specs=[ANY_SPEC] * 2,
        scratch_shapes=[dma_sems(2), dma_sems(COPIES + 1), dma_sems(COPIES + 1)],
    )(diag_blocks, arrow_blocks)
    sub_full = lax.all_gather(sub_blocks, "blk", axis=2, tiled=True)
    inverse, log_first = inverse_and_log(pivot)

    packed_shape = shape_of(packed_rows, BLOCK)
    packed_scratch = pltpu.VMEM((packed_rows, BLOCK), F32)
    pairs = [(p, p + 1) for p in evens]
    both, left_own, rest, pair_sums = remote_call(
        pair_kernel, "products_and_swap", 2, 58,
        out_shape=[shape_of(2, packed_rows, BLOCK), shape_of(*tall), packed_shape, shape_of(effects + 8, TILE)],
        in_specs=[*[ANY_SPEC] * 4, *vmem(2)],
        out_specs=[ANY_SPEC, *vmem(3)],
        scratch_shapes=[pltpu.VMEM(square, F32)] * 3
        + [pltpu.VMEM(tall, F32), pltpu.VMEM((effects, half), F32)]
        + [packed_scratch] * 3
        + [pltpu.VMEM((effects + 8, TILE), F32)] * 2
        + big * 3
        + thin * 2
        + [dma_sems(5), *[dma_sems(PACKED + 1)] * 5, dma_sems(1), dma_sems(1)],
    )(inverse, sub_full, diag_blocks, arrow_blocks, arrow_full, log_first)
    left_pair = lax.ppermute(left_own, "tm", pairs)
    left_full = lax.all_gather(left_own, "blk", axis=1, tiled=True)

    inverse, log_second, separator = inverse_of_packed(info, both, order, half)
    product = local_call(
        second_products_kernel, "second_products", 5 * order**3, 58,
        out_shape=packed_shape,
        in_specs=[SMEM_SPEC, *[ANY_SPEC] * 4],
        out_specs=vmem(1)[0],
        scratch_shapes=[pltpu.VMEM(square, F32)] * 2
        + [pltpu.VMEM((2, packed_rows - PACKED * BLOCK, BLOCK), F32), packed_scratch, dma_sems(4)]
        + big * 2
        + thin,
    )(info, inverse, left_full, both, rest)
    above = lax.ppermute(product, "tm", down)
    sums, x_high, x_low = local_call(
        second_terms_kernel, "second_terms", 3 * order**3, 58,
        out_shape=[shape_of(effects + 8, TILE)] + [shape_of(*tall, dtype=BF16)] * 2,
        in_specs=[SMEM_SPEC, *[ANY_SPEC] * 2, *vmem(3)],
        out_specs=vmem(3),
        scratch_shapes=[pltpu.VMEM(square, F32), pltpu.VMEM(tall, F32), dma_sems(2)] + big,
    )(info, inverse, left_pair, both[:, PACKED * BLOCK :], pair_sums, log_second)
    totals = remote_call(
        functools.partial(reduce_kernel, SIDE), "reduce_terms", 3,
        out_shape=shape_of(effects + 8, TILE), in_specs=vmem(1), out_specs=vmem(1)[0],
        scratch_shapes=[
            pltpu.VMEM((3, SIDE, effects + 8, TILE), F32),
            dma_sems(2), dma_sems(2, SIDE), dma_sems(2, SIDE), dma_sems(3), pltpu.SemaphoreType.DMA,
        ],
    )(sums)
    left_result = local_call(
        second_fill_kernel, "second_fill", 3 * order**3, 58,
        out_shape=shape_of(1, *tall),
        in_specs=[SMEM_SPEC, *vmem(1), *[ANY_SPEC] * 2, *vmem(2)],
        out_specs=vmem(1)[0],
        scratch_shapes=[pltpu.VMEM(square, F32), pltpu.SemaphoreType.DMA] + big,
    )(info, totals, left_full, left_own, x_high, x_low)
    packed, swapped = remote_call(
        finish_kernel, "finish_blocks", 4,
        out_shape=[packed_shape, shape_of(2 * BLOCK, BLOCK)], in_specs=vmem(2), out_specs=vmem(2),
        scratch_shapes=[dma_sems(2), dma_sems(2)],
    )(product, above)
    diag_result = local_call(
        place_kernel, "place_blocks", 2**20, 12,
        out_shape=shape_of(1, *tall), in_specs=[SMEM_SPEC, *vmem(3)], out_specs=vmem(1)[0],
    )(info, packed, swapped, separator)
    last = PACKED * BLOCK
    own_arrow = lax.dynamic_index_in_dim(both[:, last:], core, 0, keepdims=False)
    arrow_result = arrow_unpack(jnp.where(info[1] == 1, own_arrow, packed[last:]))
    return (
        diag_result,
        left_result,
        arrow_result[None],
        tip_block - totals[:effects, :effects],
        jnp.sum(totals[effects]),
    )


def solution(mesh):
    in_specs = (P("tm", None, "blk"), P("tm", None, "blk"), P("tm", None, "blk"), P())
    out_specs = (P("tm", None, "blk"), P("tm", None, "blk"), P("tm", None, "blk"), P(), P())
    return jax.shard_map(
        on_device, mesh=mesh, in_specs=in_specs, out_specs=out_specs, check_vma=False
    )
```
